32 devices in a mesh: groups: 2 (over y), tensor: 4 (over z), seq: 2 (over x), sub: 2 (over core).
Axes of the slice: x: 2, y: 2, z: 4, core: 2. Of those that a mesh axis runs over, the one named last changes fastest.
Arguments:
- hidden: bfloat16 [512, 53248], P(('groups', 'seq'), ('tensor', 'sub')), parts along dimension 0, may hold values from -6 to 6
- down_weight: bfloat16 [53248, 8192], P(('tensor', 'sub'), 'seq'), may hold values from -0.02734375 to 0.02734375
- sign_bits: int32 [8192], P('seq'), may hold values from 0 to 1
Outputs:
- sum_codes: bfloat16 [512, 8192], P(('groups', 'sub'), 'seq'), parts along dimension 0
- sum_scales: bfloat16 [512, 64], P(('groups', 'sub'), 'seq'), parts along dimension 0
The draws below stay inside these ranges and needn't reach their ends.
There are 2 independent parts, one for each index of `groups`. The reference program is written for one: setup_inputs(seed, part) draws one part's arguments, and reference() takes and returns one part's arrays. A program takes and returns all parts, laid end to end along the dimension named above; an argument that names none is the same for every part. Nothing has to cross between parts.
All inputs are finite; a program needn't handle non-finite values. Where the reference program divides by a largest or mean magnitude, that divisor is 1e-20 or more.
Results may differ from the reference program's by a relative error of at most 0.014.
Values may be sent and summed in bfloat16 or wider, within the bound.
No kernel may reach another device: no remote copies, remote signals or barrier semaphores. Data moves between devices by JAX's collectives and lax.ppermute only.
A program may use at most 192 MiB of HBM per device.

```python
import math
import jax
import jax.numpy as jnp
from jax import lax

D = 8192
FF = 53248
BLOCK = 128
TOKENS = 256
N_TENSOR = 4
N_SUB = 2


def plant(entries, key, low, largest):
    shape = entries.shape
    place = [jax.random.randint(jax.random.fold_in(key, axis), (), 0, shape[axis]) for axis in range(len(shape))]
    entries = entries.at[tuple(place)].set(low)
    longest = shape.index(max(shape))
    place[longest] = (place[longest] + 1) % shape[longest]
    return entries.at[tuple(place)].set(largest)


def spiked(array, key, source, target, blocks, factor):
    owner, partner = [(jnp.arange(array.shape[axis_at]) // (array.shape[axis_at] // blocks)).reshape([-1 if axis == axis_at else 1 for axis in range(array.ndim)]) for axis_at in (source, target)]
    chosen = jax.random.permutation(key, blocks)[partner]
    strong = (owner == chosen) | (owner == (partner + blocks // 2) % blocks)
    return jnp.where(strong, factor * array, array)


def block_levels(own_key, dims, cuts, smallest, high):
    loudness, own = 1.0, jax.random.fold_in(own_key, 6)
    for dim, parts in cuts:
        heights = jnp.exp(jax.random.uniform(jax.random.fold_in(own, dim), (parts,), jnp.float32, smallest / len(cuts), high / len(cuts)))
        loudness = loudness * jnp.repeat(heights, dims[dim] // parts).reshape([-1 if axis == dim else 1 for axis in range(len(dims))])
    return loudness


def gaussian(stream_key, shape, width, limit, shards=(), kind=jnp.bfloat16):
    result = width * jax.random.normal(stream_key, shape, jnp.float32)
    if shards:
        result = result * block_levels(stream_key, shape, shards, -0.22, 0.18)
    return jnp.clip(result, -limit, limit).astype(kind)


def heavy_noise(key, extent, spread, limit, pieces, heavy, held_as=jnp.bfloat16):
    drawn = spread * jax.random.normal(key, extent, jnp.float32)
    if pieces:
        drawn = drawn * block_levels(key, extent, pieces, -0.22, 0.18)
    return jnp.clip(spiked(drawn, jax.random.fold_in(key, 3), *heavy), -limit, limit).astype(held_as)


def setup_inputs(seed: int = 0, part: int = 0) -> dict:
    arg_keys = jax.random.split(jax.random.key(seed), 4)
    part_splits = jax.random.split(jax.random.fold_in(arg_keys[3], part), 4)
    return {
        "hidden": heavy_noise(part_splits[0], (TOKENS, FF), 1.0, 6.0, ((0, 2), (1, 8)), (1, 0, 8, 2.0)),
        "down_weight": gaussian(arg_keys[1], (FF, D), FF ** -0.5, 0.02734375, ((0, 8), (1, 2))),
        "sign_bits": plant(jax.random.randint(arg_keys[2], (D,), 0, 2), jax.random.fold_in(arg_keys[2], 1), 0, 1).astype(jnp.int32),
    }


epsilon = 1e-06

def hadamard(order):
    indices = jnp.arange(order, dtype=jnp.int32)
    parity = jnp.zeros((order, order), jnp.int32)
    for position in range(order.bit_length() - 1):
        parity = parity + (indices[:, None] >> position & 1) * (indices[None, :] >> position & 1)
    return (1 - 2 * (parity % 2)).astype(jnp.float32) / math.sqrt(order)

def rotate_blocks(values, flips):
    blocks = (values * flips[None, :]).reshape(values.shape[0], -1, BLOCK)
    rotated = jnp.einsum('tnb,bc->tnc', blocks, hadamard(BLOCK), precision=lax.Precision.HIGHEST)
    return rotated.reshape(values.shape)

def encode_blocks(values):
    blocks = values.reshape(values.shape[:-1] + (-1, BLOCK))
    scales = (lax.optimization_barrier(jnp.max(jnp.abs(blocks), axis=-1)) + epsilon).astype(jnp.bfloat16)
    encoded = (blocks / scales.astype(jnp.float32)[..., None]).astype(jnp.bfloat16)
    return (encoded.reshape(values.shape), scales)

def decode_blocks(encoded, scales):
    blocks = encoded.astype(jnp.float32).reshape(encoded.shape[:-1] + (-1, BLOCK))
    return (blocks * scales.astype(jnp.float32)[..., None]).reshape(encoded.shape)

def reference(hidden, down_weight, sign_bits):
    group_count = N_TENSOR * N_SUB
    group_width = FF // group_count
    flips = (2 * sign_bits - 1).astype(jnp.float32)

    def accumulate(summed, group_index):
        start = (group_index * group_width).astype(jnp.int32)
        hidden_part = lax.dynamic_slice_in_dim(hidden, start, group_width, 1)
        weight_part = lax.dynamic_slice_in_dim(down_weight, start, group_width, 0)
        partial_value = jnp.dot(hidden_part, weight_part, preferred_element_type=jnp.float32)
        encoded, scales = encode_blocks(rotate_blocks(partial_value, flips))
        return (summed + decode_blocks(encoded, scales), None)
    summed, _ = lax.scan(accumulate, jnp.zeros((TOKENS, D), jnp.float32), jnp.arange(group_count, dtype=jnp.int32))
    sum_codes, sum_scales = encode_blocks(summed)
    return (sum_codes, sum_scales)
```

```python
import math

import jax
import jax.numpy as jnp
from jax import lax
from jax.sharding import PartitionSpec as P

BLOCK = 128
AXES = ("tensor", "seq", "sub")
epsilon = 1e-06


def hadamard(order):
    indices = jnp.arange(order, dtype=jnp.int32)
    parity = jnp.zeros((order, order), jnp.int32)
    for position in range(order.bit_length() - 1):
        parity = parity + (indices[:, None] >> position & 1) * (indices[None, :] >> position & 1)
    return (1 - 2 * (parity % 2)).astype(jnp.float32) / math.sqrt(order)


def rotate_blocks(values, flips):
    blocks = (values * flips[None, :]).reshape(values.shape[0], -1, BLOCK)
    rotated = jnp.einsum("tnb,bc->tnc", blocks, hadamard(BLOCK), precision=lax.Precision.HIGHEST)
    return rotated.reshape(values.shape)


def encode_blocks(values):
    blocks = values.reshape(values.shape[:-1] + (-1, BLOCK))
    scales = (jnp.max(jnp.abs(blocks), axis=-1) + epsilon).astype(jnp.bfloat16)
    encoded = (blocks / scales.astype(jnp.float32)[..., None]).astype(jnp.bfloat16)
    return (encoded.reshape(values.shape), scales)


def shards(hidden, down_weight, sign_bits):
    tensor_count = lax.axis_size("tensor")
    seq_count = lax.axis_size("seq")
    sub_count = lax.axis_size("sub")
    tensor_at = lax.axis_index("tensor")
    seq_at = lax.axis_index("seq")
    sub_at = lax.axis_index("sub")
    rows, depth = hidden.shape
    per_sub = seq_count // sub_count
    piece = rows // tensor_count
    chunks = 4
    width = depth // chunks
    flips = (2 * sign_bits - 1).astype(jnp.float32)

    def linear(tensor, seq, sub):
        return (tensor * seq_count + seq) * sub_count + sub

    def owner(seq, shift):
        return (seq - shift) % seq_count // per_sub

    def chip_sum(partial_value, shift):
        total = partial_value
        for step in range(1, sub_count):
            pairs = [
                (linear(t, s, (owner(s, shift) + step) % sub_count), linear(t, s, owner(s, shift)))
                for t in range(tensor_count)
                for s in range(seq_count)
            ]
            total = total + lax.ppermute(partial_value.astype(jnp.bfloat16), AXES, pairs).astype(jnp.float32)
        return total

    def along_tensor(values, step, shift):
        pairs = [
            (linear(t, s, owner(s, shift)), linear((t + step) % tensor_count, s, owner(s, shift)))
            for t in range(tensor_count)
            for s in range(seq_count)
        ]
        return lax.ppermute(values, AXES, pairs)

    def finish(partial_value, shift):
        total = chip_sum(partial_value, shift)
        summed = lax.dynamic_slice_in_dim(total, tensor_at * piece, piece, 0)
        narrow = total.astype(jnp.bfloat16)
        for step in range(1, tensor_count):
            target = (tensor_at + step) % tensor_count
            sent = lax.dynamic_slice_in_dim(narrow, target * piece, piece, 0)
            summed = summed + along_tensor(sent, step, shift).astype(jnp.float32)
        codes, scales = encode_blocks(rotate_blocks(summed, flips))
        full_codes = jnp.zeros((rows, codes.shape[1]), jnp.bfloat16)
        full_scales = jnp.zeros((rows, scales.shape[1]), jnp.bfloat16)
        for step in range(tensor_count):
            at = (tensor_at - step) % tensor_count * piece
            held = (codes, scales)
            if step:
                held = (along_tensor(codes, step, shift), along_tensor(scales, step, shift))
            full_codes = lax.dynamic_update_slice_in_dim(full_codes, held[0], at, 0)
            full_scales = lax.dynamic_update_slice_in_dim(full_scales, held[1], at, 0)
        return full_codes, full_scales

    def from_seq(values, shift):
        return lax.ppermute(values, "seq", [(s, (s + shift) % seq_count) for s in range(seq_count)])

    results = []
    for shift in range(seq_count):
        if shift == 0:
            partial_value = jnp.dot(hidden, down_weight, preferred_element_type=jnp.float32)
        else:
            partial_value = jnp.zeros((rows, down_weight.shape[1]), jnp.float32)
            for chunk in range(chunks):
                part = slice(chunk * width, (chunk + 1) * width)
                arrived = from_seq(hidden[:, part], shift)
                partial_value = partial_value + jnp.dot(
                    arrived, down_weight[part], preferred_element_type=jnp.float32
                )
        results.append(finish(partial_value, shift))

    out = []
    for at in range(2):
        stacked = jnp.stack([result[at] for result in results])
        held = []
        for place in range(per_sub):
            shift = (seq_at - (sub_at * per_sub + place)) % seq_count
            held.append(lax.dynamic_index_in_dim(stacked, shift, 0, keepdims=False))
        out.append(jnp.concatenate(held))
    return tuple(out)


def solution(mesh):
    return jax.shard_map(
        shards,
        mesh=mesh,
        in_specs=(P(("groups", "seq"), ("tensor", "sub")), P(("tensor", "sub"), "seq"), P("seq")),
        out_specs=(P(("groups", "sub"), "seq"), P(("groups", "sub"), "seq")),
        check_vma=False,
    )
```

```python
import math

import jax
import jax.numpy as jnp
from jax import lax
from jax.sharding import PartitionSpec as P

BLOCK = 128
epsilon = 1e-06


def hadamard(order):
    indices = jnp.arange(order, dtype=jnp.int32)
    parity = jnp.zeros((order, order), jnp.int32)
    for position in range(order.bit_length() - 1):
        parity = parity + (indices[:, None] >> position & 1) * (indices[None, :] >> position & 1)
    return (1 - 2 * (parity % 2)).astype(jnp.float32) / math.sqrt(order)


def rotate_blocks(values, flips):
    blocks = (values * flips[None, :]).reshape(values.shape[0], -1, BLOCK)
    rotated = jnp.einsum("tnb,bc->tnc", blocks, hadamard(BLOCK), precision=lax.Precision.HIGHEST)
    return rotated.reshape(values.shape)


def encode_blocks(values):
    blocks = values.reshape(values.shape[:-1] + (-1, BLOCK))
    scales = (jnp.max(jnp.abs(blocks), axis=-1) + epsilon).astype(jnp.bfloat16)
    encoded = (blocks / scales.astype(jnp.float32)[..., None]).astype(jnp.bfloat16)
    return (encoded.reshape(values.shape), scales)


def shards(hidden, down_weight, sign_bits):
    seq_count = lax.axis_size("seq")
    sub_count = lax.axis_size("sub")
    seq_at = lax.axis_index("seq")
    sub_at = lax.axis_index("sub")
    rows, depth = hidden.shape
    per_sub = seq_count // sub_count
    chunks = 4
    width = depth // chunks
    flips = (2 * sign_bits - 1).astype(jnp.float32)

    def finish(partial_value):
        summed = lax.psum_scatter(
            partial_value.astype(jnp.bfloat16), ("tensor", "sub"), scatter_dimension=0, tiled=True
        ).astype(jnp.float32)
        codes, scales = encode_blocks(rotate_blocks(summed, flips))
        padding = jnp.zeros((codes.shape[0], -scales.shape[1] % BLOCK), jnp.bfloat16)
        packed = jnp.concatenate([codes, scales, padding], axis=1)
        full = lax.all_gather(packed, ("tensor", "sub"), axis=0, tiled=True)
        return full[:, : codes.shape[1]], full[:, codes.shape[1] : codes.shape[1] + scales.shape[1]]

    def from_seq(values, shift):
        return lax.ppermute(values, "seq", [(s, (s + shift) % seq_count) for s in range(seq_count)])

    results = []
    for shift in range(seq_count):
        if shift == 0:
            partial_value = jnp.dot(hidden, down_weight, preferred_element_type=jnp.float32)
        else:
            partial_value = jnp.zeros((rows, down_weight.shape[1]), jnp.float32)
            for chunk in range(chunks):
                part = slice(chunk * width, (chunk + 1) * width)
                arrived = from_seq(hidden[:, part], shift)
                partial_value = partial_value + jnp.dot(
                    arrived, down_weight[part], preferred_element_type=jnp.float32
                )
        results.append(finish(partial_value))

    out = []
    for at in range(2):
        stacked = jnp.stack([result[at] for result in results])
        held = []
        for place in range(per_sub):
            shift = (seq_at - (sub_at * per_sub + place)) % seq_count
            held.append(lax.dynamic_index_in_dim(stacked, shift, 0, keepdims=False))
        out.append(jnp.concatenate(held))
    return tuple(out)


def solution(mesh):
    return jax.shard_map(
        shards,
        mesh=mesh,
        in_specs=(P(("groups", "seq"), ("tensor", "sub")), P(("tensor", "sub"), "seq"), P("seq")),
        out_specs=(P(("groups", "sub"), "seq"), P(("groups", "sub"), "seq")),
        check_vma=False,
    )
```

```python
import functools
import math

import jax
import jax.numpy as jnp
import numpy as np
from jax import lax
from jax.experimental import pallas as pl
from jax.experimental.pallas import tpu as pltpu
from jax.sharding import PartitionSpec as P

BLOCK = 128
UNIT = 512
VMEM_LIMIT = 48 * 2**20
epsilon = 1e-06


def hadamard(order):
    indices = np.arange(order)
    parity = np.zeros((order, order), np.int64)
    for position in range(order.bit_length() - 1):
        parity = parity + (indices[:, None] >> position & 1) * (indices[None, :] >> position & 1)
    return ((1 - 2 * (parity % 2)) / math.sqrt(order)).astype(np.float32)


def multiply_body(has_total, start_ref, x_ref, w_ref, *rest):
    product = jnp.dot(x_ref[...], w_ref[...], preferred_element_type=jnp.float32)
    if has_total:
        product = product + rest[0][...]
    out_ref = rest[-1]
    out_ref[...] = product.astype(out_ref.dtype)


def multiply(x, w, row, start, columns, wide, total=None, tokens=(), dtype=jnp.float32):
    rows, depth = x.shape
    steps = columns // wide
    in_specs = [
        pl.BlockSpec((rows, depth), lambda n, s: (0, 0)),
        pl.BlockSpec((pl.Element(depth), pl.Element(wide)), lambda n, s: (row, (s[0] * steps + n) * wide)),
    ]
    operands = [x, w]
    if total is not None:
        in_specs.append(pl.BlockSpec((rows, wide), lambda n, s: (0, s[0] * steps + n)))
        operands.append(total)
    for token in tokens:
        in_specs.append(pl.BlockSpec(memory_space=pl.ANY))
        operands.append(token)
    return pl.pallas_call(
        functools.partial(multiply_body, total is not None),
        out_shape=jax.ShapeDtypeStruct((rows, columns), dtype),
        grid_spec=pltpu.PrefetchScalarGridSpec(
            num_scalar_prefetch=1,
            grid=(steps,),
            in_specs=in_specs,
            out_specs=pl.BlockSpec((rows, wide), lambda n, s: (0, n)),
        ),
        compiler_params=pltpu.CompilerParams(vmem_limit_bytes=VMEM_LIMIT),
        cost_estimate=pl.CostEstimate(
            flops=2 * rows * depth * columns, bytes_accessed=2 * depth * columns, transcendentals=0
        ),
    )(start, *operands)


def encode_body(parts_ref, flips_ref, rotation_ref, out_ref):
    count, rows, columns = parts_ref.shape
    blocks = columns // BLOCK
    held = []
    for block in range(blocks):
        at = slice(block * BLOCK, (block + 1) * BLOCK)
        total = parts_ref[0, :, at].astype(jnp.float32)
        for part in range(1, count):
            total = total + parts_ref[part, :, at].astype(jnp.float32)
        held.append(total * flips_ref[:, at])
    rotation = rotation_ref[...]
    lane = lax.broadcasted_iota(jnp.int32, (rows, BLOCK), 1)
    scales = jnp.zeros((rows, BLOCK), jnp.float32)
    for block in range(blocks):
        at = slice(block * BLOCK, (block + 1) * BLOCK)
        rotated = jnp.dot(
            held[block], rotation, precision=lax.Precision.HIGHEST, preferred_element_type=jnp.float32
        )
        largest = jnp.max(jnp.abs(rotated), axis=1, keepdims=True)
        scale = (largest + epsilon).astype(jnp.bfloat16).astype(jnp.float32)
        codes = (rotated / scale).astype(jnp.bfloat16)
        scales = jnp.where(lane == block, scale, scales)
        for part in range(count):
            out_ref[part, :, at] = codes
    for part in range(count):
        out_ref[part, :, columns:] = scales.astype(jnp.bfloat16)


def encode(parts, flips):
    count, rows, columns = parts.shape
    return pl.pallas_call(
        encode_body,
        out_shape=jax.ShapeDtypeStruct((count, rows, columns + BLOCK), jnp.bfloat16),
        compiler_params=pltpu.CompilerParams(vmem_limit_bytes=VMEM_LIMIT),
        cost_estimate=pl.CostEstimate(
            flops=12 * rows * columns * BLOCK, bytes_accessed=4 * count * rows * columns, transcendentals=0
        ),
    )(parts, flips, hadamard(BLOCK))


def choose_body(places, chosen_ref, *refs):
    out_ref = refs[-1]
    rows = refs[0].shape[0]
    for place in range(places):
        for index, ref in enumerate(refs[:-1]):

            @pl.when(chosen_ref[place] == index)
            def _():
                out_ref[place * rows : (place + 1) * rows] = ref[...]


def choose(results, chosen):
    rows, columns = results[0].shape
    vmem = pl.BlockSpec(memory_space=pltpu.VMEM)
    return pl.pallas_call(
        functools.partial(choose_body, chosen.shape[0]),
        out_shape=jax.ShapeDtypeStruct((chosen.shape[0] * rows, columns), jnp.bfloat16),
        in_specs=[pl.BlockSpec(memory_space=pltpu.SMEM)] + [vmem] * len(results),
        out_specs=vmem,
        compiler_params=pltpu.CompilerParams(vmem_limit_bytes=VMEM_LIMIT),
    )(chosen, *results)


def assemble_body(places, half, chosen_ref, here_ref, other_ref, *refs):
    codes_ref, scales_ref = refs[-2:]
    rows = refs[0].shape[0]
    scales = half // BLOCK

    def put(core, mine_ref, place):
        at = slice(place * rows, (place + 1) * rows)
        columns = slice(core * half, (core + 1) * half)
        rest = slice((1 - core) * half, (2 - core) * half)
        codes_ref[at, columns] = mine_ref[:, :half]
        codes_ref[at, rest] = other_ref[at, :half]
        pair = [mine_ref[:, half : half + scales], other_ref[at, half : half + scales]]
        scales_ref[at] = jnp.concatenate(pair if core == 0 else pair[::-1], axis=1)

    for place in range(places):
        for core in range(2):
            for index, ref in enumerate(refs[:-2]):
                pl.when((chosen_ref[place] == index) & (here_ref[0] == core))(
                    functools.partial(put, core, ref, place)
                )


def assemble(results, chosen, here, other, half):
    rows = other.shape[0]
    vmem = pl.BlockSpec(memory_space=pltpu.VMEM)
    smem = pl.BlockSpec(memory_space=pltpu.SMEM)
    return pl.pallas_call(
        functools.partial(assemble_body, chosen.shape[0], half),
        out_shape=(
            jax.ShapeDtypeStruct((rows, 2 * half), jnp.bfloat16),
            jax.ShapeDtypeStruct((rows, 2 * half // BLOCK), jnp.bfloat16),
        ),
        in_specs=[smem, smem, vmem] + [vmem] * len(results),
        out_specs=(vmem, vmem),
        compiler_params=pltpu.CompilerParams(vmem_limit_bytes=VMEM_LIMIT),
    )(chosen, here, other, *results)


def cut(depth):
    if depth % UNIT or depth < 8 * UNIT:
        return [depth]
    units = depth // UNIT
    sizes = []
    for share in (0.31, 0.31, 0.23):
        sizes.append(max(1, round(units * share)))
    sizes.append(units - sum(sizes))
    return [size * UNIT for size in sizes]


def shards(hidden, down_weight, sign_bits):
    tensor_count = lax.axis_size("tensor")
    seq_count = lax.axis_size("seq")
    sub_count = lax.axis_size("sub")
    seq_at = lax.axis_index("seq")
    sub_at = lax.axis_index("sub")
    rows, depth = hidden.shape
    half = down_weight.shape[1] // sub_count
    per_sub = seq_count // sub_count
    piece = rows // tensor_count
    wide = min(256, half)
    wide_chunk = min(512, half)
    flips = (2 * sign_bits - 1).astype(jnp.float32)[None, :]
    own_flips = lax.dynamic_slice_in_dim(flips, sub_at * half, half, 1)
    whole = jnp.zeros((1,), jnp.int32)
    here = jnp.reshape(sub_at, (1,)).astype(jnp.int32)
    there = 1 - here

    def swap(values):
        return lax.ppermute(values, "sub", [(0, 1), (1, 0)])

    def scatter(sent, kept):
        total = (kept.astype(jnp.float32) + swap(sent).astype(jnp.float32)).astype(jnp.bfloat16)
        return [total], lax.all_to_all(
            total.reshape(tensor_count, piece, half), "tensor", split_axis=0, concat_axis=0, tiled=True
        )

    def gather(parts):
        packed = encode(parts, own_flips)
        full = lax.all_to_all(packed, "tensor", split_axis=0, concat_axis=0, tiled=True)
        return [packed], full.reshape(rows, half + BLOCK)

    sizes = cut(depth)
    places = [sum(sizes[:index]) for index in range(len(sizes))]
    slices = [hidden[:, at : at + size] for at, size in zip(places, sizes)]
    arrivals = []
    for shift in range(1, seq_count):
        pairs = [(s, (s + shift) % seq_count) for s in range(seq_count)]
        arrivals.append([lax.ppermute(part, "seq", pairs) for part in slices])

    sent = multiply(hidden, down_weight, 0, there, half, wide, tokens=slices, dtype=jnp.bfloat16)
    kept = multiply(hidden, down_weight, 0, here, half, wide, tokens=[sent], dtype=jnp.bfloat16)
    tokens, parts = scatter(sent, kept)
    results = []
    for arrived in arrivals:
        total = None
        for index, (at, size) in enumerate(zip(places, sizes)):
            if index == len(sizes) // 2:
                tokens, full = gather(parts)
                results.append(full)
            if index < len(sizes) - 1:
                total = multiply(
                    arrived[index], down_weight, at, whole, sub_count * half, wide_chunk, total=total, tokens=tokens
                )
                tokens = []
            else:
                last = functools.partial(multiply, arrived[index], down_weight, at, total=total, dtype=jnp.bfloat16)
                sent = last(there, half, wide_chunk, tokens=tokens)
                kept = last(here, half, wide_chunk, tokens=[sent])
        tokens, parts = scatter(sent, kept)
    results.append(gather(parts)[1])

    def of_sub(sub):
        return jnp.stack([(seq_at - (sub * per_sub + place)) % seq_count for place in range(per_sub)])

    other = swap(choose(results, of_sub(1 - sub_at)))
    return assemble(results, of_sub(sub_at), here, other, half)


def solution(mesh):
    return jax.shard_map(
        shards,
        mesh=mesh,
        in_specs=(P(("groups", "seq"), ("tensor", "sub")), P(("tensor", "sub"), "seq"), P("seq")),
        out_specs=(P(("groups", "sub"), "seq"), P(("groups", "sub"), "seq")),
        check_vma=False,
    )
```

```python
import functools
import math

import jax
import jax.numpy as jnp
import numpy as np
from jax import lax
from jax.experimental import pallas as pl
from jax.experimental.pallas import tpu as pltpu
from jax.sharding import PartitionSpec as P

BLOCK = 128
UNIT = 512
GROUPS = 2
BUFFERS = 4
VMEM_LIMIT = 40 * 2**20
epsilon = 1e-06

SMALL = pl.CostEstimate(flops=1, bytes_accessed=1, transcendentals=0)
PARAMS = pltpu.CompilerParams(vmem_limit_bytes=VMEM_LIMIT)
VMEM = pl.BlockSpec(memory_space=pltpu.VMEM)
SMEM = pl.BlockSpec(memory_space=pltpu.SMEM)
ANY = pl.BlockSpec(memory_space=pl.ANY)


def hadamard(order):
    indices = np.arange(order)
    parity = np.zeros((order, order), np.int64)
    for position in range(order.bit_length() - 1):
        parity = parity + (indices[:, None] >> position & 1) * (indices[None, :] >> position & 1)
    return ((1 - 2 * (parity % 2)) / math.sqrt(order)).astype(np.float32)


def slice_body(places, in_ref, *out_refs):
    for (at, size), out_ref in zip(places, out_refs):
        out_ref[...] = in_ref[:, at : at + size]


def slices_of(values, places):
    return pl.pallas_call(
        functools.partial(slice_body, places),
        out_shape=[jax.ShapeDtypeStruct((values.shape[0], size), values.dtype) for _, size in places],
        in_specs=[VMEM],
        out_specs=[VMEM] * len(places),
        compiler_params=PARAMS,
        cost_estimate=SMALL,
    )(values)


def multiply_body(offsets, has_totals, splits, row, first, number, here_ref, *refs):
    lefts = len(offsets)
    left_refs, refs = refs[:lefts], refs[lefts:]
    w_ref, refs = refs[0], refs[1:]
    total_refs, refs = list(refs[: sum(has_totals)]), refs[sum(has_totals) :]
    buffer, arrived = refs[-2:]
    out_count = sum(2 if split else 1 for split in splits)
    out_refs = refs[-2 - out_count : -2]
    buffers, depth, wide = buffer.shape
    rows = left_refs[0].shape[0]
    in_half = w_ref.shape[1] // wide // 2
    steps = 2 * first if any(splits) else 2 * in_half

    def column(n):
        if not any(splits):
            return n
        side = jnp.where(n < first, 1 - here_ref[0], here_ref[0])
        return side * in_half + number * first + n - jnp.where(n < first, 0, first)

    def at(block):
        return pl.ds(pl.multiple_of(block * wide, wide), wide)

    def copy(n):
        slot = lax.rem(n, buffers)
        return pltpu.make_async_copy(
            w_ref.at[pl.ds(row, depth), at(column(n))], buffer.at[slot], arrived.at[slot]
        )

    def step(n, second):
        copy(n).wait()

        @pl.when(n + buffers - 1 < steps)
        def _():
            copy(n + buffers - 1).start()

        parts = [ref[:, offset : offset + depth] for ref, offset in zip(left_refs, offsets)]
        left = parts[0] if lefts == 1 else jnp.concatenate(parts, axis=0)
        product = jnp.dot(left, buffer[lax.rem(n, buffers)], preferred_element_type=jnp.float32)
        totals, outs = list(total_refs), list(out_refs)
        for index in range(lefts):
            value = product[index * rows : (index + 1) * rows]
            if has_totals[index]:
                value = value + totals.pop(0)[:, at(column(n))]
            if splits[index]:
                sent_ref, kept_ref = outs.pop(0), outs.pop(0)
                if second:
                    kept_ref[:, at(n - first)] = value
                else:
                    sent_ref[:, at(n)] = value.astype(sent_ref.dtype)
            else:
                outs.pop(0)[:, at(column(n))] = value

    for n in range(min(buffers - 1, steps)):
        copy(jnp.int32(n)).start()
    pl.loop(0, first)(functools.partial(step, second=False))
    pl.loop(first, steps)(functools.partial(step, second=True))


def multiply(lefts, weight, row, depth, here, totals, splits, wide, group=None, tokens=()):
    rows = lefts[0][0].shape[0]
    columns = weight.shape[1]
    number, count = group or (0, 1)
    first = columns // wide // 2 // count
    held = [total for total in totals if total is not None]
    out_shape = []
    for split in splits:
        if split:
            out_shape += [
                jax.ShapeDtypeStruct((rows, first * wide), jnp.bfloat16),
                jax.ShapeDtypeStruct((rows, first * wide), jnp.float32),
            ]
        else:
            out_shape.append(jax.ShapeDtypeStruct((rows, columns), jnp.float32))
    body = functools.partial(
        multiply_body,
        [offset for _, offset in lefts],
        [total is not None for total in totals],
        splits,
        row,
        first,
        number,
    )
    return pl.pallas_call(
        body,
        out_shape=out_shape,
        in_specs=[SMEM]
        + [VMEM] * len(lefts)
        + [ANY]
        + [VMEM] * len(held)
        + [ANY] * len(tokens),
        out_specs=[VMEM] * len(out_shape),
        scratch_shapes=[
            pltpu.VMEM((BUFFERS, depth, wide), weight.dtype),
            pltpu.SemaphoreType.DMA((BUFFERS,)),
        ],
        compiler_params=PARAMS,
        cost_estimate=SMALL,
    )(here, *[left for left, _ in lefts], weight, *held, *tokens)


def halve_body(bit_ref, kept_ref, came_ref, sent_out, kept_out):
    half = sent_out.shape[0]

    def put(bit):
        mine, other = slice(bit * half, (bit + 1) * half), slice((1 - bit) * half, (2 - bit) * half)
        kept_out[...] = kept_ref[mine] + came_ref[mine].astype(jnp.float32)
        sent_out[...] = (kept_ref[other] + came_ref[other].astype(jnp.float32)).astype(jnp.bfloat16)

    for bit in range(2):
        pl.when(bit_ref[0] == bit)(functools.partial(put, bit))


def halve(kept, came, bit):
    rows, columns = kept.shape
    half = rows // 2
    if half % 16:
        total = kept + came.astype(jnp.float32)
        sent = lax.dynamic_slice_in_dim(total, (1 - bit) * half, half, 0).astype(jnp.bfloat16)
        return sent, lax.dynamic_slice_in_dim(total, bit * half, half, 0)
    return pl.pallas_call(
        halve_body,
        out_shape=[
            jax.ShapeDtypeStruct((half, columns), jnp.bfloat16),
            jax.ShapeDtypeStruct((half, columns), jnp.float32),
        ],
        in_specs=[SMEM, VMEM, VMEM],
        out_specs=[VMEM, VMEM],
        compiler_params=PARAMS,
        cost_estimate=SMALL,
    )(jnp.reshape(bit, (1,)), kept, came)


def encode_body(kept_ref, came_ref, flips_ref, rotation_ref, out_ref):
    rows, columns = kept_ref.shape
    rotation = rotation_ref[...]
    lane = lax.broadcasted_iota(jnp.int32, (rows, BLOCK), 1)
    scales = jnp.zeros((rows, BLOCK), jnp.float32)
    for block in range(columns // BLOCK):
        at = slice(block * BLOCK, (block + 1) * BLOCK)
        total = (kept_ref[:, at] + came_ref[:, at].astype(jnp.float32)) * flips_ref[:, at]
        rotated = jnp.dot(
            total, rotation, precision=lax.Precision.HIGHEST, preferred_element_type=jnp.float32
        )
        largest = jnp.max(jnp.abs(rotated), axis=1, keepdims=True)
        scale = (largest + epsilon).astype(jnp.bfloat16).astype(jnp.float32)
        out_ref[:, at] = (rotated / scale).astype(jnp.bfloat16)
        scales = jnp.where(lane == block, scale, scales)
    out_ref[:, columns:] = scales.astype(jnp.bfloat16)


def encode(kept, came, flips):
    rows, columns = kept.shape
    return pl.pallas_call(
        encode_body,
        out_shape=jax.ShapeDtypeStruct((rows, columns + BLOCK), jnp.bfloat16),
        in_specs=[VMEM] * 4,
        out_specs=VMEM,
        compiler_params=PARAMS,
        cost_estimate=SMALL,
    )(kept, came, flips, hadamard(BLOCK))


def choose_body(blocks, pieces, width, at, rank_ref, chosen_ref, *refs):
    out_ref = refs[-1]
    rows = refs[0].shape[0]
    scales = width // BLOCK

    def put(block, place):
        begin, scale_at = at[block]
        for piece in range(pieces):
            ref = refs[block * pieces + piece]
            row = (place * pieces + rank_ref[piece]) * rows
            here = pl.ds(pl.multiple_of(row, rows), rows)
            out_ref[here, :width] = ref[:, begin : begin + width]
            out_ref[here, width : width + scales] = ref[:, scale_at : scale_at + scales]

    for place in range(chosen_ref.shape[0]):
        for block in range(blocks):
            pl.when(chosen_ref[place] == block)(functools.partial(put, block, place))


def choose(results, group, width, rank, chosen):
    picked, at = [], []
    for result in results:
        if len(result) == 1:
            pieces, begin = result[0], group * width
            at.append((begin, pieces[0].shape[1] - BLOCK + begin // BLOCK))
        else:
            pieces = result[group]
            at.append((0, width))
        picked.append(pieces)
    rows = picked[0][0].shape[0]
    count = len(picked[0])
    if rows % 16:
        blocks = []
        for pieces, (begin, scale_at) in zip(picked, at):
            block = jnp.zeros((count * rows, width + BLOCK), jnp.bfloat16)
            for index, piece in enumerate(pieces):
                scale = jnp.pad(piece[:, scale_at : scale_at + width // BLOCK], ((0, 0), (0, BLOCK - width // BLOCK)))
                part = jnp.concatenate([piece[:, begin : begin + width], scale], axis=1)
                block = lax.dynamic_update_slice_in_dim(block, part, rank[index] * rows, 0)
            blocks.append(block)
        stacked = jnp.stack(blocks)
        return jnp.concatenate([stacked[chosen[place]] for place in range(chosen.shape[0])])
    return pl.pallas_call(
        functools.partial(choose_body, len(picked), count, width, at),
        out_shape=jax.ShapeDtypeStruct((chosen.shape[0] * count * rows, width + BLOCK), jnp.bfloat16),
        in_specs=[SMEM, SMEM] + [VMEM] * (len(picked) * count),
        out_specs=VMEM,
        compiler_params=PARAMS,
        cost_estimate=SMALL,
    )(rank, chosen, *[piece for pieces in picked for piece in pieces])


def assemble_body(groups, half, here_ref, *refs):
    mine, other = refs[:groups], refs[groups : 2 * groups]
    codes_ref, scales_ref = refs[2 * groups :]
    width = half // groups
    scales = width // BLOCK

    def put(core):
        held = []
        for side, side_refs in ((core, mine), (1 - core, other)):
            for group, ref in enumerate(side_refs):
                begin = side * half + group * width
                codes_ref[:, begin : begin + width] = ref[:, :width]
                held.append((begin, ref[:, width : width + scales].astype(jnp.float32)))
        held = jnp.concatenate([value for _, value in sorted(held, key=lambda pair: pair[0])], axis=1)
        scales_ref[...] = held.T.astype(jnp.bfloat16)

    for core in range(2):
        pl.when(here_ref[0] == core)(functools.partial(put, core))


def assemble(mine, other, here, half):
    rows = mine[0].shape[0]
    codes, scales = pl.pallas_call(
        functools.partial(assemble_body, len(mine), half),
        out_shape=(
            jax.ShapeDtypeStruct((rows, 2 * half), jnp.bfloat16),
            jax.ShapeDtypeStruct((2 * half // BLOCK, rows), jnp.bfloat16),
        ),
        in_specs=[SMEM] + [VMEM] * (2 * len(mine)),
        out_specs=(VMEM, VMEM),
        compiler_params=PARAMS,
        cost_estimate=SMALL,
    )(here, *mine, *other)
    return codes, scales.T


def cut(depth):
    if depth % UNIT or depth < 8 * UNIT:
        return [depth]
    units = depth // UNIT
    sizes = []
    for share in (0.31, 0.31, 0.23):
        sizes.append(max(1, round(units * share)))
    sizes.append(units - sum(sizes))
    return [size * UNIT for size in sizes]


def shards(hidden, down_weight, sign_bits):
    tensor_count = lax.axis_size("tensor")
    seq_count = lax.axis_size("seq")
    sub_count = lax.axis_size("sub")
    tensor_at = lax.axis_index("tensor")
    seq_at = lax.axis_index("seq")
    sub_at = lax.axis_index("sub")
    rows, depth = hidden.shape
    half = down_weight.shape[1] // sub_count
    per_sub = seq_count // sub_count
    levels = tensor_count.bit_length() - 1
    bits = [tensor_at >> level & 1 for level in range(levels)]
    wide, wide_chunk = min(256, half // GROUPS), min(512, half // GROUPS)
    flips = (2 * sign_bits - 1).astype(jnp.float32)[None, :]
    own_flips = lax.dynamic_slice_in_dim(flips, sub_at * half, half, 1)
    here = jnp.reshape(sub_at, (1,)).astype(jnp.int32)

    def swap(values):
        return lax.ppermute(values, "sub", [(0, 1), (1, 0)])

    def exchange(values, level):
        return lax.ppermute(values, "tensor", [(t, t ^ 1 << level) for t in range(tensor_count)])

    def reduce(sent, kept, begin):
        came = swap(sent)
        tokens = []
        for level in range(levels):
            sent, kept = halve(kept, came, bits[level])
            tokens.append(sent)
            came = exchange(sent, level)
        packed = encode(kept, came, own_flips[:, begin : begin + kept.shape[1]])
        return tokens, packed

    def spread(packed):
        pieces = {0: packed}
        for level in reversed(range(levels)):
            for index in list(pieces):
                pieces[index ^ 1 << level] = exchange(pieces[index], level)
        return [pieces[index] for index in range(tensor_count)]

    def rank_of(index):
        return sum((index >> level & 1) << (levels - 1 - level) for level in range(levels))

    sizes = cut(depth)
    places = [(sum(sizes[:index]), size) for index, size in enumerate(sizes)]
    parts = slices_of(hidden, places)
    arrivals = []
    for shift in range(1, seq_count):
        pairs = [(s, (s + shift) % seq_count) for s in range(seq_count)]
        arrivals.append([lax.ppermute(part, "seq", pairs) for part in parts])

    single = len(sizes) == 1
    own = None
    if not single:
        rest = sizes[0]
        (own,) = multiply(
            [(hidden, rest)], down_weight, rest, depth - rest, here, [None], [False], wide, tokens=parts
        )
    outs = multiply(
        [(hidden, 0), (arrivals[0][0], 0)], down_weight, 0, sizes[0], here, [own, None], [True, single], wide_chunk
    )
    (sent, kept), first = outs[:2], outs[2:]
    own_tokens, own_packed = reduce(sent, kept, 0)
    results = [[spread(own_packed)]]
    for shift, arrived in enumerate(arrivals):
        groups = 1 if single else GROUPS
        reduced = []
        if single:
            if shift:
                first = multiply([(arrived[0], 0)], down_weight, 0, depth, here, [None], [True], wide_chunk)
            reduced.append(reduce(*first, 0)[1])
        else:
            total = first[0] if shift == 0 else None
            for index, (at, size) in enumerate(places):
                if index == 0 and shift == 0:
                    continue
                if index == len(places) - 1:
                    break
                tokens = own_tokens[index - 1 : index] if shift == 0 else ()
                (total,) = multiply(
                    [(arrived[index], 0)], down_weight, at, size, here, [total], [False], wide_chunk, tokens=tokens
                )
            tokens = [own_packed] if shift == 0 else ()
            for group in range(groups):
                sent, kept = multiply(
                    [(arrived[index], 0)], down_weight, at, size, here, [total], [True], wide_chunk,
                    group=(group, groups), tokens=tokens,
                )
                tokens = [sent]
                reduced.append(reduce(sent, kept, group * half // groups)[1])
        results.append([spread(packed) for packed in reduced])

    def of_sub(sub):
        return jnp.stack([(seq_at - (sub * per_sub + place)) % seq_count for place in range(per_sub)])

    rank = jnp.stack([rank_of(tensor_at ^ index) for index in range(tensor_count)])
    groups = max(len(result) for result in results)
    width = half // groups
    other = [swap(choose(results, group, width, rank, of_sub(1 - sub_at))) for group in range(groups)]
    mine = [choose(results, group, width, rank, of_sub(sub_at)) for group in range(groups)]
    return assemble(mine, other, here, half)


def solution(mesh):
    return jax.shard_map(
        shards,
        mesh=mesh,
        in_specs=(P(("groups", "seq"), ("tensor", "sub")), P(("tensor", "sub"), "seq"), P("seq")),
        out_specs=(P(("groups", "sub"), "seq"), P(("groups", "sub"), "seq")),
        check_vma=False,
    )
```

```python
import functools
import math

import jax
import jax.numpy as jnp
import numpy as np
from jax import lax
from jax.experimental import pallas as pl
from jax.experimental.pallas import tpu as pltpu
from jax.sharding import PartitionSpec as P

BLOCK = 128
UNIT = 512
GROUPS = 2
BUFFERS = 4
VMEM_LIMIT = 6 * 2**20
SHARES = (3, 3, 3, 2)
epsilon = 1e-06

SMALL = pl.CostEstimate(flops=1, bytes_accessed=1, transcendentals=0)
PARAMS = pltpu.CompilerParams(vmem_limit_bytes=VMEM_LIMIT)
VMEM = pl.BlockSpec(memory_space=pltpu.VMEM)
SMEM = pl.BlockSpec(memory_space=pltpu.SMEM)
ANY = pl.BlockSpec(memory_space=pl.ANY)
HBM = pl.BlockSpec(memory_space=pltpu.HBM)


def hadamard(order):
    indices = np.arange(order)
    parity = np.zeros((order, order), np.int64)
    for position in range(order.bit_length() - 1):
        parity = parity + (indices[:, None] >> position & 1) * (indices[None, :] >> position & 1)
    return ((1 - 2 * (parity % 2)) / math.sqrt(order)).astype(np.float32)


def slice_body(places, in_ref, *refs):
    out_refs, arrived = refs[:-1], refs[-1]
    copies = [
        pltpu.make_async_copy(in_ref.at[:, at : at + size], out_ref, arrived.at[index])
        for index, ((at, size), out_ref) in enumerate(zip(places, out_refs))
    ]
    for copy in copies:
        copy.start()
    for copy in copies:
        copy.wait()


def slices_of(values, places):
    return pl.pallas_call(
        functools.partial(slice_body, places),
        out_shape=[jax.ShapeDtypeStruct((values.shape[0], size), values.dtype) for _, size in places],
        in_specs=[HBM],
        out_specs=[VMEM] * len(places),
        scratch_shapes=[pltpu.SemaphoreType.DMA((len(places),))],
        compiler_params=PARAMS,
        cost_estimate=SMALL,
    )(values)


def resident_body(sizes, row, lead, *refs):
    left_refs, w_ref, refs = refs[: len(sizes)], refs[len(sizes)], refs[len(sizes) + 1 :]
    out_ref, held_ref, sems = refs[lead:]
    columns = w_ref.shape[1]
    steps, wide = sems.shape[0], columns // sems.shape[0]

    def at(n):
        return pl.ds(pl.multiple_of(n * wide, wide), wide)

    def copy(n):
        return pltpu.make_async_copy(w_ref.at[pl.ds(row, sum(sizes)), at(n)], held_ref.at[:, at(n)], sems.at[n])

    for n in range(steps):
        copy(n).start()

    def step(n):
        copy(n).wait()
        total, begin = None, 0
        for left_ref, size in zip(left_refs, sizes):
            product = jnp.dot(
                left_ref[...], held_ref[begin : begin + size, at(n)], preferred_element_type=jnp.float32
            )
            total = product if total is None else total + product
            begin += size
        out_ref[:, at(n)] = total

    pl.loop(0, steps)(step)


def multiply_resident(lefts, weight, row, wide, tokens=()):
    rows, columns = lefts[0].shape[0], weight.shape[1]
    sizes = [left.shape[1] for left in lefts]
    return pl.pallas_call(
        functools.partial(resident_body, sizes, row, len(tokens)),
        out_shape=[
            jax.ShapeDtypeStruct((rows, columns), jnp.float32),
            jax.ShapeDtypeStruct((sum(sizes), columns), weight.dtype),
        ],
        in_specs=[VMEM] * len(lefts) + [HBM] + [ANY] * len(tokens),
        out_specs=[VMEM, VMEM],
        scratch_shapes=[pltpu.SemaphoreType.DMA((columns // wide,))],
        compiler_params=PARAMS,
        cost_estimate=SMALL,
    )(*lefts, weight, *tokens)


def held_body(row, has_total, split, first, number, wide, here_ref, left_ref, w_ref, *refs):
    total_refs, out_refs = refs[:has_total], refs[len(refs) - 1 - split :]
    in_half = w_ref.shape[1] // wide // 2
    steps = 2 * first if split else 2 * in_half

    def at(block):
        return pl.ds(pl.multiple_of(block * wide, wide), wide)

    def step(n, second):
        block = n
        if split:
            block = (here_ref[0] if second else 1 - here_ref[0]) * in_half + number * first + n
            block = block - (first if second else 0)
        value = jnp.dot(left_ref[...], w_ref[row : row + left_ref.shape[1], at(block)], preferred_element_type=jnp.float32)
        if has_total:
            value = value + total_refs[0][:, at(block)]
        if second:
            out_refs[1][:, at(n - first)] = value
        else:
            out_refs[0][:, at(n)] = value.astype(out_refs[0].dtype)

    if split:
        pl.loop(0, first)(functools.partial(step, second=False))
        pl.loop(first, steps)(functools.partial(step, second=True))
    else:
        pl.loop(0, steps)(functools.partial(step, second=False))


def multiply_held(left, weight, row, facts, total, split, wide, group=(0, 1), tokens=()):
    rows, columns = left.shape[0], weight.shape[1]
    number, count = group
    first = columns // wide // 2 // count
    out_shape = [jax.ShapeDtypeStruct((rows, columns), jnp.float32)]
    if split:
        out_shape = [
            jax.ShapeDtypeStruct((rows, first * wide), jnp.bfloat16),
            jax.ShapeDtypeStruct((rows, first * wide), jnp.float32),
        ]
    held = [] if total is None else [total]
    return pl.pallas_call(
        functools.partial(held_body, row, len(held), split, first, number, wide),
        out_shape=out_shape,
        in_specs=[SMEM, VMEM, VMEM] + [VMEM] * len(held) + [ANY] * len(tokens),
        out_specs=[VMEM] * len(out_shape),
        compiler_params=PARAMS,
        cost_estimate=SMALL,
    )(facts, left, weight, *held, *tokens)


def multiply_body(offsets, has_totals, splits, row, first, number, here_ref, *refs):
    lefts = len(offsets)
    left_refs, refs = refs[:lefts], refs[lefts:]
    w_ref, refs = refs[0], refs[1:]
    total_refs, refs = list(refs[: sum(has_totals)]), refs[sum(has_totals) :]
    buffer, arrived = refs[-2:]
    out_count = sum(2 if split else 1 for split in splits)
    out_refs = refs[-2 - out_count : -2]
    buffers, depth, wide = buffer.shape
    rows = left_refs[0].shape[0]
    in_half = w_ref.shape[1] // wide // 2
    steps = 2 * first if any(splits) else 2 * in_half

    def column(n):
        if not any(splits):
            return n
        side = jnp.where(n < first, 1 - here_ref[0], here_ref[0])
        return side * in_half + number * first + n - jnp.where(n < first, 0, first)

    def at(block):
        return pl.ds(pl.multiple_of(block * wide, wide), wide)

    def copy(n):
        slot = lax.rem(n, buffers)
        return pltpu.make_async_copy(
            w_ref.at[pl.ds(row, depth), at(column(n))], buffer.at[slot], arrived.at[slot]
        )

    def step(n, second):
        copy(n).wait()

        @pl.when(n + buffers - 1 < steps)
        def _():
            copy(n + buffers - 1).start()

        parts = [ref[:, offset : offset + depth] for ref, offset in zip(left_refs, offsets)]
        left = parts[0] if lefts == 1 else jnp.concatenate(parts, axis=0)
        product = jnp.dot(left, buffer[lax.rem(n, buffers)], preferred_element_type=jnp.float32)
        totals, outs = list(total_refs), list(out_refs)
        for index in range(lefts):
            value = product[index * rows : (index + 1) * rows]
            if has_totals[index]:
                value = value + totals.pop(0)[:, at(column(n))]
            if splits[index]:
                sent_ref, kept_ref = outs.pop(0), outs.pop(0)
                if second:
                    kept_ref[:, at(n - first)] = value
                else:
                    sent_ref[:, at(n)] = value.astype(sent_ref.dtype)
            else:
                outs.pop(0)[:, at(column(n))] = value

    for n in range(min(buffers - 1, steps)):
        copy(jnp.int32(n)).start()
    pl.loop(0, first)(functools.partial(step, second=False))
    pl.loop(first, steps)(functools.partial(step, second=True))


def multiply(lefts, weight, row, depth, facts, totals, splits, wide, group=None, tokens=()):
    rows = lefts[0][0].shape[0]
    columns = weight.shape[1]
    number, count = group or (0, 1)
    first = columns // wide // 2 // count
    held = [total for total in totals if total is not None]
    out_shape = []
    for split in splits:
        if split:
            out_shape += [
                jax.ShapeDtypeStruct((rows, first * wide), jnp.bfloat16),
                jax.ShapeDtypeStruct((rows, first * wide), jnp.float32),
            ]
        else:
            out_shape.append(jax.ShapeDtypeStruct((rows, columns), jnp.float32))
    body = functools.partial(
        multiply_body,
        [offset for _, offset in lefts],
        [total is not None for total in totals],
        splits,
        row,
        first,
        number,
    )
    return pl.pallas_call(
        body,
        out_shape=out_shape,
        in_specs=[SMEM]
        + [VMEM] * len(lefts)
        + [HBM]
        + [VMEM] * len(held)
        + [ANY] * len(tokens),
        out_specs=[VMEM] * len(out_shape),
        scratch_shapes=[
            pltpu.VMEM((BUFFERS, depth, wide), weight.dtype),
            pltpu.SemaphoreType.DMA((BUFFERS,)),
        ],
        compiler_params=PARAMS,
        cost_estimate=SMALL,
    )(facts, *[left for left, _ in lefts], weight, *held, *tokens)


def halve_body(level, facts_ref, kept_ref, came_ref, *refs):
    sent_out, kept_out = refs[-2:]
    half = sent_out.shape[0]

    def put(bit):
        mine, other = slice(bit * half, (bit + 1) * half), slice((1 - bit) * half, (2 - bit) * half)
        kept_out[...] = kept_ref[mine] + came_ref[mine].astype(jnp.float32)
        sent_out[...] = (kept_ref[other] + came_ref[other].astype(jnp.float32)).astype(jnp.bfloat16)

    for bit in range(2):
        pl.when(facts_ref[1 + level] == bit)(functools.partial(put, bit))


def halve(kept, came, level, facts, tokens=()):
    rows, columns = kept.shape
    half = rows // 2
    if half % 16:
        total, bit = kept + came.astype(jnp.float32), facts[1 + level]
        sent = lax.dynamic_slice_in_dim(total, (1 - bit) * half, half, 0).astype(jnp.bfloat16)
        return sent, lax.dynamic_slice_in_dim(total, bit * half, half, 0)
    return pl.pallas_call(
        functools.partial(halve_body, level),
        out_shape=[
            jax.ShapeDtypeStruct((half, columns), jnp.bfloat16),
            jax.ShapeDtypeStruct((half, columns), jnp.float32),
        ],
        in_specs=[SMEM, VMEM, VMEM] + [ANY] * len(tokens),
        out_specs=[VMEM, VMEM],
        compiler_params=PARAMS,
        cost_estimate=SMALL,
    )(facts, kept, came, *tokens)


def encode_body(begin, facts_ref, kept_ref, came_ref, flips_ref, rotation_ref, *refs):
    out_ref = refs[-1]
    rows, columns = kept_ref.shape
    half = flips_ref.shape[1] // 2
    rotation = rotation_ref[...]
    lane = lax.broadcasted_iota(jnp.int32, (rows, BLOCK), 1)
    scales = jnp.zeros((rows, BLOCK), jnp.float32)
    for block in range(columns // BLOCK):
        at = slice(block * BLOCK, (block + 1) * BLOCK)
        flips = flips_ref[:, pl.ds(pl.multiple_of(facts_ref[0] * half + begin + block * BLOCK, BLOCK), BLOCK)]
        total = (kept_ref[:, at] + came_ref[:, at].astype(jnp.float32)) * flips
        rotated = jnp.dot(
            total, rotation, precision=lax.Precision.HIGHEST, preferred_element_type=jnp.float32
        )
        largest = jnp.max(jnp.abs(rotated), axis=1, keepdims=True)
        scale = (largest + epsilon).astype(jnp.bfloat16).astype(jnp.float32)
        out_ref[:, at] = (rotated / scale).astype(jnp.bfloat16)
        scales = jnp.where(lane == block, scale, scales)
    out_ref[:, columns:] = scales.astype(jnp.bfloat16)


def encode(kept, came, begin, facts, flips, rotation, tokens=()):
    rows, columns = kept.shape
    return pl.pallas_call(
        functools.partial(encode_body, begin),
        out_shape=jax.ShapeDtypeStruct((rows, columns + BLOCK), jnp.bfloat16),
        in_specs=[SMEM] + [VMEM] * 4 + [ANY] * len(tokens),
        out_specs=VMEM,
        compiler_params=PARAMS,
        cost_estimate=SMALL,
    )(facts, kept, came, flips, rotation, *tokens)


def choose_body(blocks, pieces, width, at, rank, chosen, places, facts_ref, *refs):
    out_ref = refs[-1]
    rows = refs[0].shape[0]
    scales = width // BLOCK

    def put(block, place):
        begin, scale_at = at[block]
        for piece in range(pieces):
            ref = refs[block * pieces + piece]
            row = (place * pieces + facts_ref[rank + piece]) * rows
            here = pl.ds(pl.multiple_of(row, rows), rows)
            out_ref[here, :width] = ref[:, begin : begin + width]
            out_ref[here, width : width + scales] = ref[:, scale_at : scale_at + scales]

    for place in range(places):
        for block in range(blocks):
            pl.when(facts_ref[chosen + place] == block)(functools.partial(put, block, place))


def choose(results, group, width, rank, chosen, places, facts):
    picked, at = [], []
    for result in results:
        if len(result) == 1:
            pieces, begin = result[0], group * width
            at.append((begin, pieces[0].shape[1] - BLOCK + begin // BLOCK))
        else:
            pieces = result[group]
            at.append((0, width))
        picked.append(pieces)
    rows = picked[0][0].shape[0]
    count = len(picked[0])
    if rows % 16:
        blocks = []
        for pieces, (begin, scale_at) in zip(picked, at):
            block = jnp.zeros((count * rows, width + BLOCK), jnp.bfloat16)
            for index, piece in enumerate(pieces):
                scale = jnp.pad(piece[:, scale_at : scale_at + width // BLOCK], ((0, 0), (0, BLOCK - width // BLOCK)))
                part = jnp.concatenate([piece[:, begin : begin + width], scale], axis=1)
                block = lax.dynamic_update_slice_in_dim(block, part, facts[rank + index] * rows, 0)
            blocks.append(block)
        stacked = jnp.stack(blocks)
        return jnp.concatenate([stacked[facts[chosen + place]] for place in range(places)])
    return pl.pallas_call(
        functools.partial(choose_body, len(picked), count, width, at, rank, chosen, places),
        out_shape=jax.ShapeDtypeStruct((places * count * rows, width + BLOCK), jnp.bfloat16),
        in_specs=[SMEM] + [VMEM] * (len(picked) * count),
        out_specs=VMEM,
        compiler_params=PARAMS,
        cost_estimate=SMALL,
    )(facts, *[piece for pieces in picked for piece in pieces])


def assemble_body(groups, half, here_ref, *refs):
    mine, other = refs[:groups], refs[groups : 2 * groups]
    codes_ref, scales_ref = refs[2 * groups :]
    width = half // groups
    scales = width // BLOCK

    def put(core):
        held = []
        for side, side_refs in ((core, mine), (1 - core, other)):
            for group, ref in enumerate(side_refs):
                begin = side * half + group * width
                codes_ref[:, begin : begin + width] = ref[:, :width]
                held.append((begin, ref[:, width : width + scales].astype(jnp.float32)))
        held = jnp.concatenate([value for _, value in sorted(held, key=lambda pair: pair[0])], axis=1)
        scales_ref[...] = held.T.astype(jnp.bfloat16)

    for core in range(2):
        pl.when(here_ref[0] == core)(functools.partial(put, core))


def assemble(mine, other, facts, half):
    rows = mine[0].shape[0]
    codes, scales = pl.pallas_call(
        functools.partial(assemble_body, len(mine), half),
        out_shape=(
            jax.ShapeDtypeStruct((rows, 2 * half), jnp.bfloat16),
            jax.ShapeDtypeStruct((2 * half // BLOCK, rows), jnp.bfloat16),
        ),
        in_specs=[SMEM] + [VMEM] * (2 * len(mine)),
        out_specs=(VMEM, VMEM),
        compiler_params=PARAMS,
        cost_estimate=SMALL,
    )(facts, *mine, *other)
    return codes, scales.T


def cut(depth):
    if depth % UNIT or depth < 8 * UNIT:
        return [depth]
    units = depth // UNIT
    sizes = [max(1, units * share // 13) for share in SHARES]
    return [size * UNIT for size in sizes + [units - sum(sizes)]]


def shards(hidden, down_weight, sign_bits):
    tensor_count = lax.axis_size("tensor")
    seq_count = lax.axis_size("seq")
    sub_count = lax.axis_size("sub")
    tensor_at = lax.axis_index("tensor")
    seq_at = lax.axis_index("seq")
    sub_at = lax.axis_index("sub")
    rows, depth = hidden.shape
    half = down_weight.shape[1] // sub_count
    per_sub = seq_count // sub_count
    levels = tensor_count.bit_length() - 1
    wide, wide_chunk = min(256, half // GROUPS), min(512, half // GROUPS)
    flips = (2 * sign_bits - 1).astype(jnp.float32)[None, :]
    rotation = jnp.asarray(hadamard(BLOCK))

    def rank_of(index):
        return sum((index >> level & 1) << (levels - 1 - level) for level in range(levels))

    def of_sub(sub):
        return [lax.rem(seq_at - (sub * per_sub + place) + seq_count, seq_count) for place in range(per_sub)]

    facts = [sub_at] + [tensor_at >> level & 1 for level in range(levels)]
    ranks = len(facts)
    facts += [rank_of(tensor_at ^ index) for index in range(tensor_count)]
    own_choice = len(facts)
    facts += of_sub(sub_at)
    other_choice = len(facts)
    facts += of_sub(1 - sub_at)
    facts = jnp.stack(facts).astype(jnp.int32)

    def swap(values):
        return lax.ppermute(values, "sub", [(0, 1), (1, 0)])

    def exchange(values, level):
        return lax.ppermute(values, "tensor", [(t, t ^ 1 << level) for t in range(tensor_count)])

    def reduce(sent, kept, begin):
        tokens = (yield None) or []
        came = swap(sent)
        for level in range(levels):
            sent, kept = halve(kept, came, level, facts, tokens)
            tokens = (yield sent) or []
            came = exchange(sent, level)
        yield encode(kept, came, begin, facts, flips, rotation, tokens)

    def spread(packed):
        pieces = {0: packed}
        for level in reversed(range(levels)):
            for index in list(pieces):
                pieces[index ^ 1 << level] = exchange(pieces[index], level)
        return [pieces[index] for index in range(tensor_count)]

    sizes = cut(depth)
    places = [(sum(sizes[:index]), size) for index, size in enumerate(sizes)]
    parts = slices_of(hidden, places)
    arrivals = []
    for shift in range(1, seq_count):
        pairs = [(s, (s + shift) % seq_count) for s in range(seq_count)]
        arrivals.append([lax.ppermute(part, "seq", pairs) for part in parts])

    if len(sizes) == 1:
        outs = multiply(
            [(parts[0], 0), (arrivals[0][0], 0)], down_weight, 0, depth, facts, [None, None], [True, True], wide_chunk
        )
        reduced = [list(reduce(*outs[:2], 0))[-1], list(reduce(*outs[2:], 0))[-1]]
        for arrived in arrivals[1:]:
            outs = multiply([(arrived[0], 0)], down_weight, 0, depth, facts, [None], [True], wide_chunk)
            reduced.append(list(reduce(*outs, 0))[-1])
        results = [[spread(packed)] for packed in reduced]
    else:
        own, held = multiply_resident(
            parts[1:], down_weight, sizes[0], wide, tokens=[parts[0], facts, flips, rotation]
        )
        sent, kept, total = multiply(
            [(parts[0], 0), (arrivals[0][0], 0)], down_weight, 0, sizes[0], facts, [own, None], [True, False], wide
        )
        own_steps = reduce(sent, kept, 0)
        next(own_steps)
        own_packed, tokens = None, []
        results = []
        for shift, arrived in enumerate(arrivals):
            if shift:
                (total,) = multiply([(arrived[0], 0)], down_weight, 0, sizes[0], facts, [None], [False], wide)
            for index in range(1, len(sizes) - 1):
                (total,) = multiply_held(
                    arrived[index], held, places[index][0] - sizes[0], facts, total, False, wide_chunk, tokens=tokens
                )
                if own_packed is None:
                    step = own_steps.send([total])
                    tokens = [step]
                    if step.shape[1] > half:
                        own_packed = step
            remote_steps = []
            for group in range(GROUPS):
                sent, kept = multiply_held(
                    arrived[-1], held, places[-1][0] - sizes[0], facts, total, True, wide_chunk,
                    group=(group, GROUPS), tokens=tokens,
                )
                tokens = [sent]
                remote_steps.append(reduce(sent, kept, group * half // GROUPS))
            if own_packed is None:
                own_packed = list(own_steps)[-1]
            if not results:
                results.append([spread(own_packed)])
            results.append([spread(list(steps)[-1]) for steps in remote_steps])
            tokens = []

    groups = max(len(result) for result in results)
    width = half // groups
    other = [swap(choose(results, group, width, ranks, other_choice, per_sub, facts)) for group in range(groups)]
    mine = [choose(results, group, width, ranks, own_choice, per_sub, facts) for group in range(groups)]
    return assemble(mine, other, facts, half)


def solution(mesh):
    return jax.shard_map(
        shards,
        mesh=mesh,
        in_specs=(P(("groups", "seq"), ("tensor", "sub")), P(("tensor", "sub"), "seq"), P("seq")),
        out_specs=(P(("groups", "sub"), "seq"), P(("groups", "sub"), "seq")),
        check_vma=False,
    )
```

```python
import functools
import math

import jax
import jax.numpy as jnp
import numpy as np
from jax import lax
from jax.experimental import pallas as pl
from jax.experimental.pallas import tpu as pltpu
from jax.sharding import PartitionSpec as P

BLOCK = 128
UNIT = 512
GROUPS = 2
VMEM_LIMIT = 6 * 2**20
SHARES = (4, 4, 3)
epsilon = 1e-06

SMALL = pl.CostEstimate(flops=1, bytes_accessed=1, transcendentals=0)
PARAMS = pltpu.CompilerParams(vmem_limit_bytes=VMEM_LIMIT)
VMEM = pl.BlockSpec(memory_space=pltpu.VMEM)
SMEM = pl.BlockSpec(memory_space=pltpu.SMEM)
ANY = pl.BlockSpec(memory_space=pl.ANY)
HBM = pl.BlockSpec(memory_space=pltpu.HBM)


def hadamard(order):
    indices = np.arange(order)
    parity = np.zeros((order, order), np.int64)
    for position in range(order.bit_length() - 1):
        parity = parity + (indices[:, None] >> position & 1) * (indices[None, :] >> position & 1)
    return ((1 - 2 * (parity % 2)) / math.sqrt(order)).astype(np.float32)


def slice_body(places, in_ref, *refs):
    out_refs, arrived = refs[:-1], refs[-1]
    copies = [
        pltpu.make_async_copy(in_ref.at[:, at : at + size], out_ref, arrived.at[index])
        for index, ((at, size), out_ref) in enumerate(zip(places, out_refs))
    ]
    for copy in copies:
        copy.start()
    for copy in copies:
        copy.wait()


def slices_of(values, places):
    return pl.pallas_call(
        functools.partial(slice_body, places),
        out_shape=[jax.ShapeDtypeStruct((values.shape[0], size), values.dtype) for _, size in places],
        in_specs=[HBM],
        out_specs=[VMEM] * len(places),
        scratch_shapes=[pltpu.SemaphoreType.DMA((len(places),))],
        compiler_params=PARAMS,
        cost_estimate=SMALL,
    )(values)


def multiply_body(spans, has_totals, splits, row, first, number, facts_ref, *refs):
    lefts = [refs[begin:end] for begin, end in spans]
    refs = refs[spans[-1][1] :]
    w_ref, refs = refs[0], refs[1:]
    total_refs, refs = list(refs[: sum(has_totals)]), refs[sum(has_totals) :]
    buffer, arrived = refs[-2:]
    out_count = sum(2 if split else 1 for split in splits)
    out_refs = refs[-2 - out_count : -2]
    steps, depth, wide = buffer.shape
    rows = lefts[0][0].shape[0]
    in_half = w_ref.shape[1] // wide // 2

    def column(n):
        if not any(splits):
            return n
        side = jnp.where(n < first, 1 - facts_ref[0], facts_ref[0])
        return side * in_half + number * first + n - jnp.where(n < first, 0, first)

    def at(block):
        return pl.ds(pl.multiple_of(block * wide, wide), wide)

    def copy(n):
        return pltpu.make_async_copy(w_ref.at[pl.ds(row, depth), at(column(n))], buffer.at[n], arrived.at[n])

    def step(n, second):
        copy(n).wait()
        product, begin = None, 0
        for index in range(len(lefts[0])):
            parts = [left[index][...] for left in lefts]
            left = parts[0] if len(parts) == 1 else jnp.concatenate(parts, axis=0)
            end = begin + left.shape[1]
            part = jnp.dot(left, buffer[n, begin:end], preferred_element_type=jnp.float32)
            product = part if product is None else product + part
            begin = end
        totals, outs = list(total_refs), list(out_refs)
        for index in range(len(lefts)):
            value = product[index * rows : (index + 1) * rows]
            if has_totals[index]:
                value = value + totals.pop(0)[:, at(column(n))]
            if splits[index]:
                sent_ref, kept_ref = outs.pop(0), outs.pop(0)
                if second:
                    kept_ref[:, at(n - first)] = value
                else:
                    sent_ref[:, at(n)] = value.astype(sent_ref.dtype)
            else:
                outs.pop(0)[:, at(column(n))] = value

    for n in range(steps):
        copy(n).start()
    pl.loop(0, first)(functools.partial(step, second=False))
    pl.loop(first, steps)(functools.partial(step, second=True))


def multiply(lefts, weight, row, facts, totals, splits, wide, group=(0, 1), tokens=()):
    rows = lefts[0][0].shape[0]
    depth = sum(part.shape[1] for part in lefts[0])
    columns = weight.shape[1]
    number, count = group
    first = columns // wide // 2 // count
    steps = 2 * first if any(splits) else columns // wide
    spans = [(index * len(left), (index + 1) * len(left)) for index, left in enumerate(lefts)]
    held = [total for total in totals if total is not None]
    out_shape = []
    for split in splits:
        if split:
            out_shape += [
                jax.ShapeDtypeStruct((rows, first * wide), jnp.bfloat16),
                jax.ShapeDtypeStruct((rows, first * wide), jnp.float32),
            ]
        else:
            out_shape.append(jax.ShapeDtypeStruct((rows, columns), jnp.float32))
    body = functools.partial(
        multiply_body, spans, [total is not None for total in totals], splits, row, first, number
    )
    return pl.pallas_call(
        body,
        out_shape=out_shape,
        in_specs=[SMEM]
        + [VMEM] * spans[-1][1]
        + [HBM]
        + [VMEM] * len(held)
        + [ANY] * len(tokens),
        out_specs=[VMEM] * len(out_shape),
        scratch_shapes=[
            pltpu.VMEM((steps, depth, wide), weight.dtype),
            pltpu.SemaphoreType.DMA((steps,)),
        ],
        compiler_params=pltpu.CompilerParams(
            vmem_limit_bytes=2 * steps * depth * wide + VMEM_LIMIT
        ),
        cost_estimate=SMALL,
    )(facts, *[part for left in lefts for part in left], weight, *held, *tokens)


def halve_body(level, facts_ref, kept_ref, came_ref, *refs):
    sent_out, kept_out = refs[-2:]
    half = sent_out.shape[0]

    def put(bit):
        mine, other = slice(bit * half, (bit + 1) * half), slice((1 - bit) * half, (2 - bit) * half)
        kept_out[...] = kept_ref[mine] + came_ref[mine].astype(jnp.float32)
        sent_out[...] = (kept_ref[other] + came_ref[other].astype(jnp.float32)).astype(jnp.bfloat16)

    for bit in range(2):
        pl.when(facts_ref[1 + level] == bit)(functools.partial(put, bit))


def halve(kept, came, level, facts, tokens=()):
    rows, columns = kept.shape
    half = rows // 2
    if half % 16:
        total, bit = kept + came.astype(jnp.float32), facts[1 + level]
        sent = lax.dynamic_slice_in_dim(total, (1 - bit) * half, half, 0).astype(jnp.bfloat16)
        return sent, lax.dynamic_slice_in_dim(total, bit * half, half, 0)
    return pl.pallas_call(
        functools.partial(halve_body, level),
        out_shape=[
            jax.ShapeDtypeStruct((half, columns), jnp.bfloat16),
            jax.ShapeDtypeStruct((half, columns), jnp.float32),
        ],
        in_specs=[SMEM, VMEM, VMEM] + [ANY] * len(tokens),
        out_specs=[VMEM, VMEM],
        compiler_params=PARAMS,
        cost_estimate=SMALL,
    )(facts, kept, came, *tokens)


def encode_body(begin, facts_ref, kept_ref, came_ref, flips_ref, rotation_ref, *refs):
    out_ref = refs[-1]
    rows, columns = kept_ref.shape
    half = flips_ref.shape[1] // 2
    rotation = rotation_ref[...]
    lane = lax.broadcasted_iota(jnp.int32, (rows, BLOCK), 1)
    scales = jnp.zeros((rows, BLOCK), jnp.float32)
    for block in range(columns // BLOCK):
        at = slice(block * BLOCK, (block + 1) * BLOCK)
        flips = flips_ref[:, pl.ds(pl.multiple_of(facts_ref[0] * half + begin + block * BLOCK, BLOCK), BLOCK)]
        total = (kept_ref[:, at] + came_ref[:, at].astype(jnp.float32)) * flips
        rotated = jnp.dot(
            total, rotation, precision=lax.Precision.HIGHEST, preferred_element_type=jnp.float32
        )
        largest = jnp.max(jnp.abs(rotated), axis=1, keepdims=True)
        scale = (largest + epsilon).astype(jnp.bfloat16).astype(jnp.float32)
        out_ref[:, at] = (rotated / scale).astype(jnp.bfloat16)
        scales = jnp.where(lane == block, scale, scales)
    out_ref[:, columns:] = scales.astype(jnp.bfloat16)


def encode(kept, came, begin, facts, flips, rotation, tokens=()):
    rows, columns = kept.shape
    return pl.pallas_call(
        functools.partial(encode_body, begin),
        out_shape=jax.ShapeDtypeStruct((rows, columns + BLOCK), jnp.bfloat16),
        in_specs=[SMEM] + [VMEM] * 4 + [ANY] * len(tokens),
        out_specs=VMEM,
        compiler_params=PARAMS,
        cost_estimate=SMALL,
    )(facts, kept, came, flips, rotation, *tokens)


def choose_body(blocks, pieces, width, at, rank, chosen, places, facts_ref, *refs):
    out_ref = refs[-1]
    rows = refs[0].shape[0]
    scales = width // BLOCK

    def put(block, place):
        begin, scale_at = at[block]
        for piece in range(pieces):
            ref = refs[block * pieces + piece]
            row = (place * pieces + facts_ref[rank + piece]) * rows
            here = pl.ds(pl.multiple_of(row, rows), rows)
            out_ref[here, :width] = ref[:, begin : begin + width]
            out_ref[here, width : width + scales] = ref[:, scale_at : scale_at + scales]

    for place in range(places):
        for block in range(blocks):
            pl.when(facts_ref[chosen + place] == block)(functools.partial(put, block, place))


def choose(results, group, width, rank, chosen, places, facts):
    picked, at = [], []
    for result in results:
        if len(result) == 1:
            pieces, begin = result[0], group * width
            at.append((begin, pieces[0].shape[1] - BLOCK + begin // BLOCK))
        else:
            pieces = result[group]
            at.append((0, width))
        picked.append(pieces)
    rows = picked[0][0].shape[0]
    count = len(picked[0])
    if rows % 16:
        blocks = []
        for pieces, (begin, scale_at) in zip(picked, at):
            block = jnp.zeros((count * rows, width + BLOCK), jnp.bfloat16)
            for index, piece in enumerate(pieces):
                scale = jnp.pad(piece[:, scale_at : scale_at + width // BLOCK], ((0, 0), (0, BLOCK - width // BLOCK)))
                part = jnp.concatenate([piece[:, begin : begin + width], scale], axis=1)
                block = lax.dynamic_update_slice_in_dim(block, part, facts[rank + index] * rows, 0)
            blocks.append(block)
        stacked = jnp.stack(blocks)
        return jnp.concatenate([stacked[facts[chosen + place]] for place in range(places)])
    return pl.pallas_call(
        functools.partial(choose_body, len(picked), count, width, at, rank, chosen, places),
        out_shape=jax.ShapeDtypeStruct((places * count * rows, width + BLOCK), jnp.bfloat16),
        in_specs=[SMEM] + [VMEM] * (len(picked) * count),
        out_specs=VMEM,
        compiler_params=PARAMS,
        cost_estimate=SMALL,
    )(facts, *[piece for pieces in picked for piece in pieces])


def assemble_body(groups, half, here_ref, *refs):
    mine, other = refs[:groups], refs[groups : 2 * groups]
    codes_ref, scales_ref = refs[2 * groups :]
    width = half // groups
    scales = width // BLOCK

    def put(core):
        held = []
        for side, side_refs in ((core, mine), (1 - core, other)):
            for group, ref in enumerate(side_refs):
                begin = side * half + group * width
                codes_ref[:, begin : begin + width] = ref[:, :width]
                held.append((begin, ref[:, width : width + scales].astype(jnp.float32)))
        held = jnp.concatenate([value for _, value in sorted(held, key=lambda pair: pair[0])], axis=1)
        scales_ref[...] = held.T.astype(jnp.bfloat16)

    for core in range(2):
        pl.when(here_ref[0] == core)(functools.partial(put, core))


def assemble(mine, other, facts, half):
    rows = mine[0].shape[0]
    codes, scales = pl.pallas_call(
        functools.partial(assemble_body, len(mine), half),
        out_shape=(
            jax.ShapeDtypeStruct((rows, 2 * half), jnp.bfloat16),
            jax.ShapeDtypeStruct((2 * half // BLOCK, rows), jnp.bfloat16),
        ),
        in_specs=[SMEM] + [VMEM] * (2 * len(mine)),
        out_specs=(VMEM, VMEM),
        compiler_params=PARAMS,
        cost_estimate=SMALL,
    )(facts, *mine, *other)
    return codes, scales.T


def cut(depth):
    if depth % UNIT or depth < 8 * UNIT:
        return [depth]
    units = depth // UNIT
    sizes = [max(1, units * share // 13) for share in SHARES]
    return [size * UNIT for size in sizes + [units - sum(sizes)]]


def shards(hidden, down_weight, sign_bits):
    tensor_count = lax.axis_size("tensor")
    seq_count = lax.axis_size("seq")
    sub_count = lax.axis_size("sub")
    tensor_at = lax.axis_index("tensor")
    seq_at = lax.axis_index("seq")
    sub_at = lax.axis_index("sub")
    rows, depth = hidden.shape
    half = down_weight.shape[1] // sub_count
    per_sub = seq_count // sub_count
    levels = tensor_count.bit_length() - 1
    wide, wide_chunk = min(256, half // GROUPS), min(512, half // GROUPS)
    flips = (2 * sign_bits - 1).astype(jnp.float32)[None, :]
    rotation = jnp.asarray(hadamard(BLOCK))

    def rank_of(index):
        return sum((index >> level & 1) << (levels - 1 - level) for level in range(levels))

    def of_sub(sub):
        return [lax.rem(seq_at - (sub * per_sub + place) + seq_count, seq_count) for place in range(per_sub)]

    facts = [sub_at] + [tensor_at >> level & 1 for level in range(levels)]
    ranks = len(facts)
    facts += [rank_of(tensor_at ^ index) for index in range(tensor_count)]
    own_choice = len(facts)
    facts += of_sub(sub_at)
    other_choice = len(facts)
    facts += of_sub(1 - sub_at)
    facts = jnp.stack(facts).astype(jnp.int32)

    def swap(values):
        return lax.ppermute(values, "sub", [(0, 1), (1, 0)])

    def exchange(values, level):
        return lax.ppermute(values, "tensor", [(t, t ^ 1 << level) for t in range(tensor_count)])

    def reduce(sent, kept, begin):
        tokens = (yield None) or []
        came = swap(sent)
        for level in range(levels):
            sent, kept = halve(kept, came, level, facts, tokens)
            tokens = (yield sent) or []
            came = exchange(sent, level)
        yield encode(kept, came, begin, facts, flips, rotation, tokens)

    def spread(packed):
        pieces = {0: packed}
        for level in reversed(range(levels)):
            for index in list(pieces):
                pieces[index ^ 1 << level] = exchange(pieces[index], level)
        return [pieces[index] for index in range(tensor_count)]

    sizes = cut(depth)
    places = [(sum(sizes[:index]), size) for index, size in enumerate(sizes)]
    parts = slices_of(hidden, places)
    arrivals = []
    for shift in range(1, seq_count):
        pairs = [(s, (s + shift) % seq_count) for s in range(seq_count)]
        arrivals.append([lax.ppermute(part, "seq", pairs) for part in parts])

    if len(sizes) == 1:
        outs = multiply(
            [[parts[0]], [arrivals[0][0]]], down_weight, 0, facts, [None, None], [True, True], wide_chunk
        )
        reduced = [list(reduce(*outs[:2], 0))[-1], list(reduce(*outs[2:], 0))[-1]]
        for arrived in arrivals[1:]:
            outs = multiply([[arrived[0]]], down_weight, 0, facts, [None], [True], wide_chunk)
            reduced.append(list(reduce(*outs, 0))[-1])
        results = [[spread(packed)] for packed in reduced]
    else:
        (own,) = multiply(
            [parts[1:]], down_weight, sizes[0], facts, [None], [False], wide,
            tokens=[parts[0], flips, rotation],
        )
        sent, kept, total = multiply(
            [[parts[0]], [arrivals[0][0]]], down_weight, 0, facts, [own, None], [True, False], wide_chunk
        )
        own_steps = reduce(sent, kept, 0)
        next(own_steps)
        own_packed, tokens = None, []
        results = []
        for shift, arrived in enumerate(arrivals):
            if shift:
                (total,) = multiply([[arrived[0]]], down_weight, 0, facts, [None], [False], wide_chunk)
            for index in range(1, len(sizes) - 1):
                (total,) = multiply(
                    [[arrived[index]]], down_weight, places[index][0], facts, [total], [False], wide_chunk, tokens=tokens
                )
                if own_packed is None:
                    step = own_steps.send([total])
                    tokens = [step]
                    if step.shape[1] > half:
                        own_packed = step
            remote_steps = []
            for group in range(GROUPS):
                sent, kept = multiply(
                    [[arrived[-1]]], down_weight, places[-1][0], facts, [total], [True], wide_chunk,
                    group=(group, GROUPS), tokens=tokens,
                )
                tokens = [sent]
                remote_steps.append(reduce(sent, kept, group * half // GROUPS))
                if own_packed is None:
                    own_packed = own_steps.send(tokens)
                    tokens = [own_packed]
            if not results:
                results.append([spread(own_packed)])
            results.append([spread(list(steps)[-1]) for steps in remote_steps])
            tokens = []

    groups = max(len(result) for result in results)
    width = half // groups
    other = [swap(choose(results, group, width, ranks, other_choice, per_sub, facts)) for group in range(groups)]
    mine = [choose(results, group, width, ranks, own_choice, per_sub, facts) for group in range(groups)]
    return assemble(mine, other, facts, half)


def solution(mesh):
    return jax.shard_map(
        shards,
        mesh=mesh,
        in_specs=(P(("groups", "seq"), ("tensor", "sub")), P(("tensor", "sub"), "seq"), P("seq")),
        out_specs=(P(("groups", "sub"), "seq"), P(("groups", "sub"), "seq")),
        check_vma=False,
    )
```

```python
import functools
import math

import jax
import jax.numpy as jnp
import numpy as np
from jax import lax
from jax.experimental import pallas as pl
from jax.experimental.pallas import tpu as pltpu
from jax.sharding import PartitionSpec as P

BLOCK = 128
UNIT = 512
GROUPS = 2
VMEM_LIMIT = 6 * 2**20
SHARES = (4, 5, 2)
epsilon = 1e-06

SMALL = pl.CostEstimate(flops=1, bytes_accessed=1, transcendentals=0)
PARAMS = pltpu.CompilerParams(vmem_limit_bytes=VMEM_LIMIT)
VMEM = pl.BlockSpec(memory_space=pltpu.VMEM)
ANY = pl.BlockSpec(memory_space=pl.ANY)
HBM = pl.BlockSpec(memory_space=pltpu.HBM)


def hadamard(order):
    indices = np.arange(order)
    parity = np.zeros((order, order), np.int64)
    for position in range(order.bit_length() - 1):
        parity = parity + (indices[:, None] >> position & 1) * (indices[None, :] >> position & 1)
    return ((1 - 2 * (parity % 2)) / math.sqrt(order)).astype(np.float32)


def slice_body(places, in_ref, *refs):
    out_refs, arrived = refs[:-1], refs[-1]
    copies = [
        pltpu.make_async_copy(in_ref.at[:, at : at + size], out_ref, arrived.at[index])
        for index, ((at, size), out_ref) in enumerate(zip(places, out_refs))
    ]
    for copy in copies:
        copy.start()
    for copy in copies:
        copy.wait()


def slices_of(values, places):
    return pl.pallas_call(
        functools.partial(slice_body, places),
        out_shape=[jax.ShapeDtypeStruct((values.shape[0], size), values.dtype) for _, size in places],
        in_specs=[HBM],
        out_specs=[VMEM] * len(places),
        scratch_shapes=[pltpu.SemaphoreType.DMA((len(places),))],
        compiler_params=PARAMS,
        cost_estimate=SMALL,
    )(values)


def multiply_body(spans, has_totals, splits, row, groups, *refs):
    lefts = [refs[begin:end] for begin, end in spans]
    refs = refs[spans[-1][1] :]
    w_ref, refs = refs[0], refs[1:]
    total_refs, refs = list(refs[: sum(has_totals)]), refs[sum(has_totals) :]
    buffer, arrived = refs[-2:]
    out_count = sum(2 * groups if split else 1 for split in splits)
    out_refs = refs[-2 - out_count : -2]
    steps, depth, wide = buffer.shape
    rows = lefts[0][0].shape[0]
    first = steps // 2 // groups
    here = lax.axis_index("sub")

    def column(n):
        if not any(splits):
            return n
        group, place = n // (2 * first), n % (2 * first)
        side, place = (here, place - first) if place >= first else (1 - here, place)
        return side * (steps // 2) + group * first + place

    def at(block):
        return pl.ds(pl.multiple_of(block * wide, wide), wide)

    def copy(n):
        return pltpu.make_async_copy(w_ref.at[pl.ds(row, depth), at(column(n))], buffer.at[n], arrived.at[n])

    def step(n):
        copy(n).wait()
        product, begin = None, 0
        for index in range(len(lefts[0])):
            parts = [left[index][...] for left in lefts]
            left = parts[0] if len(parts) == 1 else jnp.concatenate(parts, axis=0)
            end = begin + left.shape[1]
            part = jnp.dot(left, buffer[n, begin:end], preferred_element_type=jnp.float32)
            product = part if product is None else product + part
            begin = end
        totals, outs = list(total_refs), list(out_refs)
        for index in range(len(lefts)):
            value = product[index * rows : (index + 1) * rows]
            if has_totals[index]:
                value = value + totals.pop(0)[:, at(column(n))]
            if splits[index]:
                group, place = n // (2 * first), n % (2 * first)
                out_ref = outs[2 * group + place // first]
                begin = place % first * wide
                out_ref[:, begin : begin + wide] = value.astype(out_ref.dtype)
                outs = outs[2 * groups :]
            else:
                outs.pop(0)[:, at(column(n))] = value

    for n in range(steps):
        copy(n).start()
    if any(splits):
        for n in range(steps):
            step(n)
    else:
        pl.loop(0, steps)(step)


def multiply(lefts, weight, row, totals, splits, wide, groups=1, tokens=()):
    rows = lefts[0][0].shape[0]
    depth = sum(part.shape[1] for part in lefts[0])
    columns = weight.shape[1]
    steps = columns // wide
    spans = [(index * len(left), (index + 1) * len(left)) for index, left in enumerate(lefts)]
    held = [total for total in totals if total is not None]
    out_shape = []
    for split in splits:
        if split:
            out_shape += [
                jax.ShapeDtypeStruct((rows, columns // 2 // groups), jnp.bfloat16),
                jax.ShapeDtypeStruct((rows, columns // 2 // groups), jnp.float32),
            ] * groups
        else:
            out_shape.append(jax.ShapeDtypeStruct((rows, columns), jnp.float32))
    body = functools.partial(
        multiply_body, spans, [total is not None for total in totals], splits, row, groups
    )
    return pl.pallas_call(
        body,
        out_shape=out_shape,
        in_specs=[VMEM] * spans[-1][1] + [HBM] + [VMEM] * len(held) + [ANY] * len(tokens),
        out_specs=[VMEM] * len(out_shape),
        scratch_shapes=[
            pltpu.VMEM((steps, depth, wide), weight.dtype),
            pltpu.SemaphoreType.DMA((steps,)),
        ],
        compiler_params=pltpu.CompilerParams(
            vmem_limit_bytes=2 * steps * depth * wide + VMEM_LIMIT
        ),
        cost_estimate=SMALL,
    )(*[part for left in lefts for part in left], weight, *held, *tokens)


def gate(values, tokens):
    return pl.pallas_call(
        lambda *refs: None,
        out_shape=jax.ShapeDtypeStruct(values.shape, values.dtype),
        in_specs=[ANY] * (1 + len(tokens)),
        out_specs=ANY,
        input_output_aliases={0: 0},
        compiler_params=PARAMS,
        cost_estimate=SMALL,
    )(values, *tokens)


def halve_body(level, kept_ref, came_ref, *refs):
    sent_out, kept_out = refs[-2:]
    half = sent_out.shape[0]

    def put(bit):
        mine, other = slice(bit * half, (bit + 1) * half), slice((1 - bit) * half, (2 - bit) * half)
        kept_out[...] = kept_ref[mine] + came_ref[mine].astype(jnp.float32)
        sent_out[...] = (kept_ref[other] + came_ref[other].astype(jnp.float32)).astype(jnp.bfloat16)

    for bit in range(2):
        pl.when(lax.axis_index("tensor") >> level & 1 == bit)(functools.partial(put, bit))


def halve(kept, came, level, tokens=()):
    rows, columns = kept.shape
    half = rows // 2
    if half % 16:
        total, bit = kept + came.astype(jnp.float32), lax.axis_index("tensor") >> level & 1
        sent = lax.dynamic_slice_in_dim(total, (1 - bit) * half, half, 0).astype(jnp.bfloat16)
        return sent, lax.dynamic_slice_in_dim(total, bit * half, half, 0)
    return pl.pallas_call(
        functools.partial(halve_body, level),
        out_shape=[
            jax.ShapeDtypeStruct((half, columns), jnp.bfloat16),
            jax.ShapeDtypeStruct((half, columns), jnp.float32),
        ],
        in_specs=[VMEM, VMEM] + [ANY] * len(tokens),
        out_specs=[VMEM, VMEM],
        compiler_params=PARAMS,
        cost_estimate=SMALL,
    )(kept, came, *tokens)


def encode_body(begin, kept_ref, came_ref, flips_ref, rotation_ref, *refs):
    out_ref = refs[-1]
    rows, columns = kept_ref.shape
    half = flips_ref.shape[1] // 2
    rotation = rotation_ref[...]
    lane = lax.broadcasted_iota(jnp.int32, (rows, BLOCK), 1)
    scales = jnp.zeros((rows, BLOCK), jnp.float32)
    for block in range(columns // BLOCK):
        at = slice(block * BLOCK, (block + 1) * BLOCK)
        flips = flips_ref[:, pl.ds(pl.multiple_of(lax.axis_index("sub") * half + begin + block * BLOCK, BLOCK), BLOCK)]
        total = (kept_ref[:, at] + came_ref[:, at].astype(jnp.float32)) * flips
        rotated = jnp.dot(
            total, rotation, precision=lax.Precision.HIGHEST, preferred_element_type=jnp.float32
        )
        largest = jnp.max(jnp.abs(rotated), axis=1, keepdims=True)
        scale = (largest + epsilon).astype(jnp.bfloat16).astype(jnp.float32)
        out_ref[:, at] = (rotated / scale).astype(jnp.bfloat16)
        scales = jnp.where(lane == block, scale, scales)
    out_ref[:, columns:] = scales.astype(jnp.bfloat16)


def encode(kept, came, begin, flips, rotation, tokens=()):
    rows, columns = kept.shape
    return pl.pallas_call(
        functools.partial(encode_body, begin),
        out_shape=jax.ShapeDtypeStruct((rows, columns + BLOCK), jnp.bfloat16),
        in_specs=[VMEM] * 4 + [ANY] * len(tokens),
        out_specs=VMEM,
        compiler_params=PARAMS,
        cost_estimate=SMALL,
    )(kept, came, flips, rotation, *tokens)


def rank_of(index, count):
    levels = count.bit_length() - 1
    return sum((index >> level & 1) << (levels - 1 - level) for level in range(levels))


def block_of(other, place, places, blocks):
    sub = lax.axis_index("sub")
    sub = 1 - sub if other else sub
    return lax.rem(lax.axis_index("seq") - (sub * places + place) + blocks, blocks)


def choose_body(blocks, pieces, width, at, other, places, *refs):
    out_ref = refs[-1]
    rows = refs[0].shape[0]
    scales = width // BLOCK

    def put(block, place):
        begin, scale_at = at[block]
        for piece in range(pieces):
            ref = refs[block * pieces + piece]
            row = (place * pieces + rank_of(lax.axis_index("tensor") ^ piece, pieces)) * rows
            here = pl.ds(pl.multiple_of(row, rows), rows)
            out_ref[here, :width] = ref[:, begin : begin + width]
            out_ref[here, width : width + scales] = ref[:, scale_at : scale_at + scales]

    for place in range(places):
        for block in range(blocks):
            pl.when(block_of(other, place, places, blocks) == block)(functools.partial(put, block, place))


def choose(results, group, width, other, places):
    picked, at = [], []
    for result in results:
        if len(result) == 1:
            pieces, begin = result[0], group * width
            at.append((begin, pieces[0].shape[1] - BLOCK + begin // BLOCK))
        else:
            pieces = result[group]
            at.append((0, width))
        picked.append(pieces)
    rows = picked[0][0].shape[0]
    count = len(picked[0])
    if rows % 16:
        blocks = []
        for pieces, (begin, scale_at) in zip(picked, at):
            block = jnp.zeros((count * rows, width + BLOCK), jnp.bfloat16)
            for index, piece in enumerate(pieces):
                scale = jnp.pad(piece[:, scale_at : scale_at + width // BLOCK], ((0, 0), (0, BLOCK - width // BLOCK)))
                part = jnp.concatenate([piece[:, begin : begin + width], scale], axis=1)
                block = lax.dynamic_update_slice_in_dim(block, part, rank_of(lax.axis_index("tensor") ^ index, count) * rows, 0)
            blocks.append(block)
        stacked = jnp.stack(blocks)
        return jnp.concatenate([stacked[block_of(other, place, places, len(blocks))] for place in range(places)])
    return pl.pallas_call(
        functools.partial(choose_body, len(picked), count, width, at, other, places),
        out_shape=jax.ShapeDtypeStruct((places * count * rows, width + BLOCK), jnp.bfloat16),
        in_specs=[VMEM] * (len(picked) * count),
        out_specs=VMEM,
        compiler_params=PARAMS,
        cost_estimate=SMALL,
    )(*[piece for pieces in picked for piece in pieces])


def assemble_body(groups, half, *refs):
    mine, other = refs[:groups], refs[groups : 2 * groups]
    codes_ref, scales_ref = refs[2 * groups :]
    width = half // groups
    scales = width // BLOCK

    def put(core):
        held = []
        for side, side_refs in ((core, mine), (1 - core, other)):
            for group, ref in enumerate(side_refs):
                begin = side * half + group * width
                codes_ref[:, begin : begin + width] = ref[:, :width]
                held.append((begin, ref[:, width : width + scales].astype(jnp.float32)))
        held = jnp.concatenate([value for _, value in sorted(held, key=lambda pair: pair[0])], axis=1)
        scales_ref[...] = held.T.astype(jnp.bfloat16)

    for core in range(2):
        pl.when(lax.axis_index("sub") == core)(functools.partial(put, core))


def assemble(mine, other, half):
    rows = mine[0].shape[0]
    codes, scales = pl.pallas_call(
        functools.partial(assemble_body, len(mine), half),
        out_shape=(
            jax.ShapeDtypeStruct((rows, 2 * half), jnp.bfloat16),
            jax.ShapeDtypeStruct((2 * half // BLOCK, rows), jnp.bfloat16),
        ),
        in_specs=[VMEM] * (2 * len(mine)),
        out_specs=(VMEM, VMEM),
        compiler_params=PARAMS,
        cost_estimate=SMALL,
    )(*mine, *other)
    return codes, scales.T


def cut(depth):
    if depth % UNIT or depth < 8 * UNIT:
        return [depth]
    units = depth // UNIT
    sizes = [max(1, units * share // 13) for share in SHARES]
    return [size * UNIT for size in sizes + [units - sum(sizes)]]


def shards(hidden, down_weight, sign_bits):
    tensor_count = lax.axis_size("tensor")
    seq_count = lax.axis_size("seq")
    sub_count = lax.axis_size("sub")
    depth = hidden.shape[1]
    half = down_weight.shape[1] // sub_count
    per_sub = seq_count // sub_count
    levels = tensor_count.bit_length() - 1
    wide, wide_chunk = min(256, half // GROUPS), min(512, half // GROUPS)
    flips = (2 * sign_bits - 1).astype(jnp.float32)[None, :]
    rotation = jnp.asarray(hadamard(BLOCK))

    def swap(values):
        return lax.ppermute(values, "sub", [(0, 1), (1, 0)])

    def exchange(values, level):
        return lax.ppermute(values, "tensor", [(t, t ^ 1 << level) for t in range(tensor_count)])

    def reduce(sent, kept, begin):
        tokens = (yield None) or []
        came = swap(sent)
        for level in range(levels):
            sent, kept = halve(kept, came, level, tokens)
            tokens = (yield sent) or []
            came = exchange(sent, level)
        yield encode(kept, came, begin, flips, rotation, tokens)

    def spread(packed):
        pieces = {0: packed}
        for level in reversed(range(levels)):
            for index in list(pieces):
                pieces[index ^ 1 << level] = exchange(pieces[index], level)
        return [pieces[index] for index in range(tensor_count)]

    sizes = cut(depth)
    places = [sum(sizes[:index]) for index in range(len(sizes))]
    parts = slices_of(hidden, list(zip(places, sizes)))
    arrivals = []
    for shift in range(1, seq_count):
        pairs = [(s, (s + shift) % seq_count) for s in range(seq_count)]
        arrivals.append([lax.ppermute(part, "seq", pairs) for part in parts])

    if len(sizes) == 1:
        outs = multiply([[parts[0]], [arrivals[0][0]]], down_weight, 0, [None, None], [True, True], wide_chunk)
        reduced = [list(reduce(*outs[:2], 0))[-1], list(reduce(*outs[2:], 0))[-1]]
        for arrived in arrivals[1:]:
            outs = multiply([[arrived[0]]], down_weight, 0, [None], [True], wide_chunk)
            reduced.append(list(reduce(*outs, 0))[-1])
        results = [[spread(packed)] for packed in reduced]
    else:
        (own,) = multiply([parts[1:]], down_weight, sizes[0], [None], [False], wide, tokens=parts[:1])
        sent, kept, total = multiply(
            [[parts[0]], [arrivals[0][0]]], down_weight, 0, [own, None], [True, False], wide_chunk
        )
        own_steps = reduce(sent, kept, 0)
        next(own_steps)
        tokens = [own_steps.send([arrivals[0][1]])]
        results = []
        for shift, arrived in enumerate(arrivals):
            if shift:
                (total,) = multiply([[arrived[0]]], down_weight, 0, [None], [False], wide_chunk)
            for index in range(1, len(sizes) - 1):
                (total,) = multiply(
                    [[arrived[index]]], down_weight, places[index], [total], [False], wide_chunk, tokens=tokens
                )
                if not results:
                    step = own_steps.send([total])
                    tokens = [step]
                    if step.shape[1] > half:
                        results.append([spread(step)])
            if not results:
                results.append([spread(list(own_steps)[-1])])
            outs = multiply(
                [[arrived[-1]]], down_weight, places[-1], [total], [True], wide_chunk, groups=GROUPS, tokens=tokens
            )
            remote = []
            for group in range(GROUPS):
                sent, kept = outs[2 * group : 2 * group + 2]
                if group == GROUPS - 1 and shift == 0 and levels > 1:
                    sent = gate(sent, [results[0][0][1], results[0][0][1 << levels - 1]])
                steps = reduce(sent, kept, group * half // GROUPS)
                next(steps)
                wait = []
                for level in range(levels + 1):
                    packed = steps.send(wait)
                    wait = results[0][0][1:] if group == 0 and shift == 0 and level == 0 else []
                remote.append(spread(packed))
            results.append(remote)
            tokens = []

    groups = max(len(result) for result in results)
    width = half // groups
    other = [swap(choose(results, group, width, True, per_sub)) for group in range(groups)]
    mine = [choose(results, group, width, False, per_sub) for group in range(groups)]
    return assemble(mine, other, half)


def solution(mesh):
    return jax.shard_map(
        shards,
        mesh=mesh,
        in_specs=(P(("groups", "seq"), ("tensor", "sub")), P(("tensor", "sub"), "seq"), P("seq")),
        out_specs=(P(("groups", "sub"), "seq"), P(("groups", "sub"), "seq")),
        check_vma=False,
    )
```

```python
import functools
import math

import jax
import jax.numpy as jnp
import numpy as np
from jax import lax
from jax.experimental import pallas as pl
from jax.experimental.pallas import tpu as pltpu
from jax.sharding import PartitionSpec as P

BLOCK = 128
UNIT = 512
GROUPS = 2
VMEM_LIMIT = 6 * 2**20
SHARES = (4, 3, 3)
epsilon = 1e-06

SMALL = pl.CostEstimate(flops=1, bytes_accessed=1, transcendentals=0)
PARAMS = pltpu.CompilerParams(vmem_limit_bytes=VMEM_LIMIT)
VMEM = pl.BlockSpec(memory_space=pltpu.VMEM)
ANY = pl.BlockSpec(memory_space=pl.ANY)
HBM = pl.BlockSpec(memory_space=pltpu.HBM)


def hadamard(order):
    indices = np.arange(order)
    parity = np.zeros((order, order), np.int64)
    for position in range(order.bit_length() - 1):
        parity = parity + (indices[:, None] >> position & 1) * (indices[None, :] >> position & 1)
    return ((1 - 2 * (parity % 2)) / math.sqrt(order)).astype(np.float32)


def slice_body(places, in_ref, *refs):
    out_refs, arrived = refs[:-1], refs[-1]
    copies = [
        pltpu.make_async_copy(in_ref.at[:, at : at + size], out_ref, arrived.at[index])
        for index, ((at, size), out_ref) in enumerate(zip(places, out_refs))
    ]
    for copy in copies:
        copy.start()
    for copy in copies:
        copy.wait()


def slices_of(values, places):
    return pl.pallas_call(
        functools.partial(slice_body, places),
        out_shape=[jax.ShapeDtypeStruct((values.shape[0], size), values.dtype) for _, size in places],
        in_specs=[HBM],
        out_specs=[VMEM] * len(places),
        scratch_shapes=[pltpu.SemaphoreType.DMA((len(places),))],
        compiler_params=PARAMS,
        cost_estimate=SMALL,
    )(values)


def multiply_body(spans, has_totals, splits, row, groups, *refs):
    lefts = [refs[begin:end] for begin, end in spans]
    refs = refs[spans[-1][1] :]
    w_ref, refs = refs[0], refs[1:]
    total_refs, refs = list(refs[: sum(has_totals)]), refs[sum(has_totals) :]
    buffer, arrived = refs[-2:]
    out_count = sum(2 * groups if split else 1 for split in splits)
    out_refs = refs[-2 - out_count : -2]
    steps, depth, wide = buffer.shape
    rows = lefts[0][0].shape[0]
    first = steps // 2 // groups
    here = lax.axis_index("sub")

    def column(n):
        if not any(splits):
            return n
        group, place = n // (2 * first), n % (2 * first)
        side, place = (here, place - first) if place >= first else (1 - here, place)
        return side * (steps // 2) + group * first + place

    def at(block):
        return pl.ds(pl.multiple_of(block * wide, wide), wide)

    def copy(n):
        return pltpu.make_async_copy(w_ref.at[pl.ds(row, depth), at(column(n))], buffer.at[n], arrived.at[n])

    def step(n):
        copy(n).wait()
        product, begin = None, 0
        for index in range(len(lefts[0])):
            parts = [left[index][...] for left in lefts]
            left = parts[0] if len(parts) == 1 else jnp.concatenate(parts, axis=0)
            end = begin + left.shape[1]
            part = jnp.dot(left, buffer[n, begin:end], preferred_element_type=jnp.float32)
            product = part if product is None else product + part
            begin = end
        totals, outs = list(total_refs), list(out_refs)
        for index in range(len(lefts)):
            value = product[index * rows : (index + 1) * rows]
            if has_totals[index]:
                value = value + totals.pop(0)[:, at(column(n))]
            if splits[index]:
                group, place = n // (2 * first), n % (2 * first)
                out_ref = outs[2 * group + place // first]
                begin = place % first * wide
                out_ref[:, begin : begin + wide] = value.astype(out_ref.dtype)
                outs = outs[2 * groups :]
            else:
                outs.pop(0)[:, at(column(n))] = value

    for n in range(steps):
        copy(n).start()
    if any(splits):
        for n in range(steps):
            step(n)
    else:
        pl.loop(0, steps)(step)


def multiply(lefts, weight, row, totals, splits, wide, groups=1, tokens=()):
    rows = lefts[0][0].shape[0]
    depth = sum(part.shape[1] for part in lefts[0])
    columns = weight.shape[1]
    steps = columns // wide
    spans = [(index * len(left), (index + 1) * len(left)) for index, left in enumerate(lefts)]
    held = [total for total in totals if total is not None]
    out_shape = []
    for split in splits:
        if split:
            out_shape += [
                jax.ShapeDtypeStruct((rows, columns // 2 // groups), jnp.bfloat16),
                jax.ShapeDtypeStruct((rows, columns // 2 // groups), jnp.float32),
            ] * groups
        else:
            out_shape.append(jax.ShapeDtypeStruct((rows, columns), jnp.float32))
    body = functools.partial(
        multiply_body, spans, [total is not None for total in totals], splits, row, groups
    )
    return pl.pallas_call(
        body,
        out_shape=out_shape,
        in_specs=[VMEM] * spans[-1][1] + [HBM] + [VMEM] * len(held) + [ANY] * len(tokens),
        out_specs=[VMEM] * len(out_shape),
        scratch_shapes=[
            pltpu.VMEM((steps, depth, wide), weight.dtype),
            pltpu.SemaphoreType.DMA((steps,)),
        ],
        compiler_params=pltpu.CompilerParams(
            vmem_limit_bytes=2 * steps * depth * wide + VMEM_LIMIT
        ),
        cost_estimate=SMALL,
    )(*[part for left in lefts for part in left], weight, *held, *tokens)


def gate(values, tokens):
    return pl.pallas_call(
        lambda *refs: None,
        out_shape=jax.ShapeDtypeStruct(values.shape, values.dtype),
        in_specs=[ANY] * (1 + len(tokens)),
        out_specs=ANY,
        input_output_aliases={0: 0},
        compiler_params=PARAMS,
        cost_estimate=SMALL,
    )(values, *tokens)


def halve_body(level, count, *refs):
    kept_refs, came_refs, (sent_out, kept_out) = refs[:count], refs[count : 2 * count], refs[-2:]
    half, columns = sent_out.shape
    width = columns // count

    def put(bit):
        mine, other = slice(bit * half, (bit + 1) * half), slice((1 - bit) * half, (2 - bit) * half)
        for index, (kept_ref, came_ref) in enumerate(zip(kept_refs, came_refs)):
            at = slice(index * width, (index + 1) * width)
            kept_out[:, at] = kept_ref[mine] + came_ref[mine].astype(jnp.float32)
            sent_out[:, at] = (kept_ref[other] + came_ref[other].astype(jnp.float32)).astype(jnp.bfloat16)

    for bit in range(2):
        pl.when(lax.axis_index("tensor") >> level & 1 == bit)(functools.partial(put, bit))


def halve(kept, came, level, tokens=()):
    rows, columns = kept[0].shape
    half, columns = rows // 2, columns * len(kept)
    if half % 16:
        total = jnp.concatenate(kept, axis=1) + jnp.concatenate(came, axis=1).astype(jnp.float32)
        bit = lax.axis_index("tensor") >> level & 1
        sent = lax.dynamic_slice_in_dim(total, (1 - bit) * half, half, 0).astype(jnp.bfloat16)
        return sent, lax.dynamic_slice_in_dim(total, bit * half, half, 0)
    return pl.pallas_call(
        functools.partial(halve_body, level, len(kept)),
        out_shape=[
            jax.ShapeDtypeStruct((half, columns), jnp.bfloat16),
            jax.ShapeDtypeStruct((half, columns), jnp.float32),
        ],
        in_specs=[VMEM] * (2 * len(kept)) + [ANY] * len(tokens),
        out_specs=[VMEM, VMEM],
        compiler_params=PARAMS,
        cost_estimate=SMALL,
    )(*kept, *came, *tokens)


def encode_body(begin, kept_ref, came_ref, flips_ref, rotation_ref, *refs):
    out_ref = refs[-1]
    rows, columns = kept_ref.shape
    half = flips_ref.shape[1] // 2
    rotation = rotation_ref[...]
    lane = lax.broadcasted_iota(jnp.int32, (rows, BLOCK), 1)
    scales = jnp.zeros((rows, BLOCK), jnp.float32)
    for block in range(columns // BLOCK):
        at = slice(block * BLOCK, (block + 1) * BLOCK)
        flips = flips_ref[:, pl.ds(pl.multiple_of(lax.axis_index("sub") * half + begin + block * BLOCK, BLOCK), BLOCK)]
        total = (kept_ref[:, at] + came_ref[:, at].astype(jnp.float32)) * flips
        rotated = jnp.dot(
            total, rotation, precision=lax.Precision.HIGHEST, preferred_element_type=jnp.float32
        )
        largest = jnp.max(jnp.abs(rotated), axis=1, keepdims=True)
        scale = (largest + epsilon).astype(jnp.bfloat16).astype(jnp.float32)
        out_ref[:, at] = (rotated / scale).astype(jnp.bfloat16)
        scales = jnp.where(lane == block, scale, scales)
    out_ref[:, columns:] = scales.astype(jnp.bfloat16)


def encode(kept, came, begin, flips, rotation, tokens=()):
    rows, columns = kept.shape
    return pl.pallas_call(
        functools.partial(encode_body, begin),
        out_shape=jax.ShapeDtypeStruct((rows, columns + BLOCK), jnp.bfloat16),
        in_specs=[VMEM] * 4 + [ANY] * len(tokens),
        out_specs=VMEM,
        compiler_params=PARAMS,
        cost_estimate=SMALL,
    )(kept, came, flips, rotation, *tokens)


def rank_of(index, count):
    levels = count.bit_length() - 1
    return sum((index >> level & 1) << (levels - 1 - level) for level in range(levels))


def block_of(other, place, places, blocks):
    sub = lax.axis_index("sub")
    sub = 1 - sub if other else sub
    return lax.rem(lax.axis_index("seq") - (sub * places + place) + blocks, blocks)


def choose_body(blocks, pieces, width, at, other, places, *refs):
    out_ref = refs[-1]
    rows = refs[0].shape[0]
    scales = width // BLOCK

    def put(block, place):
        begin, scale_at = at[block]
        for piece in range(pieces):
            ref = refs[block * pieces + piece]
            row = (place * pieces + rank_of(lax.axis_index("tensor") ^ piece, pieces)) * rows
            here = pl.ds(pl.multiple_of(row, rows), rows)
            out_ref[here, :width] = ref[:, begin : begin + width]
            out_ref[here, width : width + scales] = ref[:, scale_at : scale_at + scales]

    for place in range(places):
        for block in range(blocks):
            pl.when(block_of(other, place, places, blocks) == block)(functools.partial(put, block, place))


def choose(results, group, width, other, places):
    picked, at = [], []
    for result in results:
        if len(result) == 1:
            pieces, begin = result[0], group * width
            at.append((begin, pieces[0].shape[1] - BLOCK + begin // BLOCK))
        else:
            pieces = result[group]
            at.append((0, width))
        picked.append(pieces)
    rows = picked[0][0].shape[0]
    count = len(picked[0])
    if rows % 16:
        blocks = []
        for pieces, (begin, scale_at) in zip(picked, at):
            block = jnp.zeros((count * rows, width + BLOCK), jnp.bfloat16)
            for index, piece in enumerate(pieces):
                scale = jnp.pad(piece[:, scale_at : scale_at + width // BLOCK], ((0, 0), (0, BLOCK - width // BLOCK)))
                part = jnp.concatenate([piece[:, begin : begin + width], scale], axis=1)
                block = lax.dynamic_update_slice_in_dim(block, part, rank_of(lax.axis_index("tensor") ^ index, count) * rows, 0)
            blocks.append(block)
        stacked = jnp.stack(blocks)
        return jnp.concatenate([stacked[block_of(other, place, places, len(blocks))] for place in range(places)])
    return pl.pallas_call(
        functools.partial(choose_body, len(picked), count, width, at, other, places),
        out_shape=jax.ShapeDtypeStruct((places * count * rows, width + BLOCK), jnp.bfloat16),
        in_specs=[VMEM] * (len(picked) * count),
        out_specs=VMEM,
        compiler_params=PARAMS,
        cost_estimate=SMALL,
    )(*[piece for pieces in picked for piece in pieces])


def assemble_body(groups, half, *refs):
    mine, other = refs[:groups], refs[groups : 2 * groups]
    codes_ref, scales_ref = refs[2 * groups :]
    width = half // groups
    scales = width // BLOCK

    def put(core):
        held = []
        for side, side_refs in ((core, mine), (1 - core, other)):
            for group, ref in enumerate(side_refs):
                begin = side * half + group * width
                codes_ref[:, begin : begin + width] = ref[:, :width]
                held.append((begin, ref[:, width : width + scales].astype(jnp.float32)))
        held = jnp.concatenate([value for _, value in sorted(held, key=lambda pair: pair[0])], axis=1)
        scales_ref[...] = held.T.astype(jnp.bfloat16)

    for core in range(2):
        pl.when(lax.axis_index("sub") == core)(functools.partial(put, core))


def assemble(mine, other, half):
    rows = mine[0].shape[0]
    codes, scales = pl.pallas_call(
        functools.partial(assemble_body, len(mine), half),
        out_shape=(
            jax.ShapeDtypeStruct((rows, 2 * half), jnp.bfloat16),
            jax.ShapeDtypeStruct((2 * half // BLOCK, rows), jnp.bfloat16),
        ),
        in_specs=[VMEM] * (2 * len(mine)),
        out_specs=(VMEM, VMEM),
        compiler_params=PARAMS,
        cost_estimate=SMALL,
    )(*mine, *other)
    return codes, scales.T


def cut(depth):
    if depth % UNIT or depth < 8 * UNIT:
        return [depth]
    units = depth // UNIT
    sizes = [max(1, units * share // 13) for share in SHARES]
    return [size * UNIT for size in sizes + [units - sum(sizes)]]


def shards(hidden, down_weight, sign_bits):
    tensor_count = lax.axis_size("tensor")
    seq_count = lax.axis_size("seq")
    sub_count = lax.axis_size("sub")
    depth = hidden.shape[1]
    half = down_weight.shape[1] // sub_count
    per_sub = seq_count // sub_count
    levels = tensor_count.bit_length() - 1
    wide, wide_chunk = min(256, half // GROUPS), min(512, half // GROUPS)
    flips = (2 * sign_bits - 1).astype(jnp.float32)[None, :]
    rotation = jnp.asarray(hadamard(BLOCK))

    def swap(values):
        return lax.ppermute(values, "sub", [(0, 1), (1, 0)])

    def exchange(values, level):
        return lax.ppermute(values, "tensor", [(t, t ^ 1 << level) for t in range(tensor_count)])

    def reduce(halves, begin):
        tokens = (yield None) or []
        kept, came = halves[1::2], [swap(sent) for sent in halves[::2]]
        for level in range(levels):
            sent, held = halve(kept, came, level, tokens)
            tokens = (yield sent) or []
            kept, came = [held], [exchange(sent, level)]
        yield encode(kept[0], came[0], begin, flips, rotation, tokens)

    def spread(packed):
        pieces = {0: packed}
        for level in reversed(range(levels)):
            for index in list(pieces):
                pieces[index ^ 1 << level] = exchange(pieces[index], level)
        return [pieces[index] for index in range(tensor_count)]

    sizes = cut(depth)
    places = [sum(sizes[:index]) for index in range(len(sizes))]
    parts = slices_of(hidden, list(zip(places, sizes)))
    arrivals = []
    for shift in range(1, seq_count):
        pairs = [(s, (s + shift) % seq_count) for s in range(seq_count)]
        arrivals.append([lax.ppermute(part, "seq", pairs) for part in parts])

    if len(sizes) == 1:
        outs = multiply([[parts[0]], [arrivals[0][0]]], down_weight, 0, [None, None], [True, True], wide_chunk)
        reduced = [list(reduce(outs[:2], 0))[-1], list(reduce(outs[2:], 0))[-1]]
        for arrived in arrivals[1:]:
            outs = multiply([[arrived[0]]], down_weight, 0, [None], [True], wide_chunk)
            reduced.append(list(reduce(outs, 0))[-1])
        results = [[spread(packed)] for packed in reduced]
    else:
        (own,) = multiply([parts[1:]], down_weight, sizes[0], [None], [False], wide, tokens=parts[:1])
        *halves, total = multiply(
            [[parts[0]], [arrivals[0][0]]], down_weight, 0, [own, None], [True, False], wide_chunk, groups=GROUPS
        )
        own_steps = reduce(halves, 0)
        next(own_steps)
        tokens = [own_steps.send([arrivals[0][1]])]
        results = []
        for shift, arrived in enumerate(arrivals):
            if shift:
                (total,) = multiply([[arrived[0]]], down_weight, 0, [None], [False], wide_chunk)
            for index in range(1, len(sizes) - 1):
                (total,) = multiply(
                    [[arrived[index]]], down_weight, places[index], [total], [False], wide_chunk, tokens=tokens
                )
                if not results:
                    step = own_steps.send([total])
                    tokens = [step]
                    if step.shape[1] > half:
                        results.append([spread(step)])
            if not results:
                results.append([spread(list(own_steps)[-1])])
            outs = multiply(
                [[arrived[-1]]], down_weight, places[-1], [total], [True], wide_chunk, groups=GROUPS, tokens=tokens
            )
            remote, all_steps = [], []
            for group in range(GROUPS):
                sent, kept = outs[2 * group : 2 * group + 2]
                if group == GROUPS - 1 and shift == 0 and levels > 1:
                    sent = gate(sent, [results[0][0][1], results[0][0][1 << levels - 1]])
                all_steps.append(reduce([sent, kept], group * half // GROUPS))
                next(all_steps[-1])
            last = []
            for level in range(levels + 1):
                for group, steps in enumerate(all_steps):
                    wait = list(last) if group == 0 else []
                    if group == 0 and level == 1 and shift == 0:
                        wait += results[0][0][1:]
                    if remote:
                        wait.append(remote[-1][1])
                    step = steps.send(wait)
                    if level == levels:
                        remote.append(spread(step))
                last = [step]
            results.append(remote)
            tokens = []

    groups = max(len(result) for result in results)
    width = half // groups
    other = [swap(choose(results, group, width, True, per_sub)) for group in range(groups)]
    mine = [choose(results, group, width, False, per_sub) for group in range(groups)]
    return assemble(mine, other, half)


def solution(mesh):
    return jax.shard_map(
        shards,
        mesh=mesh,
        in_specs=(P(("groups", "seq"), ("tensor", "sub")), P(("tensor", "sub"), "seq"), P("seq")),
        out_specs=(P(("groups", "sub"), "seq"), P(("groups", "sub"), "seq")),
        check_vma=False,
    )
```

```python
import functools
import math

import jax
import jax.numpy as jnp
import numpy as np
from jax import lax
from jax.experimental import pallas as pl
from jax.experimental.pallas import tpu as pltpu
from jax.sharding import PartitionSpec as P

BLOCK = 128
UNIT = 512
GROUPS = 2
VMEM_LIMIT = 6 * 2**20
SHARES = (4, 4, 3)
epsilon = 1e-06

SMALL = pl.CostEstimate(flops=1, bytes_accessed=1, transcendentals=0)
PARAMS = pltpu.CompilerParams(vmem_limit_bytes=VMEM_LIMIT)
VMEM = pl.BlockSpec(memory_space=pltpu.VMEM)
ANY = pl.BlockSpec(memory_space=pl.ANY)
HBM = pl.BlockSpec(memory_space=pltpu.HBM)


def hadamard(order):
    indices = np.arange(order)
    parity = np.zeros((order, order), np.int64)
    for position in range(order.bit_length() - 1):
        parity = parity + (indices[:, None] >> position & 1) * (indices[None, :] >> position & 1)
    return ((1 - 2 * (parity % 2)) / math.sqrt(order)).astype(np.float32)


def slice_body(places, in_ref, *refs):
    out_refs, arrived = refs[:-1], refs[-1]
    copies = [
        pltpu.make_async_copy(in_ref.at[:, at : at + size], out_ref, arrived.at[index])
        for index, ((at, size), out_ref) in enumerate(zip(places, out_refs))
    ]
    for copy in copies:
        copy.start()
    for copy in copies:
        copy.wait()


def slices_of(values, places):
    return pl.pallas_call(
        functools.partial(slice_body, places),
        out_shape=[jax.ShapeDtypeStruct((values.shape[0], size), values.dtype) for _, size in places],
        in_specs=[HBM],
        out_specs=[VMEM] * len(places),
        scratch_shapes=[pltpu.SemaphoreType.DMA((len(places),))],
        compiler_params=PARAMS,
        cost_estimate=SMALL,
    )(values)


def multiply_body(spans, has_totals, splits, row, groups, *refs):
    lefts = [refs[begin:end] for begin, end in spans]
    refs = refs[spans[-1][1] :]
    w_ref, refs = refs[0], refs[1:]
    total_refs, refs = list(refs[: sum(has_totals)]), refs[sum(has_totals) :]
    buffer, arrived = refs[-2:]
    out_count = sum(2 * groups if split else 1 for split in splits)
    out_refs = refs[-2 - out_count : -2]
    steps, depth, wide = buffer.shape
    rows = lefts[0][0].shape[0]
    first = steps // 2 // groups
    here = lax.axis_index("sub")

    def column(n):
        if not any(splits):
            return n
        group, place = n // (2 * first), n % (2 * first)
        side, place = (here, place - first) if place >= first else (1 - here, place)
        return side * (steps // 2) + group * first + place

    def at(block):
        return pl.ds(pl.multiple_of(block * wide, wide), wide)

    def copy(n):
        return pltpu.make_async_copy(w_ref.at[pl.ds(row, depth), at(column(n))], buffer.at[n], arrived.at[n])

    def step(n):
        copy(n).wait()
        product, begin = None, 0
        for index in range(len(lefts[0])):
            parts = [left[index][...] for left in lefts]
            left = parts[0] if len(parts) == 1 else jnp.concatenate(parts, axis=0)
            end = begin + left.shape[1]
            part = jnp.dot(left, buffer[n, begin:end], preferred_element_type=jnp.float32)
            product = part if product is None else product + part
            begin = end
        totals, outs = list(total_refs), list(out_refs)
        for index in range(len(lefts)):
            value = product[index * rows : (index + 1) * rows]
            if has_totals[index]:
                value = value + totals.pop(0)[:, at(column(n))]
            if splits[index]:
                group, place = n // (2 * first), n % (2 * first)
                out_ref = outs[2 * group + place // first]
                begin = place % first * wide
                out_ref[:, begin : begin + wide] = value.astype(out_ref.dtype)
                outs = outs[2 * groups :]
            else:
                outs.pop(0)[:, at(column(n))] = value

    for n in range(steps):
        copy(n).start()
    if any(splits):
        for n in range(steps):
            step(n)
    else:
        pl.loop(0, steps)(step)


def multiply(lefts, weight, row, totals, splits, wide, groups=1, tokens=()):
    rows = lefts[0][0].shape[0]
    depth = sum(part.shape[1] for part in lefts[0])
    columns = weight.shape[1]
    steps = columns // wide
    spans = [(index * len(left), (index + 1) * len(left)) for index, left in enumerate(lefts)]
    held = [total for total in totals if total is not None]
    out_shape = []
    for split in splits:
        if split:
            out_shape += [
                jax.ShapeDtypeStruct((rows, columns // 2 // groups), jnp.bfloat16),
                jax.ShapeDtypeStruct((rows, columns // 2 // groups), jnp.float32),
            ] * groups
        else:
            out_shape.append(jax.ShapeDtypeStruct((rows, columns), jnp.float32))
    body = functools.partial(
        multiply_body, spans, [total is not None for total in totals], splits, row, groups
    )
    return pl.pallas_call(
        body,
        out_shape=out_shape,
        in_specs=[VMEM] * spans[-1][1] + [HBM] + [VMEM] * len(held) + [ANY] * len(tokens),
        out_specs=[VMEM] * len(out_shape),
        scratch_shapes=[
            pltpu.VMEM((steps, depth, wide), weight.dtype),
            pltpu.SemaphoreType.DMA((steps,)),
        ],
        compiler_params=pltpu.CompilerParams(
            vmem_limit_bytes=2 * steps * depth * wide + VMEM_LIMIT
        ),
        cost_estimate=SMALL,
    )(*[part for left in lefts for part in left], weight, *held, *tokens)


def gate(values, tokens):
    return pl.pallas_call(
        lambda *refs: None,
        out_shape=jax.ShapeDtypeStruct(values.shape, values.dtype),
        in_specs=[ANY] * (1 + len(tokens)),
        out_specs=ANY,
        input_output_aliases={0: 0},
        compiler_params=PARAMS,
        cost_estimate=SMALL,
    )(values, *tokens)


def halve_body(level, count, *refs):
    kept_refs, came_refs, (sent_out, kept_out) = refs[:count], refs[count : 2 * count], refs[-2:]
    half, columns = sent_out.shape
    width = columns // count

    def put(bit):
        mine, other = slice(bit * half, (bit + 1) * half), slice((1 - bit) * half, (2 - bit) * half)
        for index, (kept_ref, came_ref) in enumerate(zip(kept_refs, came_refs)):
            at = slice(index * width, (index + 1) * width)
            kept_out[:, at] = kept_ref[mine] + came_ref[mine].astype(jnp.float32)
            sent_out[:, at] = (kept_ref[other] + came_ref[other].astype(jnp.float32)).astype(jnp.bfloat16)

    for bit in range(2):
        pl.when(lax.axis_index("tensor") >> level & 1 == bit)(functools.partial(put, bit))


def halve(kept, came, level, tokens=()):
    rows, columns = kept[0].shape
    half, columns = rows // 2, columns * len(kept)
    if half % 16:
        total = jnp.concatenate(kept, axis=1) + jnp.concatenate(came, axis=1).astype(jnp.float32)
        bit = lax.axis_index("tensor") >> level & 1
        sent = lax.dynamic_slice_in_dim(total, (1 - bit) * half, half, 0).astype(jnp.bfloat16)
        return sent, lax.dynamic_slice_in_dim(total, bit * half, half, 0)
    return pl.pallas_call(
        functools.partial(halve_body, level, len(kept)),
        out_shape=[
            jax.ShapeDtypeStruct((half, columns), jnp.bfloat16),
            jax.ShapeDtypeStruct((half, columns), jnp.float32),
        ],
        in_specs=[VMEM] * (2 * len(kept)) + [ANY] * len(tokens),
        out_specs=[VMEM, VMEM],
        compiler_params=PARAMS,
        cost_estimate=SMALL,
    )(*kept, *came, *tokens)


def encode_body(begin, kept_ref, came_ref, flips_ref, rotation_ref, *refs):
    out_ref = refs[-1]
    rows, columns = kept_ref.shape
    half = flips_ref.shape[1] // 2
    rotation = rotation_ref[...]
    lane = lax.broadcasted_iota(jnp.int32, (rows, BLOCK), 1)
    scales = jnp.zeros((rows, BLOCK), jnp.float32)
    for block in range(columns // BLOCK):
        at = slice(block * BLOCK, (block + 1) * BLOCK)
        flips = flips_ref[:, pl.ds(pl.multiple_of(lax.axis_index("sub") * half + begin + block * BLOCK, BLOCK), BLOCK)]
        total = (kept_ref[:, at] + came_ref[:, at].astype(jnp.float32)) * flips
        rotated = jnp.dot(
            total, rotation, precision=lax.Precision.HIGHEST, preferred_element_type=jnp.float32
        )
        largest = jnp.max(jnp.abs(rotated), axis=1, keepdims=True)
        scale = (largest + epsilon).astype(jnp.bfloat16).astype(jnp.float32)
        out_ref[:, at] = (rotated / scale).astype(jnp.bfloat16)
        scales = jnp.where(lane == block, scale, scales)
    out_ref[:, columns:] = scales.astype(jnp.bfloat16)


def encode(kept, came, begin, flips, rotation, tokens=()):
    rows, columns = kept.shape
    return pl.pallas_call(
        functools.partial(encode_body, begin),
        out_shape=jax.ShapeDtypeStruct((rows, columns + BLOCK), jnp.bfloat16),
        in_specs=[VMEM] * 4 + [ANY] * len(tokens),
        out_specs=VMEM,
        compiler_params=PARAMS,
        cost_estimate=SMALL,
    )(kept, came, flips, rotation, *tokens)


def rank_of(index, count):
    levels = count.bit_length() - 1
    return sum((index >> level & 1) << (levels - 1 - level) for level in range(levels))


def block_of(other, place, places, blocks):
    sub = lax.axis_index("sub")
    sub = 1 - sub if other else sub
    return lax.rem(lax.axis_index("seq") - (sub * places + place) + blocks, blocks)


def choose_body(blocks, pieces, width, at, other, places, *refs):
    out_ref = refs[-1]
    rows = refs[0].shape[0]
    scales = width // BLOCK

    def put(block, place):
        begin, scale_at = at[block]
        for piece in range(pieces):
            ref = refs[block * pieces + piece]
            row = (place * pieces + rank_of(lax.axis_index("tensor") ^ piece, pieces)) * rows
            here = pl.ds(pl.multiple_of(row, rows), rows)
            out_ref[here, :width] = ref[:, begin : begin + width]
            out_ref[here, width : width + scales] = ref[:, scale_at : scale_at + scales]

    for place in range(places):
        for block in range(blocks):
            pl.when(block_of(other, place, places, blocks) == block)(functools.partial(put, block, place))


def choose(results, group, width, other, places):
    picked, at = [], []
    for result in results:
        if len(result) == 1:
            pieces, begin = result[0], group * width
            at.append((begin, pieces[0].shape[1] - BLOCK + begin // BLOCK))
        else:
            pieces = result[group]
            at.append((0, width))
        picked.append(pieces)
    rows = picked[0][0].shape[0]
    count = len(picked[0])
    if rows % 16:
        blocks = []
        for pieces, (begin, scale_at) in zip(picked, at):
            block = jnp.zeros((count * rows, width + BLOCK), jnp.bfloat16)
            for index, piece in enumerate(pieces):
                scale = jnp.pad(piece[:, scale_at : scale_at + width // BLOCK], ((0, 0), (0, BLOCK - width // BLOCK)))
                part = jnp.concatenate([piece[:, begin : begin + width], scale], axis=1)
                block = lax.dynamic_update_slice_in_dim(block, part, rank_of(lax.axis_index("tensor") ^ index, count) * rows, 0)
            blocks.append(block)
        stacked = jnp.stack(blocks)
        return jnp.concatenate([stacked[block_of(other, place, places, len(blocks))] for place in range(places)])
    return pl.pallas_call(
        functools.partial(choose_body, len(picked), count, width, at, other, places),
        out_shape=jax.ShapeDtypeStruct((places * count * rows, width + BLOCK), jnp.bfloat16),
        in_specs=[VMEM] * (len(picked) * count),
        out_specs=VMEM,
        compiler_params=PARAMS,
        cost_estimate=SMALL,
    )(*[piece for pieces in picked for piece in pieces])


def assemble_body(groups, half, *refs):
    mine, other = refs[:groups], refs[groups : 2 * groups]
    codes_ref, scales_ref = refs[2 * groups :]
    width = half // groups
    scales = width // BLOCK

    def put(core):
        held = []
        for side, side_refs in ((core, mine), (1 - core, other)):
            for group, ref in enumerate(side_refs):
                begin = side * half + group * width
                codes_ref[:, begin : begin + width] = ref[:, :width]
                held.append((begin, ref[:, width : width + scales].astype(jnp.float32)))
        held = jnp.concatenate([value for _, value in sorted(held, key=lambda pair: pair[0])], axis=1)
        scales_ref[...] = held.T.astype(jnp.bfloat16)

    for core in range(2):
        pl.when(lax.axis_index("sub") == core)(functools.partial(put, core))


def assemble(mine, other, half):
    rows = mine[0].shape[0]
    codes, scales = pl.pallas_call(
        functools.partial(assemble_body, len(mine), half),
        out_shape=(
            jax.ShapeDtypeStruct((rows, 2 * half), jnp.bfloat16),
            jax.ShapeDtypeStruct((2 * half // BLOCK, rows), jnp.bfloat16),
        ),
        in_specs=[VMEM] * (2 * len(mine)),
        out_specs=(VMEM, VMEM),
        compiler_params=PARAMS,
        cost_estimate=SMALL,
    )(*mine, *other)
    return codes, scales.T


def cut(depth):
    if depth % UNIT or depth < 8 * UNIT:
        return [depth]
    units = depth // UNIT
    sizes = [max(1, units * share // 13) for share in SHARES]
    return [size * UNIT for size in sizes + [units - sum(sizes)]]


def shards(hidden, down_weight, sign_bits):
    tensor_count = lax.axis_size("tensor")
    seq_count = lax.axis_size("seq")
    sub_count = lax.axis_size("sub")
    depth = hidden.shape[1]
    half = down_weight.shape[1] // sub_count
    per_sub = seq_count // sub_count
    levels = tensor_count.bit_length() - 1
    wide, wide_chunk = min(256, half // GROUPS), min(512, half // GROUPS)
    flips = (2 * sign_bits - 1).astype(jnp.float32)[None, :]
    rotation = jnp.asarray(hadamard(BLOCK))

    def swap(values):
        return lax.ppermute(values, "sub", [(0, 1), (1, 0)])

    def exchange(values, level):
        return lax.ppermute(values, "tensor", [(t, t ^ 1 << level) for t in range(tensor_count)])

    def reduce(halves, begin):
        tokens = (yield None) or []
        kept, came = halves[1::2], [swap(sent) for sent in halves[::2]]
        for level in range(levels):
            sent, held = halve(kept, came, level, tokens)
            tokens = (yield sent) or []
            kept, came = [held], [exchange(sent, level)]
        yield encode(kept[0], came[0], begin, flips, rotation, tokens)

    def spread(packed):
        pieces = {0: packed}
        for level in reversed(range(levels)):
            for index in list(pieces):
                pieces[index ^ 1 << level] = exchange(pieces[index], level)
        return [pieces[index] for index in range(tensor_count)]

    sizes = cut(depth)
    places = [sum(sizes[:index]) for index in range(len(sizes))]
    parts = slices_of(hidden, list(zip(places, sizes)))
    arrivals = []
    for shift in range(1, seq_count):
        pairs = [(s, (s + shift) % seq_count) for s in range(seq_count)]
        arrivals.append([lax.ppermute(part, "seq", pairs) for part in parts])

    if len(sizes) == 1:
        outs = multiply([[parts[0]], [arrivals[0][0]]], down_weight, 0, [None, None], [True, True], wide_chunk)
        reduced = [list(reduce(outs[:2], 0))[-1], list(reduce(outs[2:], 0))[-1]]
        for arrived in arrivals[1:]:
            outs = multiply([[arrived[0]]], down_weight, 0, [None], [True], wide_chunk)
            reduced.append(list(reduce(outs, 0))[-1])
        results = [[spread(packed)] for packed in reduced]
    else:
        (own,) = multiply([parts[1:]], down_weight, sizes[0], [None], [False], wide, tokens=parts[:1])
        *halves, total = multiply(
            [[parts[0]], [arrivals[0][0]]], down_weight, 0, [own, None], [True, False], wide_chunk, groups=GROUPS
        )
        own_steps = reduce(halves, 0)
        next(own_steps)
        tokens = [own_steps.send([arrivals[0][1]])]
        results = []
        for shift, arrived in enumerate(arrivals):
            if shift:
                (total,) = multiply([[arrived[0]]], down_weight, 0, [None], [False], wide_chunk)
            for index in range(1, len(sizes) - 1):
                (total,) = multiply(
                    [[arrived[index]]], down_weight, places[index], [total], [False], wide_chunk, tokens=tokens
                )
                if not results:
                    step = own_steps.send([total])
                    tokens = [step]
                    if step.shape[1] > half:
                        results.append([spread(step)])
            if not results:
                results.append([spread(list(own_steps)[-1])])
            outs = multiply(
                [[arrived[-1]]], down_weight, places[-1], [total], [True], wide_chunk, groups=GROUPS, tokens=tokens
            )
            remote, all_steps = [], []
            for group in range(GROUPS):
                sent, kept = outs[2 * group : 2 * group + 2]
                if group == GROUPS - 1 and shift == 0 and levels > 1:
                    sent = gate(sent, [results[0][0][1], results[0][0][1 << levels - 1]])
                all_steps.append(reduce([sent, kept], group * half // GROUPS))
                next(all_steps[-1])
            last = []
            for level in range(levels + 1):
                for group, steps in enumerate(all_steps):
                    wait = list(last) if group == 0 else []
                    if group == 0 and level == 1 and shift == 0:
                        wait += results[0][0][1:]
                    step = steps.send(wait)
                    if level == levels:
                        remote.append(spread(step))
                last = [step]
            results.append(remote)
            tokens = []

    groups = max(len(result) for result in results)
    width = half // groups
    other = [swap(choose(results, group, width, True, per_sub)) for group in range(groups)]
    mine = [choose(results, group, width, False, per_sub) for group in range(groups)]
    return assemble(mine, other, half)


def solution(mesh):
    return jax.shard_map(
        shards,
        mesh=mesh,
        in_specs=(P(("groups", "seq"), ("tensor", "sub")), P(("tensor", "sub"), "seq"), P("seq")),
        out_specs=(P(("groups", "sub"), "seq"), P(("groups", "sub"), "seq")),
        check_vma=False,
    )
```

```python
import functools
import math

import jax
import jax.numpy as jnp
import numpy as np
from jax import lax
from jax.experimental import pallas as pl
from jax.experimental.pallas import tpu as pltpu
from jax.sharding import PartitionSpec as P

BLOCK = 128
UNIT = 512
GROUPS = 2
VMEM_LIMIT = 6 * 2**20
SHARES = (4, 3, 4)
epsilon = 1e-06

SMALL = pl.CostEstimate(flops=1, bytes_accessed=1, transcendentals=0)
PARAMS = pltpu.CompilerParams(vmem_limit_bytes=VMEM_LIMIT)
VMEM = pl.BlockSpec(memory_space=pltpu.VMEM)
ANY = pl.BlockSpec(memory_space=pl.ANY)
HBM = pl.BlockSpec(memory_space=pltpu.HBM)


def hadamard(order):
    indices = np.arange(order)
    parity = np.zeros((order, order), np.int64)
    for position in range(order.bit_length() - 1):
        parity = parity + (indices[:, None] >> position & 1) * (indices[None, :] >> position & 1)
    return ((1 - 2 * (parity % 2)) / math.sqrt(order)).astype(np.float32)


def slice_body(places, in_ref, *refs):
    out_refs, arrived = refs[:-1], refs[-1]
    copies = [
        pltpu.make_async_copy(in_ref.at[:, at : at + size], out_ref, arrived.at[index])
        for index, ((at, size), out_ref) in enumerate(zip(places, out_refs))
    ]
    for copy in copies:
        copy.start()
    for copy in copies:
        copy.wait()


def slices_of(values, places):
    return pl.pallas_call(
        functools.partial(slice_body, places),
        out_shape=[jax.ShapeDtypeStruct((values.shape[0], size), values.dtype) for _, size in places],
        in_specs=[HBM],
        out_specs=[VMEM] * len(places),
        scratch_shapes=[pltpu.SemaphoreType.DMA((len(places),))],
        compiler_params=PARAMS,
        cost_estimate=SMALL,
    )(values)


def multiply_body(spans, has_totals, splits, row, groups, only, *refs):
    lefts = [refs[begin:end] for begin, end in spans]
    refs = refs[spans[-1][1] :]
    w_ref, refs = refs[0], refs[1:]
    total_refs, refs = list(refs[: sum(has_totals)]), refs[sum(has_totals) :]
    buffer, arrived = refs[-2:]
    outs_of_split = 2 if only is not None else 2 * groups
    out_count = sum(outs_of_split if split else 1 for split in splits)
    out_refs = refs[-2 - out_count : -2]
    steps, depth, wide = buffer.shape
    rows = lefts[0][0].shape[0]
    in_half = w_ref.shape[1] // wide // 2
    first = in_half // groups
    here = lax.axis_index("sub")

    def column(n):
        if not any(splits):
            return n
        group, place = n // (2 * first), n % (2 * first)
        group = group if only is None else only
        side, place = (here, place - first) if place >= first else (1 - here, place)
        return side * in_half + group * first + place

    def at(block):
        return pl.ds(pl.multiple_of(block * wide, wide), wide)

    def copy(n):
        return pltpu.make_async_copy(w_ref.at[pl.ds(row, depth), at(column(n))], buffer.at[n], arrived.at[n])

    def step(n):
        copy(n).wait()
        product, begin = None, 0
        for index in range(len(lefts[0])):
            parts = [left[index][...] for left in lefts]
            left = parts[0] if len(parts) == 1 else jnp.concatenate(parts, axis=0)
            end = begin + left.shape[1]
            part = jnp.dot(left, buffer[n, begin:end], preferred_element_type=jnp.float32)
            product = part if product is None else product + part
            begin = end
        totals, outs = list(total_refs), list(out_refs)
        for index in range(len(lefts)):
            value = product[index * rows : (index + 1) * rows]
            if has_totals[index]:
                value = value + totals.pop(0)[:, at(column(n))]
            if splits[index]:
                group, place = n // (2 * first), n % (2 * first)
                out_ref = outs[2 * group + place // first]
                begin = place % first * wide
                out_ref[:, begin : begin + wide] = value.astype(out_ref.dtype)
                outs = outs[outs_of_split:]
            else:
                outs.pop(0)[:, at(column(n))] = value

    for n in range(steps):
        copy(n).start()
    if any(splits):
        for n in range(steps):
            step(n)
    else:
        pl.loop(0, steps)(step)


def multiply(lefts, weight, row, totals, splits, wide, groups=1, only=None, tokens=()):
    rows = lefts[0][0].shape[0]
    depth = sum(part.shape[1] for part in lefts[0])
    columns = weight.shape[1]
    steps = columns // wide // (1 if only is None else groups)
    spans = [(index * len(left), (index + 1) * len(left)) for index, left in enumerate(lefts)]
    held = [total for total in totals if total is not None]
    out_shape = []
    for split in splits:
        if split:
            out_shape += [
                jax.ShapeDtypeStruct((rows, columns // 2 // groups), jnp.bfloat16),
                jax.ShapeDtypeStruct((rows, columns // 2 // groups), jnp.float32),
            ] * (groups if only is None else 1)
        else:
            out_shape.append(jax.ShapeDtypeStruct((rows, columns), jnp.float32))
    body = functools.partial(
        multiply_body, spans, [total is not None for total in totals], splits, row, groups, only
    )
    return pl.pallas_call(
        body,
        out_shape=out_shape,
        in_specs=[VMEM] * spans[-1][1] + [HBM] + [VMEM] * len(held) + [ANY] * len(tokens),
        out_specs=[VMEM] * len(out_shape),
        scratch_shapes=[
            pltpu.VMEM((steps, depth, wide), weight.dtype),
            pltpu.SemaphoreType.DMA((steps,)),
        ],
        compiler_params=pltpu.CompilerParams(
            vmem_limit_bytes=2 * steps * depth * wide + VMEM_LIMIT
        ),
        cost_estimate=SMALL,
    )(*[part for left in lefts for part in left], weight, *held, *tokens)


def gate(values, tokens):
    return pl.pallas_call(
        lambda *refs: None,
        out_shape=jax.ShapeDtypeStruct(values.shape, values.dtype),
        in_specs=[ANY] * (1 + len(tokens)),
        out_specs=ANY,
        input_output_aliases={0: 0},
        compiler_params=PARAMS,
        cost_estimate=SMALL,
    )(values, *tokens)


def halve_body(level, count, *refs):
    kept_refs, came_refs, (sent_out, kept_out) = refs[:count], refs[count : 2 * count], refs[-2:]
    half, columns = sent_out.shape
    width = columns // count

    def put(bit):
        mine, other = slice(bit * half, (bit + 1) * half), slice((1 - bit) * half, (2 - bit) * half)
        for index, (kept_ref, came_ref) in enumerate(zip(kept_refs, came_refs)):
            at = slice(index * width, (index + 1) * width)
            kept_out[:, at] = kept_ref[mine] + came_ref[mine].astype(jnp.float32)
            sent_out[:, at] = (kept_ref[other] + came_ref[other].astype(jnp.float32)).astype(jnp.bfloat16)

    for bit in range(2):
        pl.when(lax.axis_index("tensor") >> level & 1 == bit)(functools.partial(put, bit))


def halve(kept, came, level, tokens=()):
    rows, columns = kept[0].shape
    half, columns = rows // 2, columns * len(kept)
    if half % 16:
        total = jnp.concatenate(kept, axis=1) + jnp.concatenate(came, axis=1).astype(jnp.float32)
        bit = lax.axis_index("tensor") >> level & 1
        sent = lax.dynamic_slice_in_dim(total, (1 - bit) * half, half, 0).astype(jnp.bfloat16)
        return sent, lax.dynamic_slice_in_dim(total, bit * half, half, 0)
    return pl.pallas_call(
        functools.partial(halve_body, level, len(kept)),
        out_shape=[
            jax.ShapeDtypeStruct((half, columns), jnp.bfloat16),
            jax.ShapeDtypeStruct((half, columns), jnp.float32),
        ],
        in_specs=[VMEM] * (2 * len(kept)) + [ANY] * len(tokens),
        out_specs=[VMEM, VMEM],
        compiler_params=PARAMS,
        cost_estimate=SMALL,
    )(*kept, *came, *tokens)


def encode_body(begin, kept_ref, came_ref, flips_ref, rotation_ref, *refs):
    out_ref = refs[-1]
    rows, columns = kept_ref.shape
    half = flips_ref.shape[1] // 2
    rotation = rotation_ref[...]
    lane = lax.broadcasted_iota(jnp.int32, (rows, BLOCK), 1)
    scales = jnp.zeros((rows, BLOCK), jnp.float32)
    for block in range(columns // BLOCK):
        at = slice(block * BLOCK, (block + 1) * BLOCK)
        flips = flips_ref[:, pl.ds(pl.multiple_of(lax.axis_index("sub") * half + begin + block * BLOCK, BLOCK), BLOCK)]
        total = (kept_ref[:, at] + came_ref[:, at].astype(jnp.float32)) * flips
        rotated = jnp.dot(
            total, rotation, precision=lax.Precision.HIGHEST, preferred_element_type=jnp.float32
        )
        largest = jnp.max(jnp.abs(rotated), axis=1, keepdims=True)
        scale = (largest + epsilon).astype(jnp.bfloat16).astype(jnp.float32)
        out_ref[:, at] = (rotated / scale).astype(jnp.bfloat16)
        scales = jnp.where(lane == block, scale, scales)
    out_ref[:, columns:] = scales.astype(jnp.bfloat16)


def encode(kept, came, begin, flips, rotation, tokens=()):
    rows, columns = kept.shape
    return pl.pallas_call(
        functools.partial(encode_body, begin),
        out_shape=jax.ShapeDtypeStruct((rows, columns + BLOCK), jnp.bfloat16),
        in_specs=[VMEM] * 4 + [ANY] * len(tokens),
        out_specs=VMEM,
        compiler_params=PARAMS,
        cost_estimate=SMALL,
    )(kept, came, flips, rotation, *tokens)


def rank_of(index, count):
    levels = count.bit_length() - 1
    return sum((index >> level & 1) << (levels - 1 - level) for level in range(levels))


def block_of(other, place, places, blocks):
    sub = lax.axis_index("sub")
    sub = 1 - sub if other else sub
    return lax.rem(lax.axis_index("seq") - (sub * places + place) + blocks, blocks)


def choose_body(blocks, pieces, width, at, other, places, *refs):
    out_ref = refs[-1]
    rows = refs[0].shape[0]
    scales = width // BLOCK

    def put(block, place):
        begin, scale_at = at[block]
        for piece in range(pieces):
            ref = refs[block * pieces + piece]
            row = (place * pieces + rank_of(lax.axis_index("tensor") ^ piece, pieces)) * rows
            here = pl.ds(pl.multiple_of(row, rows), rows)
            out_ref[here, :width] = ref[:, begin : begin + width]
            out_ref[here, width : width + scales] = ref[:, scale_at : scale_at + scales]

    for place in range(places):
        for block in range(blocks):
            pl.when(block_of(other, place, places, blocks) == block)(functools.partial(put, block, place))


def choose(results, group, width, other, places):
    picked, at = [], []
    for result in results:
        if len(result) == 1:
            pieces, begin = result[0], group * width
            at.append((begin, pieces[0].shape[1] - BLOCK + begin // BLOCK))
        else:
            pieces = result[group]
            at.append((0, width))
        picked.append(pieces)
    rows = picked[0][0].shape[0]
    count = len(picked[0])
    if rows % 16:
        blocks = []
        for pieces, (begin, scale_at) in zip(picked, at):
            block = jnp.zeros((count * rows, width + BLOCK), jnp.bfloat16)
            for index, piece in enumerate(pieces):
                scale = jnp.pad(piece[:, scale_at : scale_at + width // BLOCK], ((0, 0), (0, BLOCK - width // BLOCK)))
                part = jnp.concatenate([piece[:, begin : begin + width], scale], axis=1)
                block = lax.dynamic_update_slice_in_dim(block, part, rank_of(lax.axis_index("tensor") ^ index, count) * rows, 0)
            blocks.append(block)
        stacked = jnp.stack(blocks)
        return jnp.concatenate([stacked[block_of(other, place, places, len(blocks))] for place in range(places)])
    return pl.pallas_call(
        functools.partial(choose_body, len(picked), count, width, at, other, places),
        out_shape=jax.ShapeDtypeStruct((places * count * rows, width + BLOCK), jnp.bfloat16),
        in_specs=[VMEM] * (len(picked) * count),
        out_specs=VMEM,
        compiler_params=PARAMS,
        cost_estimate=SMALL,
    )(*[piece for pieces in picked for piece in pieces])


def assemble_body(groups, half, *refs):
    mine, other = refs[:groups], refs[groups : 2 * groups]
    codes_ref, scales_ref = refs[2 * groups :]
    width = half // groups
    scales = width // BLOCK

    def put(core):
        held = []
        for side, side_refs in ((core, mine), (1 - core, other)):
            for group, ref in enumerate(side_refs):
                begin = side * half + group * width
                codes_ref[:, begin : begin + width] = ref[:, :width]
                held.append((begin, ref[:, width : width + scales].astype(jnp.float32)))
        held = jnp.concatenate([value for _, value in sorted(held, key=lambda pair: pair[0])], axis=1)
        scales_ref[...] = held.T.astype(jnp.bfloat16)

    for core in range(2):
        pl.when(lax.axis_index("sub") == core)(functools.partial(put, core))


def assemble(mine, other, half):
    rows = mine[0].shape[0]
    codes, scales = pl.pallas_call(
        functools.partial(assemble_body, len(mine), half),
        out_shape=(
            jax.ShapeDtypeStruct((rows, 2 * half), jnp.bfloat16),
            jax.ShapeDtypeStruct((2 * half // BLOCK, rows), jnp.bfloat16),
        ),
        in_specs=[VMEM] * (2 * len(mine)),
        out_specs=(VMEM, VMEM),
        compiler_params=PARAMS,
        cost_estimate=SMALL,
    )(*mine, *other)
    return codes, scales.T


def cut(depth):
    if depth % UNIT or depth < 8 * UNIT:
        return [depth]
    units = depth // UNIT
    sizes = [max(1, units * share // 13) for share in SHARES]
    return [size * UNIT for size in sizes + [units - sum(sizes)]]


def shards(hidden, down_weight, sign_bits):
    tensor_count = lax.axis_size("tensor")
    seq_count = lax.axis_size("seq")
    sub_count = lax.axis_size("sub")
    depth = hidden.shape[1]
    half = down_weight.shape[1] // sub_count
    per_sub = seq_count // sub_count
    levels = tensor_count.bit_length() - 1
    wide, wide_chunk = min(256, half // GROUPS), min(512, half // GROUPS)
    flips = (2 * sign_bits - 1).astype(jnp.float32)[None, :]
    rotation = jnp.asarray(hadamard(BLOCK))

    def swap(values):
        return lax.ppermute(values, "sub", [(0, 1), (1, 0)])

    def exchange(values, level):
        return lax.ppermute(values, "tensor", [(t, t ^ 1 << level) for t in range(tensor_count)])

    def reduce(halves, begin):
        tokens = (yield None) or []
        kept, came = halves[1::2], [swap(sent) for sent in halves[::2]]
        for level in range(levels):
            sent, held = halve(kept, came, level, tokens)
            tokens = (yield sent) or []
            kept, came = [held], [exchange(sent, level)]
        yield encode(kept[0], came[0], begin, flips, rotation, tokens)

    def spread(packed):
        pieces = {0: packed}
        for level in reversed(range(levels)):
            for index in list(pieces):
                pieces[index ^ 1 << level] = exchange(pieces[index], level)
        return [pieces[index] for index in range(tensor_count)]

    sizes = cut(depth)
    places = [sum(sizes[:index]) for index in range(len(sizes))]
    parts = slices_of(hidden, list(zip(places, sizes)))
    arrivals = []
    for shift in range(1, seq_count):
        pairs = [(s, (s + shift) % seq_count) for s in range(seq_count)]
        arrivals.append([lax.ppermute(part, "seq", pairs) for part in parts])

    if len(sizes) == 1:
        outs = multiply([[parts[0]], [arrivals[0][0]]], down_weight, 0, [None, None], [True, True], wide_chunk)
        reduced = [list(reduce(outs[:2], 0))[-1], list(reduce(outs[2:], 0))[-1]]
        for arrived in arrivals[1:]:
            outs = multiply([[arrived[0]]], down_weight, 0, [None], [True], wide_chunk)
            reduced.append(list(reduce(outs, 0))[-1])
        results = [[spread(packed)] for packed in reduced]
    else:
        (own,) = multiply([parts[1:]], down_weight, sizes[0], [None], [False], wide, tokens=parts[:1])
        *halves, total = multiply(
            [[parts[0]], [arrivals[0][0]]], down_weight, 0, [own, None], [True, False], wide_chunk, groups=GROUPS
        )
        own_steps = reduce(halves, 0)
        next(own_steps)
        tokens = [own_steps.send([arrivals[0][1]])]
        results = []
        for shift, arrived in enumerate(arrivals):
            if shift:
                (total,) = multiply([[arrived[0]]], down_weight, 0, [None], [False], wide_chunk)
            for index in range(1, len(sizes) - 1):
                (total,) = multiply(
                    [[arrived[index]]], down_weight, places[index], [total], [False], wide_chunk, tokens=tokens
                )
                if not results:
                    step = own_steps.send([total])
                    tokens = [step]
                    if step.shape[1] > half:
                        results.append([spread(step)])
            if not results:
                results.append([spread(list(own_steps)[-1])])
            remote, all_steps = [], []
            for group in range(GROUPS):
                sent, kept = multiply(
                    [[arrived[-1]]], down_weight, places[-1], [total], [True], wide_chunk,
                    groups=GROUPS, only=group, tokens=tokens,
                )
                tokens = [sent]
                if group == GROUPS - 1 and shift == 0 and levels > 1:
                    sent = gate(sent, [results[0][0][1], results[0][0][1 << levels - 1]])
                all_steps.append(reduce([sent, kept], group * half // GROUPS))
                next(all_steps[-1])
            last = []
            for level in range(levels + 1):
                for group, steps in enumerate(all_steps):
                    wait = list(last) if group == 0 else []
                    if group == 0 and level == levels and shift == 0:
                        wait += results[0][0][1:]
                    step = steps.send(wait)
                    if level == levels:
                        remote.append(spread(step))
                last = [step]
            results.append(remote)
            tokens = []

    groups = max(len(result) for result in results)
    width = half // groups
    other = [swap(choose(results, group, width, True, per_sub)) for group in range(groups)]
    mine = [choose(results, group, width, False, per_sub) for group in range(groups)]
    return assemble(mine, other, half)


def solution(mesh):
    return jax.shard_map(
        shards,
        mesh=mesh,
        in_specs=(P(("groups", "seq"), ("tensor", "sub")), P(("tensor", "sub"), "seq"), P("seq")),
        out_specs=(P(("groups", "sub"), "seq"), P(("groups", "sub"), "seq")),
        check_vma=False,
    )
```

```python
import functools
import math

import jax
import jax.numpy as jnp
import numpy as np
from jax import lax
from jax.experimental import pallas as pl
from jax.experimental.pallas import tpu as pltpu
from jax.sharding import PartitionSpec as P

BLOCK = 128
UNIT = 512
GROUPS = 2
VMEM_LIMIT = 6 * 2**20
SHARES = (4, 4, 3)
epsilon = 1e-06

SMALL = pl.CostEstimate(flops=1, bytes_accessed=1, transcendentals=0)
PARAMS = pltpu.CompilerParams(vmem_limit_bytes=VMEM_LIMIT)
VMEM = pl.BlockSpec(memory_space=pltpu.VMEM)
ANY = pl.BlockSpec(memory_space=pl.ANY)
HBM = pl.BlockSpec(memory_space=pltpu.HBM)


def hadamard(order):
    indices = np.arange(order)
    parity = np.zeros((order, order), np.int64)
    for position in range(order.bit_length() - 1):
        parity = parity + (indices[:, None] >> position & 1) * (indices[None, :] >> position & 1)
    return ((1 - 2 * (parity % 2)) / math.sqrt(order)).astype(np.float32)


def slice_body(places, in_ref, *refs):
    out_refs, arrived = refs[:-1], refs[-1]
    copies = [
        pltpu.make_async_copy(in_ref.at[:, at : at + size], out_ref, arrived.at[index])
        for index, ((at, size), out_ref) in enumerate(zip(places, out_refs))
    ]
    for copy in copies:
        copy.start()
    for copy in copies:
        copy.wait()


def slices_of(values, places):
    return pl.pallas_call(
        functools.partial(slice_body, places),
        out_shape=[jax.ShapeDtypeStruct((values.shape[0], size), values.dtype) for _, size in places],
        in_specs=[HBM],
        out_specs=[VMEM] * len(places),
        scratch_shapes=[pltpu.SemaphoreType.DMA((len(places),))],
        compiler_params=PARAMS,
        cost_estimate=SMALL,
    )(values)


def multiply_body(spans, has_totals, splits, row, groups, only, *refs):
    lefts = [refs[begin:end] for begin, end in spans]
    refs = refs[spans[-1][1] :]
    w_ref, refs = refs[0], refs[1:]
    total_refs, refs = list(refs[: sum(has_totals)]), refs[sum(has_totals) :]
    buffer, arrived = refs[-2:]
    outs_of_split = 2 if only is not None else 2 * groups
    out_count = sum(outs_of_split if split else 1 for split in splits)
    out_refs = refs[-2 - out_count : -2]
    steps, depth, wide = buffer.shape
    rows = lefts[0][0].shape[0]
    in_half = w_ref.shape[1] // wide // 2
    first = in_half // groups
    here = lax.axis_index("sub")

    def column(n):
        if not any(splits):
            return n
        group, place = n // (2 * first), n % (2 * first)
        group = group if only is None else only
        side, place = (here, place - first) if place >= first else (1 - here, place)
        return side * in_half + group * first + place

    def at(block):
        return pl.ds(pl.multiple_of(block * wide, wide), wide)

    def copy(n):
        return pltpu.make_async_copy(w_ref.at[pl.ds(row, depth), at(column(n))], buffer.at[n], arrived.at[n])

    def step(n):
        copy(n).wait()
        product, begin = None, 0
        for index in range(len(lefts[0])):
            parts = [left[index][...] for left in lefts]
            left = parts[0] if len(parts) == 1 else jnp.concatenate(parts, axis=0)
            end = begin + left.shape[1]
            part = jnp.dot(left, buffer[n, begin:end], preferred_element_type=jnp.float32)
            product = part if product is None else product + part
            begin = end
        totals, outs = list(total_refs), list(out_refs)
        for index in range(len(lefts)):
            value = product[index * rows : (index + 1) * rows]
            if has_totals[index]:
                value = value + totals.pop(0)[:, at(column(n))]
            if splits[index]:
                group, place = n // (2 * first), n % (2 * first)
                out_ref = outs[2 * group + place // first]
                begin = place % first * wide
                out_ref[:, begin : begin + wide] = value.astype(out_ref.dtype)
                outs = outs[outs_of_split:]
            else:
                outs.pop(0)[:, at(column(n))] = value

    for n in range(steps):
        copy(n).start()
    if any(splits):
        for n in range(steps):
            step(n)
    else:
        pl.loop(0, steps)(step)


def multiply(lefts, weight, row, totals, splits, wide, groups=1, only=None, tokens=()):
    rows = lefts[0][0].shape[0]
    depth = sum(part.shape[1] for part in lefts[0])
    columns = weight.shape[1]
    steps = columns // wide // (1 if only is None else groups)
    spans = [(index * len(left), (index + 1) * len(left)) for index, left in enumerate(lefts)]
    held = [total for total in totals if total is not None]
    out_shape = []
    for split in splits:
        if split:
            out_shape += [
                jax.ShapeDtypeStruct((rows, columns // 2 // groups), jnp.bfloat16),
                jax.ShapeDtypeStruct((rows, columns // 2 // groups), jnp.float32),
            ] * (groups if only is None else 1)
        else:
            out_shape.append(jax.ShapeDtypeStruct((rows, columns), jnp.float32))
    body = functools.partial(
        multiply_body, spans, [total is not None for total in totals], splits, row, groups, only
    )
    return pl.pallas_call(
        body,
        out_shape=out_shape,
        in_specs=[VMEM] * spans[-1][1] + [HBM] + [VMEM] * len(held) + [ANY] * len(tokens),
        out_specs=[VMEM] * len(out_shape),
        scratch_shapes=[
            pltpu.VMEM((steps, depth, wide), weight.dtype),
            pltpu.SemaphoreType.DMA((steps,)),
        ],
        compiler_params=pltpu.CompilerParams(
            vmem_limit_bytes=2 * steps * depth * wide + VMEM_LIMIT
        ),
        cost_estimate=SMALL,
    )(*[part for left in lefts for part in left], weight, *held, *tokens)


def gate(values, tokens):
    return pl.pallas_call(
        lambda *refs: None,
        out_shape=jax.ShapeDtypeStruct(values.shape, values.dtype),
        in_specs=[ANY] * (1 + len(tokens)),
        out_specs=ANY,
        input_output_aliases={0: 0},
        compiler_params=PARAMS,
        cost_estimate=SMALL,
    )(values, *tokens)


def halve_body(level, count, *refs):
    kept_refs, came_refs, (sent_out, kept_out) = refs[:count], refs[count : 2 * count], refs[-2:]
    half, columns = sent_out.shape
    width = columns // count

    def put(bit):
        mine, other = slice(bit * half, (bit + 1) * half), slice((1 - bit) * half, (2 - bit) * half)
        for index, (kept_ref, came_ref) in enumerate(zip(kept_refs, came_refs)):
            at = slice(index * width, (index + 1) * width)
            kept_out[:, at] = kept_ref[mine] + came_ref[mine].astype(jnp.float32)
            sent_out[:, at] = (kept_ref[other] + came_ref[other].astype(jnp.float32)).astype(jnp.bfloat16)

    for bit in range(2):
        pl.when(lax.axis_index("tensor") >> level & 1 == bit)(functools.partial(put, bit))


def halve(kept, came, level, tokens=()):
    rows, columns = kept[0].shape
    half, columns = rows // 2, columns * len(kept)
    if half % 16:
        total = jnp.concatenate(kept, axis=1) + jnp.concatenate(came, axis=1).astype(jnp.float32)
        bit = lax.axis_index("tensor") >> level & 1
        sent = lax.dynamic_slice_in_dim(total, (1 - bit) * half, half, 0).astype(jnp.bfloat16)
        return sent, lax.dynamic_slice_in_dim(total, bit * half, half, 0)
    return pl.pallas_call(
        functools.partial(halve_body, level, len(kept)),
        out_shape=[
            jax.ShapeDtypeStruct((half, columns), jnp.bfloat16),
            jax.ShapeDtypeStruct((half, columns), jnp.float32),
        ],
        in_specs=[VMEM] * (2 * len(kept)) + [ANY] * len(tokens),
        out_specs=[VMEM, VMEM],
        compiler_params=PARAMS,
        cost_estimate=SMALL,
    )(*kept, *came, *tokens)


def encode_body(begin, lane, last, kept_ref, came_ref, scales_ref, flips_ref, rotation_ref, *refs):
    rows, columns = kept_ref.shape
    half = flips_ref.shape[1] // 2
    rotation = rotation_ref[...]
    lanes = lax.broadcasted_iota(jnp.int32, (rows, BLOCK), 1)
    scales = scales_ref[...]
    for block in range(columns // BLOCK):
        at = slice(block * BLOCK, (block + 1) * BLOCK)
        place = lax.axis_index("sub") * half + begin + block * BLOCK
        flips = flips_ref[:, pl.ds(pl.multiple_of(place, BLOCK), BLOCK)]
        total = (kept_ref[:, at] + came_ref[:, at].astype(jnp.float32)) * flips
        rotated = jnp.dot(
            total, rotation, precision=lax.Precision.HIGHEST, preferred_element_type=jnp.float32
        )
        largest = jnp.max(jnp.abs(rotated), axis=1, keepdims=True)
        scale = (largest + epsilon).astype(jnp.bfloat16).astype(jnp.float32)
        refs[-1 if last else -2][:, at] = (rotated / scale).astype(jnp.bfloat16)
        scales = jnp.where(lanes == lane + block, scale, scales)
    if last:
        refs[-1][:, columns:] = scales.astype(jnp.bfloat16)
    else:
        refs[-1][...] = scales


def encode(kept, came, begin, scales, lane, last, flips, rotation, tokens=()):
    rows, columns = kept.shape
    if last:
        out_shape = [jax.ShapeDtypeStruct((rows, columns + BLOCK), jnp.bfloat16)]
    else:
        out_shape = [
            jax.ShapeDtypeStruct((rows, columns), jnp.bfloat16),
            jax.ShapeDtypeStruct((rows, BLOCK), jnp.float32),
        ]
    return pl.pallas_call(
        functools.partial(encode_body, begin, lane, last),
        out_shape=out_shape,
        in_specs=[VMEM] * 5 + [ANY] * len(tokens),
        out_specs=[VMEM] * len(out_shape),
        compiler_params=PARAMS,
        cost_estimate=SMALL,
    )(kept, came, scales, flips, rotation, *tokens)


def rank_of(index, count):
    levels = count.bit_length() - 1
    return sum((index >> level & 1) << (levels - 1 - level) for level in range(levels))


def block_of(other, place, places, blocks):
    sub = lax.axis_index("sub")
    sub = 1 - sub if other else sub
    return lax.rem(lax.axis_index("seq") - (sub * places + place) + blocks, blocks)


def choose_body(blocks, count, width, begins, other, places, scales, *refs):
    out_ref = refs[-1]
    rows = refs[0].shape[0]

    def put(block, place):
        for piece in range(count):
            row = (place * count + rank_of(lax.axis_index("tensor") ^ piece, count)) * rows
            here = pl.ds(pl.multiple_of(row, rows), rows)
            begin = begins[block]
            out_ref[here, :width] = refs[block * count + piece][:, begin : begin + width]
            if scales:
                ref = refs[blocks * count + piece]
                at = ref.shape[1] - BLOCK + block * scales
                out_ref[here, width : width + scales] = ref[:, at : at + scales]

    for place in range(places):
        for block in range(blocks):
            pl.when(block_of(other, place, places, blocks) == block)(functools.partial(put, block, place))


def choose(results, group, width, other, places, scales, tokens):
    picked = [result[0] if len(result) == 1 else result[group] for result in results]
    begins = [group * width if len(result) == 1 else 0 for result in results]
    last = results[-1][-1] if scales else []
    rows, count = picked[0][0].shape[0], len(picked[0])
    columns = width + (BLOCK if scales else 0)
    if rows % 16:
        blocks = []
        for block, (pieces, begin) in enumerate(zip(picked, begins)):
            held = jnp.zeros((count * rows, columns), jnp.bfloat16)
            for index, piece in enumerate(pieces):
                part = piece[:, begin : begin + width]
                if scales:
                    at = last[index].shape[1] - BLOCK + block * scales
                    scale = jnp.pad(last[index][:, at : at + scales], ((0, 0), (0, BLOCK - scales)))
                    part = jnp.concatenate([part, scale], axis=1)
                row = rank_of(lax.axis_index("tensor") ^ index, count) * rows
                held = lax.dynamic_update_slice_in_dim(held, part, row, 0)
            blocks.append(held)
        stacked = jnp.stack(blocks)
        return jnp.concatenate([stacked[block_of(other, place, places, len(blocks))] for place in range(places)])
    operands = [piece for pieces in picked for piece in pieces] + last
    return pl.pallas_call(
        functools.partial(choose_body, len(picked), count, width, begins, other, places, scales),
        out_shape=jax.ShapeDtypeStruct((places * count * rows, columns), jnp.bfloat16),
        in_specs=[VMEM] * len(operands) + [ANY] * len(tokens),
        out_specs=VMEM,
        compiler_params=PARAMS,
        cost_estimate=SMALL,
    )(*operands, *tokens)


def place_body(mine, half, widths, groups, scales, held, *refs):
    refs = refs[held:]
    codes_ref, sems = refs[-3] if scales else refs[-2], refs[-1]
    sub = lax.axis_index("sub")
    side = sub if mine else 1 - sub

    def copies(core):
        return [
            pltpu.make_async_copy(
                ref.at[:, :width], codes_ref.at[:, pl.ds(core * half + group * width, width)], sems.at[index]
            )
            for index, (ref, width, group) in enumerate(zip(refs, widths, groups))
        ]

    def put(core):
        for copy in copies(core):
            copy.start()
        if scales:
            pair = [ref[:, width : width + scales] for ref, width in ((refs[len(widths)], widths[-1]), (refs[len(widths) - 1], widths[-1]))]
            pair = pair if core == 1 else pair[::-1]
            held = jnp.concatenate([value.astype(jnp.float32) for value in pair], axis=1)
            refs[-2][...] = held.T.astype(jnp.bfloat16)
        for copy in copies(core):
            copy.wait()

    for core in range(2):
        pl.when(side == core)(functools.partial(put, core))


def put_codes(arrays, groups, width, half, mine, codes=None, scales_of=None):
    rows = arrays[0].shape[0]
    scales = half // BLOCK if scales_of is not None else 0
    operands = list(arrays) + ([scales_of] if scales else [])
    out_shape = [jax.ShapeDtypeStruct((rows, 2 * half), jnp.bfloat16)]
    out_specs = [HBM]
    if scales:
        out_shape.append(jax.ShapeDtypeStruct((2 * scales, rows), jnp.bfloat16))
        out_specs.append(VMEM)
    held = [] if codes is None else [codes]
    return pl.pallas_call(
        functools.partial(place_body, mine, half, [width] * len(arrays), groups, scales, len(held)),
        out_shape=out_shape,
        in_specs=[HBM] * len(held) + [VMEM] * len(operands),
        out_specs=out_specs,
        input_output_aliases={0: 0} if held else {},
        scratch_shapes=[pltpu.SemaphoreType.DMA((len(arrays),))],
        compiler_params=PARAMS,
        cost_estimate=SMALL,
    )(*held, *operands)


def cut(depth):
    if depth % UNIT or depth < 8 * UNIT:
        return [depth]
    units = depth // UNIT
    sizes = [max(1, units * share // 13) for share in SHARES]
    return [size * UNIT for size in sizes + [units - sum(sizes)]]


def shards(hidden, down_weight, sign_bits):
    tensor_count = lax.axis_size("tensor")
    seq_count = lax.axis_size("seq")
    sub_count = lax.axis_size("sub")
    depth = hidden.shape[1]
    half = down_weight.shape[1] // sub_count
    per_sub = seq_count // sub_count
    levels = tensor_count.bit_length() - 1
    wide, wide_chunk = min(256, half // GROUPS), min(512, half // GROUPS)
    flips = (2 * sign_bits - 1).astype(jnp.float32)[None, :]
    rotation = jnp.asarray(hadamard(BLOCK))

    def swap(values):
        return lax.ppermute(values, "sub", [(0, 1), (1, 0)])

    def exchange(values, level):
        return lax.ppermute(values, "tensor", [(t, t ^ 1 << level) for t in range(tensor_count)])

    def reduce(halves, begin, block, last):
        tokens = (yield None) or []
        kept, came = halves[1::2], [swap(sent) for sent in halves[::2]]
        for level in range(levels):
            sent, held = halve(kept, came, level, tokens)
            tokens = (yield sent) or []
            kept, came = [held], [exchange(sent, level)]
        packed, *rest = encode(
            kept[0], came[0], begin, scales[-1], (block * half + begin) // BLOCK, last, flips, rotation, tokens
        )
        scales.extend(rest)
        yield packed

    def spread(packed):
        pieces = {0: packed}
        for level in reversed(range(levels)):
            for index in list(pieces):
                pieces[index ^ 1 << level] = exchange(pieces[index], level)
        return [pieces[index] for index in range(tensor_count)]

    scales = [jnp.zeros((hidden.shape[0] // tensor_count, BLOCK), jnp.float32)]
    sizes = cut(depth)
    places = [sum(sizes[:index]) for index in range(len(sizes))]
    parts = slices_of(hidden, list(zip(places, sizes)))
    arrivals = []
    for shift in range(1, seq_count):
        pairs = [(s, (s + shift) % seq_count) for s in range(seq_count)]
        arrivals.append([lax.ppermute(part, "seq", pairs) for part in parts])

    if len(sizes) == 1:
        outs = multiply([[parts[0]], [arrivals[0][0]]], down_weight, 0, [None, None], [True, True], wide_chunk)
        reduced = [list(reduce(outs[:2], 0, 0, False))[-1], list(reduce(outs[2:], 0, 1, seq_count == 2))[-1]]
        for block, arrived in enumerate(arrivals[1:], 2):
            outs = multiply([[arrived[0]]], down_weight, 0, [None], [True], wide_chunk)
            reduced.append(list(reduce(outs, 0, block, block == seq_count - 1))[-1])
        results = [[spread(packed)] for packed in reduced]
    else:
        (own,) = multiply([parts[1:]], down_weight, sizes[0], [None], [False], wide, tokens=parts[:1])
        *halves, total = multiply(
            [[parts[0]], [arrivals[0][0]]], down_weight, 0, [own, None], [True, False], wide_chunk, groups=GROUPS
        )
        own_steps = reduce(halves, 0, 0, False)
        next(own_steps)
        tokens = [own_steps.send([arrivals[0][1]])]
        results = []
        for shift, arrived in enumerate(arrivals):
            if shift:
                (total,) = multiply([[arrived[0]]], down_weight, 0, [None], [False], wide_chunk)
            for index in range(1, len(sizes) - 1):
                (total,) = multiply(
                    [[arrived[index]]], down_weight, places[index], [total], [False], wide_chunk, tokens=tokens
                )
                if not results:
                    step = own_steps.send([total])
                    tokens = [step]
                    if step.shape[0] * tensor_count == hidden.shape[0] and len(scales) > 1:
                        results.append([spread(step)])
            if not results:
                results.append([spread(list(own_steps)[-1])])
            remote, all_steps = [], []
            for group in range(GROUPS):
                sent, kept = multiply(
                    [[arrived[-1]]], down_weight, places[-1], [total], [True], wide_chunk,
                    groups=GROUPS, only=group, tokens=tokens,
                )
                tokens = [sent]
                if group == GROUPS - 1 and shift == 0 and levels > 1:
                    sent = gate(sent, [results[0][0][1], results[0][0][1 << levels - 1]])
                all_steps.append(reduce([sent, kept], group * half // GROUPS, shift + 1, shift == seq_count - 2 and group == GROUPS - 1))
                next(all_steps[-1])
            last = []
            for level in range(levels + 1):
                for group, steps in enumerate(all_steps):
                    wait = list(last) if group == 0 else []
                    if group == GROUPS - 1 and level == levels and shift == 0:
                        wait += results[0][0][1:]
                    step = steps.send(wait)
                    if level == levels:
                        if remote and levels > 1:
                            step = gate(step, [remote[-1][1], remote[-1][1 << levels - 1]])
                        remote.append(spread(step))
                last = [step]
            results.append(remote)
            tokens = []

    groups = max(len(result) for result in results)
    width = half // groups
    last = groups - 1

    def chosen(group, other, tokens):
        return choose(results, group, width, other, per_sub, half // BLOCK if group == last else 0, tokens)

    came = []
    for group in range(groups):
        came.append(swap(chosen(group, True, came[-1:])))
    mine = [chosen(group, False, []) for group in range(groups)]
    (codes,) = put_codes(mine, list(range(groups)), width, half, True)
    if last:
        (codes,) = put_codes(came[:last], list(range(last)), width, half, False, codes)
    codes, flat = put_codes(came[last:], [last], width, half, False, codes, mine[last])
    return codes, flat.T


def solution(mesh):
    return jax.shard_map(
        shards,
        mesh=mesh,
        in_specs=(P(("groups", "seq"), ("tensor", "sub")), P(("tensor", "sub"), "seq"), P("seq")),
        out_specs=(P(("groups", "sub"), "seq"), P(("groups", "sub"), "seq")),
        check_vma=False,
    )
```

```python
import functools
import math

import jax
import jax.numpy as jnp
import numpy as np
from jax import lax
from jax.experimental import pallas as pl
from jax.experimental.pallas import tpu as pltpu
from jax.sharding import PartitionSpec as P

BLOCK = 128
UNIT = 512
GROUPS = 2
VMEM_LIMIT = 6 * 2**20
SHARES = (4, 4, 3)
epsilon = 1e-06

SMALL = pl.CostEstimate(flops=1, bytes_accessed=1, transcendentals=0)
PARAMS = pltpu.CompilerParams(vmem_limit_bytes=VMEM_LIMIT)
VMEM = pl.BlockSpec(memory_space=pltpu.VMEM)
ANY = pl.BlockSpec(memory_space=pl.ANY)
HBM = pl.BlockSpec(memory_space=pltpu.HBM)


def hadamard(order):
    indices = np.arange(order)
    parity = np.zeros((order, order), np.int64)
    for position in range(order.bit_length() - 1):
        parity = parity + (indices[:, None] >> position & 1) * (indices[None, :] >> position & 1)
    return ((1 - 2 * (parity % 2)) / math.sqrt(order)).astype(np.float32)


def slice_body(places, in_ref, *refs):
    out_refs, arrived = refs[:-1], refs[-1]
    copies = [
        pltpu.make_async_copy(in_ref.at[:, at : at + size], out_ref, arrived.at[index])
        for index, ((at, size), out_ref) in enumerate(zip(places, out_refs))
    ]
    for copy in copies:
        copy.start()
    for copy in copies:
        copy.wait()


def slices_of(values, places):
    return pl.pallas_call(
        functools.partial(slice_body, places),
        out_shape=[jax.ShapeDtypeStruct((values.shape[0], size), values.dtype) for _, size in places],
        in_specs=[HBM],
        out_specs=[VMEM] * len(places),
        scratch_shapes=[pltpu.SemaphoreType.DMA((len(places),))],
        compiler_params=PARAMS,
        cost_estimate=SMALL,
    )(values)


def multiply_body(spans, has_totals, splits, row, groups, only, *refs):
    lefts = [refs[begin:end] for begin, end in spans]
    refs = refs[spans[-1][1] :]
    w_ref, refs = refs[0], refs[1:]
    total_refs, refs = list(refs[: sum(has_totals)]), refs[sum(has_totals) :]
    buffer, arrived = refs[-2:]
    outs_of_split = 2 if only is not None else 2 * groups
    out_count = sum(outs_of_split if split else 1 for split in splits)
    out_refs = refs[-2 - out_count : -2]
    steps, depth, wide = buffer.shape
    rows = lefts[0][0].shape[0]
    in_half = w_ref.shape[1] // wide // 2
    first = in_half // groups
    here = lax.axis_index("sub")

    def column(n):
        if not any(splits):
            return n
        group, place = n // (2 * first), n % (2 * first)
        group = group if only is None else only
        side, place = (here, place - first) if place >= first else (1 - here, place)
        return side * in_half + group * first + place

    def at(block):
        return pl.ds(pl.multiple_of(block * wide, wide), wide)

    def copy(n):
        return pltpu.make_async_copy(w_ref.at[pl.ds(row, depth), at(column(n))], buffer.at[n], arrived.at[n])

    def step(n):
        copy(n).wait()
        product, begin = None, 0
        for index in range(len(lefts[0])):
            parts = [left[index][...] for left in lefts]
            left = parts[0] if len(parts) == 1 else jnp.concatenate(parts, axis=0)
            end = begin + left.shape[1]
            part = jnp.dot(left, buffer[n, begin:end], preferred_element_type=jnp.float32)
            product = part if product is None else product + part
            begin = end
        totals, outs = list(total_refs), list(out_refs)
        for index in range(len(lefts)):
            value = product[index * rows : (index + 1) * rows]
            if has_totals[index]:
                value = value + totals.pop(0)[:, at(column(n))]
            if splits[index]:
                group, place = n // (2 * first), n % (2 * first)
                out_ref = outs[2 * group + place // first]
                begin = place % first * wide
                out_ref[:, begin : begin + wide] = value.astype(out_ref.dtype)
                outs = outs[outs_of_split:]
            else:
                outs.pop(0)[:, at(column(n))] = value

    for n in range(steps):
        copy(n).start()
    if any(splits):
        for n in range(steps):
            step(n)
    else:
        pl.loop(0, steps)(step)


def multiply(lefts, weight, row, totals, splits, wide, groups=1, only=None, tokens=()):
    rows = lefts[0][0].shape[0]
    depth = sum(part.shape[1] for part in lefts[0])
    columns = weight.shape[1]
    steps = columns // wide // (1 if only is None else groups)
    spans = [(index * len(left), (index + 1) * len(left)) for index, left in enumerate(lefts)]
    held = [total for total in totals if total is not None]
    out_shape = []
    for split in splits:
        if split:
            out_shape += [
                jax.ShapeDtypeStruct((rows, columns // 2 // groups), jnp.bfloat16),
                jax.ShapeDtypeStruct((rows, columns // 2 // groups), jnp.float32),
            ] * (groups if only is None else 1)
        else:
            out_shape.append(jax.ShapeDtypeStruct((rows, columns), jnp.float32))
    body = functools.partial(
        multiply_body, spans, [total is not None for total in totals], splits, row, groups, only
    )
    return pl.pallas_call(
        body,
        out_shape=out_shape,
        in_specs=[VMEM] * spans[-1][1] + [HBM] + [VMEM] * len(held) + [ANY] * len(tokens),
        out_specs=[VMEM] * len(out_shape),
        scratch_shapes=[
            pltpu.VMEM((steps, depth, wide), weight.dtype),
            pltpu.SemaphoreType.DMA((steps,)),
        ],
        compiler_params=pltpu.CompilerParams(
            vmem_limit_bytes=2 * steps * depth * wide + VMEM_LIMIT
        ),
        cost_estimate=SMALL,
    )(*[part for left in lefts for part in left], weight, *held, *tokens)


def gate(values, tokens):
    return pl.pallas_call(
        lambda *refs: None,
        out_shape=jax.ShapeDtypeStruct(values.shape, values.dtype),
        in_specs=[ANY] * (1 + len(tokens)),
        out_specs=ANY,
        input_output_aliases={0: 0},
        compiler_params=PARAMS,
        cost_estimate=SMALL,
    )(values, *tokens)


def halve_body(level, count, *refs):
    kept_refs, came_refs, (sent_out, kept_out) = refs[:count], refs[count : 2 * count], refs[-2:]
    half, columns = sent_out.shape
    width = columns // count

    def put(bit):
        mine, other = slice(bit * half, (bit + 1) * half), slice((1 - bit) * half, (2 - bit) * half)
        for index, (kept_ref, came_ref) in enumerate(zip(kept_refs, came_refs)):
            at = slice(index * width, (index + 1) * width)
            kept_out[:, at] = kept_ref[mine] + came_ref[mine].astype(jnp.float32)
            sent_out[:, at] = (kept_ref[other] + came_ref[other].astype(jnp.float32)).astype(jnp.bfloat16)

    for bit in range(2):
        pl.when(lax.axis_index("tensor") >> level & 1 == bit)(functools.partial(put, bit))


def halve(kept, came, level, tokens=()):
    rows, columns = kept[0].shape
    half, columns = rows // 2, columns * len(kept)
    if half % 16:
        total = jnp.concatenate(kept, axis=1) + jnp.concatenate(came, axis=1).astype(jnp.float32)
        bit = lax.axis_index("tensor") >> level & 1
        sent = lax.dynamic_slice_in_dim(total, (1 - bit) * half, half, 0).astype(jnp.bfloat16)
        return sent, lax.dynamic_slice_in_dim(total, bit * half, half, 0)
    return pl.pallas_call(
        functools.partial(halve_body, level, len(kept)),
        out_shape=[
            jax.ShapeDtypeStruct((half, columns), jnp.bfloat16),
            jax.ShapeDtypeStruct((half, columns), jnp.float32),
        ],
        in_specs=[VMEM] * (2 * len(kept)) + [ANY] * len(tokens),
        out_specs=[VMEM, VMEM],
        compiler_params=PARAMS,
        cost_estimate=SMALL,
    )(*kept, *came, *tokens)


def encode_body(begin, lane, last, kept_ref, came_ref, scales_ref, flips_ref, rotation_ref, *refs):
    out_ref = refs[-1 if last else -2]
    rows, columns = kept_ref.shape
    half = flips_ref.shape[1] // 2
    rotation = rotation_ref[...]
    lanes = lax.broadcasted_iota(jnp.int32, (rows, BLOCK), 1)
    scales = scales_ref[...]
    for block in range(columns // BLOCK):
        at = slice(block * BLOCK, (block + 1) * BLOCK)
        place = lax.axis_index("sub") * half + begin + block * BLOCK
        flips = flips_ref[:, pl.ds(pl.multiple_of(place, BLOCK), BLOCK)]
        total = (kept_ref[:, at] + came_ref[:, at].astype(jnp.float32)) * flips
        rotated = jnp.dot(
            total, rotation, precision=lax.Precision.HIGHEST, preferred_element_type=jnp.float32
        )
        largest = jnp.max(jnp.abs(rotated), axis=1, keepdims=True)
        scale = (largest + epsilon).astype(jnp.bfloat16).astype(jnp.float32)
        out_ref[:, at] = (rotated / scale).astype(jnp.bfloat16)
        scales = jnp.where(lanes == lane + block, scale, scales)
    if last:
        out_ref[:, columns:] = scales.astype(jnp.bfloat16)
    else:
        refs[-1][...] = scales


def encode(kept, came, begin, scales, lane, last, flips, rotation, tokens=()):
    rows, columns = kept.shape
    out_shape = [jax.ShapeDtypeStruct((rows, columns + (BLOCK if last else 0)), jnp.bfloat16)]
    if not last:
        out_shape.append(jax.ShapeDtypeStruct((rows, BLOCK), jnp.float32))
    return pl.pallas_call(
        functools.partial(encode_body, begin, lane, last),
        out_shape=out_shape,
        in_specs=[VMEM] * 5 + [ANY] * len(tokens),
        out_specs=[VMEM] * len(out_shape),
        compiler_params=PARAMS,
        cost_estimate=SMALL,
    )(kept, came, scales, flips, rotation, *tokens)


def rank_of(index, count):
    levels = count.bit_length() - 1
    return sum((index >> level & 1) << (levels - 1 - level) for level in range(levels))


def block_of(other, place, places, blocks):
    sub = lax.axis_index("sub")
    sub = 1 - sub if other else sub
    return lax.rem(lax.axis_index("seq") - (sub * places + place) + blocks, blocks)


def choose_body(blocks, count, width, begins, other, places, scales, lane, *refs):
    out_ref = refs[-1]
    rows = refs[0].shape[0]

    def put(block, place):
        for piece in range(count):
            row = (place * count + rank_of(lax.axis_index("tensor") ^ piece, count)) * rows
            here = pl.ds(pl.multiple_of(row, rows), rows)
            begin = begins[block]
            out_ref[here, :width] = refs[block * count + piece][:, begin : begin + width]
            ref = refs[(blocks - 1) * count + piece]
            at = ref.shape[1] - BLOCK + block * scales + lane
            out_ref[here, width : width + width // BLOCK] = ref[:, at : at + width // BLOCK]

    for place in range(places):
        for block in range(blocks):
            pl.when(block_of(other, place, places, blocks) == block)(functools.partial(put, block, place))


def choose(results, group, width, other, places, scales):
    picked = [result[0] if len(result) == 1 else result[group] for result in results]
    begins = [group * width if len(result) == 1 else 0 for result in results]
    lane = group * (width // BLOCK)
    rows, count = picked[0][0].shape[0], len(picked[0])
    columns = width + BLOCK
    if rows % 16:
        blocks = []
        for block, (pieces, begin) in enumerate(zip(picked, begins)):
            held = jnp.zeros((count * rows, columns), jnp.bfloat16)
            for index, piece in enumerate(pieces):
                part = piece[:, begin : begin + width]
                at = picked[-1][index].shape[1] - BLOCK + block * scales + lane
                scale = picked[-1][index][:, at : at + width // BLOCK]
                part = jnp.concatenate([part, jnp.pad(scale, ((0, 0), (0, BLOCK - width // BLOCK)))], axis=1)
                row = rank_of(lax.axis_index("tensor") ^ index, count) * rows
                held = lax.dynamic_update_slice_in_dim(held, part, row, 0)
            blocks.append(held)
        stacked = jnp.stack(blocks)
        return jnp.concatenate([stacked[block_of(other, place, places, len(blocks))] for place in range(places)])
    operands = [piece for pieces in picked for piece in pieces]
    return pl.pallas_call(
        functools.partial(choose_body, len(picked), count, width, begins, other, places, scales, lane),
        out_shape=jax.ShapeDtypeStruct((places * count * rows, columns), jnp.bfloat16),
        in_specs=[VMEM] * len(operands),
        out_specs=VMEM,
        compiler_params=PARAMS,
        cost_estimate=SMALL,
    )(*operands)


def place_body(mine, half, width, count, held, *refs):
    refs = refs[held:]
    scaled = len(refs) > count + 2
    codes_ref, sems = refs[-3 if scaled else -2], refs[-1]
    sub = lax.axis_index("sub")
    side = sub if mine else 1 - sub

    def copies(core):
        return [
            pltpu.make_async_copy(
                refs[group].at[:, :width], codes_ref.at[:, pl.ds(core * half + group * width, width)], sems.at[group]
            )
            for group in range(count)
        ]

    def put(core):
        for copy in copies(core):
            copy.start()
        if scaled:
            order = refs[count : 2 * count] + refs[:count] if core else refs[: 2 * count]
            scales = [ref[:, width : width + width // BLOCK].astype(jnp.float32) for ref in order]
            refs[-2][...] = jnp.concatenate(scales, axis=1).T.astype(jnp.bfloat16)
        for copy in copies(core):
            copy.wait()

    for core in range(2):
        pl.when(side == core)(functools.partial(put, core))


def put_codes(arrays, width, half, mine, codes=None, mine_too=()):
    rows = arrays[0].shape[0]
    operands = list(arrays) + list(mine_too)
    out_shape = [jax.ShapeDtypeStruct((rows, 2 * half), jnp.bfloat16)]
    out_specs = [HBM]
    if mine_too:
        out_shape.append(jax.ShapeDtypeStruct((2 * half // BLOCK, rows), jnp.bfloat16))
        out_specs.append(VMEM)
    held = [] if codes is None else [codes]
    return pl.pallas_call(
        functools.partial(place_body, mine, half, width, len(arrays), len(held)),
        out_shape=out_shape,
        in_specs=[HBM] * len(held) + [VMEM] * len(operands),
        out_specs=out_specs,
        input_output_aliases={0: 0} if held else {},
        scratch_shapes=[pltpu.SemaphoreType.DMA((len(arrays),))],
        compiler_params=PARAMS,
        cost_estimate=SMALL,
    )(*held, *operands)


def cut(depth):
    if depth % UNIT or depth < 8 * UNIT:
        return [depth]
    units = depth // UNIT
    sizes = [max(1, units * share // 13) for share in SHARES]
    return [size * UNIT for size in sizes + [units - sum(sizes)]]


def shards(hidden, down_weight, sign_bits):
    tensor_count = lax.axis_size("tensor")
    seq_count = lax.axis_size("seq")
    sub_count = lax.axis_size("sub")
    depth = hidden.shape[1]
    half = down_weight.shape[1] // sub_count
    per_sub = seq_count // sub_count
    levels = tensor_count.bit_length() - 1
    wide, wide_chunk = min(256, half // GROUPS), min(512, half // GROUPS)
    flips = (2 * sign_bits - 1).astype(jnp.float32)[None, :]
    rotation = jnp.asarray(hadamard(BLOCK))

    def swap(values):
        return lax.ppermute(values, "sub", [(0, 1), (1, 0)])

    def exchange(values, level):
        return lax.ppermute(values, "tensor", [(t, t ^ 1 << level) for t in range(tensor_count)])

    def reduce(halves, begin, block, base, last):
        tokens = (yield None) or []
        kept, came = halves[1::2], [swap(sent) for sent in halves[::2]]
        for level in range(levels):
            sent, held = halve(kept, came, level, tokens)
            tokens = (yield sent) or []
            kept, came = [held], [exchange(sent, level)]
        packed, *base[:] = encode(
            kept[0], came[0], begin, base[0], (block * half + begin) // BLOCK, last, flips, rotation, tokens
        )
        yield packed

    def spread(packed):
        pieces = {0: packed}
        for level in reversed(range(levels)):
            for index in list(pieces):
                pieces[index ^ 1 << level] = exchange(pieces[index], level)
        return [pieces[index] for index in range(tensor_count)]

    zeros = jnp.zeros((hidden.shape[0] // tensor_count, BLOCK), jnp.float32)
    sizes = cut(depth)
    places = [sum(sizes[:index]) for index in range(len(sizes))]
    parts = slices_of(hidden, list(zip(places, sizes)))
    arrivals = []
    for shift in range(1, seq_count):
        pairs = [(s, (s + shift) % seq_count) for s in range(seq_count)]
        arrivals.append([lax.ppermute(part, "seq", pairs) for part in parts])

    if len(sizes) == 1:
        outs = multiply([[parts[0]], [arrivals[0][0]]], down_weight, 0, [None, None], [True, True], wide_chunk)
        base = [zeros]
        reduced = [list(reduce(outs[:2], 0, 0, base, False))[-1], list(reduce(outs[2:], 0, 1, base, seq_count == 2))[-1]]
        for block, arrived in enumerate(arrivals[1:], 2):
            outs = multiply([[arrived[0]]], down_weight, 0, [None], [True], wide_chunk)
            reduced.append(list(reduce(outs, 0, block, base, block == seq_count - 1))[-1])
        results = [[spread(packed)] for packed in reduced]
    else:
        (own,) = multiply([parts[1:]], down_weight, sizes[0], [None], [False], wide, tokens=parts[:1])
        *halves, total = multiply(
            [[parts[0]], [arrivals[0][0]]], down_weight, 0, [own, None], [True, False], wide_chunk, groups=GROUPS
        )
        own_base = [zeros]
        own_steps = reduce(halves, 0, 0, own_base, False)
        next(own_steps)
        tokens = [own_steps.send([arrivals[0][1]])]
        results = []
        for shift, arrived in enumerate(arrivals):
            if shift:
                (total,) = multiply([[arrived[0]]], down_weight, 0, [None], [False], wide_chunk)
            for index in range(1, len(sizes) - 1):
                (total,) = multiply(
                    [[arrived[index]]], down_weight, places[index], [total], [False], wide_chunk, tokens=tokens
                )
                if not results:
                    step = own_steps.send([total])
                    tokens = [step]
                    if own_base[0] is not zeros:
                        results.append([spread(step)])
            if not results:
                results.append([spread(list(own_steps)[-1])])
            if shift == 0:
                bases = [list(own_base) for _ in range(GROUPS)]
            remote, all_steps = [], []
            for group in range(GROUPS):
                sent, kept = multiply(
                    [[arrived[-1]]], down_weight, places[-1], [total], [True], wide_chunk,
                    groups=GROUPS, only=group, tokens=tokens,
                )
                tokens = [sent]
                if group == GROUPS - 1 and shift == 0 and levels > 1:
                    sent = gate(sent, [results[0][0][1], results[0][0][1 << levels - 1]])
                all_steps.append(reduce([sent, kept], group * half // GROUPS, shift + 1, bases[group], shift == seq_count - 2))
                next(all_steps[-1])
            last = []
            for level in range(levels + 1):
                for group, steps in enumerate(all_steps):
                    wait = list(last) if group == 0 else []
                    if group == GROUPS - 1 and level == levels and shift == 0:
                        wait += results[0][0][1:]
                    step = steps.send(wait)
                    if level == levels:
                        remote.append(spread(step))
                last = [step]
            results.append(remote)
            tokens = []

    groups = max(len(result) for result in results)
    width = half // groups

    def chosen(other):
        return [choose(results, group, width, other, per_sub, half // BLOCK) for group in range(groups)]

    came = [swap(values) for values in chosen(True)]
    mine = chosen(False)
    (codes,) = put_codes(mine, width, half, True)
    codes, flat = put_codes(came, width, half, False, codes, mine)
    return codes, flat.T


def solution(mesh):
    return jax.shard_map(
        shards,
        mesh=mesh,
        in_specs=(P(("groups", "seq"), ("tensor", "sub")), P(("tensor", "sub"), "seq"), P("seq")),
        out_specs=(P(("groups", "sub"), "seq"), P(("groups", "sub"), "seq")),
        check_vma=False,
    )
```

```python
import functools
import math

import jax
import jax.numpy as jnp
import numpy as np
from jax import lax
from jax.experimental import pallas as pl
from jax.experimental.pallas import tpu as pltpu
from jax.sharding import PartitionSpec as P

BLOCK = 128
UNIT = 512
GROUPS = 2
VMEM_LIMIT = 6 * 2**20
SLICE_LIMIT = 61 * 2**20 + 2**19
SHARES = (4, 4, 3)
epsilon = 1e-06

SMALL = pl.CostEstimate(flops=1, bytes_accessed=1, transcendentals=0)
PARAMS = pltpu.CompilerParams(vmem_limit_bytes=VMEM_LIMIT)
VMEM = pl.BlockSpec(memory_space=pltpu.VMEM)
ANY = pl.BlockSpec(memory_space=pl.ANY)
HBM = pl.BlockSpec(memory_space=pltpu.HBM)


def hadamard(order):
    indices = np.arange(order)
    parity = np.zeros((order, order), np.int64)
    for position in range(order.bit_length() - 1):
        parity = parity + (indices[:, None] >> position & 1) * (indices[None, :] >> position & 1)
    return ((1 - 2 * (parity % 2)) / math.sqrt(order)).astype(np.float32)


def slice_body(places, in_ref, *refs):
    out_refs, arrived = refs[:-1], refs[-1]
    copies = [
        pltpu.make_async_copy(in_ref.at[:, at : at + size], out_ref, arrived.at[index])
        for index, ((at, size), out_ref) in enumerate(zip(places, out_refs))
    ]
    for copy in copies:
        copy.start()
    for copy in copies:
        copy.wait()


def slices_of(values, places):
    return pl.pallas_call(
        functools.partial(slice_body, places),
        out_shape=[jax.ShapeDtypeStruct((values.shape[0], size), values.dtype) for _, size in places],
        in_specs=[HBM],
        out_specs=[VMEM] * len(places),
        scratch_shapes=[pltpu.SemaphoreType.DMA((len(places),))],
        compiler_params=pltpu.CompilerParams(vmem_limit_bytes=SLICE_LIMIT),
        cost_estimate=SMALL,
    )(values)


def multiply_body(spans, has_totals, splits, row, groups, only, *refs):
    lefts = [refs[begin:end] for begin, end in spans]
    refs = refs[spans[-1][1] :]
    w_ref, refs = refs[0], refs[1:]
    total_refs, refs = list(refs[: sum(has_totals)]), refs[sum(has_totals) :]
    buffer, arrived = refs[-2:]
    outs_of_split = 2 if only is not None else 2 * groups
    out_count = sum(outs_of_split if split else 1 for split in splits)
    out_refs = refs[-2 - out_count : -2]
    steps, depth, wide = buffer.shape
    rows = lefts[0][0].shape[0]
    in_half = w_ref.shape[1] // wide // 2
    first = in_half // groups
    here = lax.axis_index("sub")

    def column(n):
        if not any(splits):
            return n
        group, place = n // (2 * first), n % (2 * first)
        group = group if only is None else only
        side, place = (here, place - first) if place >= first else (1 - here, place)
        return side * in_half + group * first + place

    def at(block):
        return pl.ds(pl.multiple_of(block * wide, wide), wide)

    def copy(n):
        return pltpu.make_async_copy(w_ref.at[pl.ds(row, depth), at(column(n))], buffer.at[n], arrived.at[n])

    def step(n):
        copy(n).wait()
        product, begin = None, 0
        for index in range(len(lefts[0])):
            parts = [left[index][...] for left in lefts]
            left = parts[0] if len(parts) == 1 else jnp.concatenate(parts, axis=0)
            end = begin + left.shape[1]
            part = jnp.dot(left, buffer[n, begin:end], preferred_element_type=jnp.float32)
            product = part if product is None else product + part
            begin = end
        totals, outs = list(total_refs), list(out_refs)
        for index in range(len(lefts)):
            value = product[index * rows : (index + 1) * rows]
            if has_totals[index]:
                value = value + totals.pop(0)[:, at(column(n))]
            if splits[index]:
                group, place = n // (2 * first), n % (2 * first)
                out_ref = outs[2 * group + place // first]
                begin = place % first * wide
                out_ref[:, begin : begin + wide] = value.astype(out_ref.dtype)
                outs = outs[outs_of_split:]
            else:
                outs.pop(0)[:, at(column(n))] = value

    for n in range(steps):
        copy(n).start()
    if any(splits):
        for n in range(steps):
            step(n)
    else:
        pl.loop(0, steps)(step)


def multiply(lefts, weight, row, totals, splits, wide, groups=1, only=None, tokens=()):
    rows = lefts[0][0].shape[0]
    depth = sum(part.shape[1] for part in lefts[0])
    columns = weight.shape[1]
    steps = columns // wide // (1 if only is None else groups)
    spans = [(index * len(left), (index + 1) * len(left)) for index, left in enumerate(lefts)]
    held = [total for total in totals if total is not None]
    out_shape = []
    for split in splits:
        if split:
            out_shape += [
                jax.ShapeDtypeStruct((rows, columns // 2 // groups), jnp.bfloat16),
                jax.ShapeDtypeStruct((rows, columns // 2 // groups), jnp.float32),
            ] * (groups if only is None else 1)
        else:
            out_shape.append(jax.ShapeDtypeStruct((rows, columns), jnp.float32))
    body = functools.partial(
        multiply_body, spans, [total is not None for total in totals], splits, row, groups, only
    )
    return pl.pallas_call(
        body,
        out_shape=out_shape,
        in_specs=[VMEM] * spans[-1][1] + [HBM] + [VMEM] * len(held) + [ANY] * len(tokens),
        out_specs=[VMEM] * len(out_shape),
        scratch_shapes=[
            pltpu.VMEM((steps, depth, wide), weight.dtype),
            pltpu.SemaphoreType.DMA((steps,)),
        ],
        compiler_params=pltpu.CompilerParams(
            vmem_limit_bytes=2 * steps * depth * wide + VMEM_LIMIT
        ),
        cost_estimate=SMALL,
    )(*[part for left in lefts for part in left], weight, *held, *tokens)


def gate(values, tokens):
    return pl.pallas_call(
        lambda *refs: None,
        out_shape=jax.ShapeDtypeStruct(values.shape, values.dtype),
        in_specs=[ANY] * (1 + len(tokens)),
        out_specs=ANY,
        input_output_aliases={0: 0},
        compiler_params=PARAMS,
        cost_estimate=SMALL,
    )(values, *tokens)


def halve_body(level, count, *refs):
    kept_refs, came_refs, (sent_out, kept_out) = refs[:count], refs[count : 2 * count], refs[-2:]
    half, columns = sent_out.shape
    width = columns // count

    def put(bit):
        mine, other = slice(bit * half, (bit + 1) * half), slice((1 - bit) * half, (2 - bit) * half)
        for index, (kept_ref, came_ref) in enumerate(zip(kept_refs, came_refs)):
            at = slice(index * width, (index + 1) * width)
            kept_out[:, at] = kept_ref[mine] + came_ref[mine].astype(jnp.float32)
            sent_out[:, at] = (kept_ref[other] + came_ref[other].astype(jnp.float32)).astype(jnp.bfloat16)

    for bit in range(2):
        pl.when(lax.axis_index("tensor") >> level & 1 == bit)(functools.partial(put, bit))


def halve(kept, came, level, tokens=()):
    rows, columns = kept[0].shape
    half, columns = rows // 2, columns * len(kept)
    if half % 16:
        total = jnp.concatenate(kept, axis=1) + jnp.concatenate(came, axis=1).astype(jnp.float32)
        bit = lax.axis_index("tensor") >> level & 1
        sent = lax.dynamic_slice_in_dim(total, (1 - bit) * half, half, 0).astype(jnp.bfloat16)
        return sent, lax.dynamic_slice_in_dim(total, bit * half, half, 0)
    return pl.pallas_call(
        functools.partial(halve_body, level, len(kept)),
        out_shape=[
            jax.ShapeDtypeStruct((half, columns), jnp.bfloat16),
            jax.ShapeDtypeStruct((half, columns), jnp.float32),
        ],
        in_specs=[VMEM] * (2 * len(kept)) + [ANY] * len(tokens),
        out_specs=[VMEM, VMEM],
        compiler_params=PARAMS,
        cost_estimate=SMALL,
    )(*kept, *came, *tokens)


def encode_body(begin, lane, last, kept_ref, came_ref, scales_ref, flips_ref, rotation_ref, *refs):
    out_ref = refs[-1 if last else -2]
    rows, columns = kept_ref.shape
    half = flips_ref.shape[1] // 2
    blocks = columns // BLOCK
    lanes = lax.broadcasted_iota(jnp.int32, (rows, BLOCK), 1)
    scales = scales_ref[...]
    totals = []
    for block in range(blocks):
        at = slice(block * BLOCK, (block + 1) * BLOCK)
        place = lax.axis_index("sub") * half + begin + block * BLOCK
        flips = flips_ref[:, pl.ds(pl.multiple_of(place, BLOCK), BLOCK)]
        totals.append((kept_ref[:, at] + came_ref[:, at].astype(jnp.float32)) * flips)
    rotated = jnp.dot(
        jnp.concatenate(totals, axis=0),
        rotation_ref[...],
        precision=lax.Precision.HIGHEST,
        preferred_element_type=jnp.float32,
    )
    largest = jnp.max(jnp.abs(rotated), axis=1, keepdims=True)
    scale = (largest + epsilon).astype(jnp.bfloat16).astype(jnp.float32)
    codes = rotated / scale
    for block in range(blocks):
        part = slice(block * rows, (block + 1) * rows)
        out_ref[:, block * BLOCK : (block + 1) * BLOCK] = codes[part].astype(jnp.bfloat16)
        scales = jnp.where(lanes == lane + block, scale[part], scales)
    if last:
        out_ref[:, columns:] = scales.astype(jnp.bfloat16)
    else:
        refs[-1][...] = scales


def encode(kept, came, begin, scales, lane, last, flips, rotation, tokens=()):
    rows, columns = kept.shape
    out_shape = [jax.ShapeDtypeStruct((rows, columns + (BLOCK if last else 0)), jnp.bfloat16)]
    if not last:
        out_shape.append(jax.ShapeDtypeStruct((rows, BLOCK), jnp.float32))
    return pl.pallas_call(
        functools.partial(encode_body, begin, lane, last),
        out_shape=out_shape,
        in_specs=[VMEM] * 5 + [ANY] * len(tokens),
        out_specs=[VMEM] * len(out_shape),
        compiler_params=PARAMS,
        cost_estimate=SMALL,
    )(kept, came, scales, flips, rotation, *tokens)


def rank_of(index, count):
    levels = count.bit_length() - 1
    return sum((index >> level & 1) << (levels - 1 - level) for level in range(levels))


def block_of(other, place, places, blocks):
    sub = lax.axis_index("sub")
    sub = 1 - sub if other else sub
    return lax.rem(lax.axis_index("seq") - (sub * places + place) + blocks, blocks)


def choose_body(blocks, count, width, begins, other, places, scales, lane, *refs):
    out_ref = refs[-1]
    rows = refs[0].shape[0]

    def put(block, place):
        for piece in range(count):
            row = (place * count + rank_of(lax.axis_index("tensor") ^ piece, count)) * rows
            here = pl.ds(pl.multiple_of(row, rows), rows)
            begin = begins[block]
            out_ref[here, :width] = refs[block * count + piece][:, begin : begin + width]
            ref = refs[(blocks - 1) * count + piece]
            at = ref.shape[1] - BLOCK + block * scales + lane
            out_ref[here, width : width + width // BLOCK] = ref[:, at : at + width // BLOCK]

    for place in range(places):
        for block in range(blocks):
            pl.when(block_of(other, place, places, blocks) == block)(functools.partial(put, block, place))


def choose(results, group, width, other, places, scales):
    picked = [result[0] if len(result) == 1 else result[group] for result in results]
    begins = [group * width if len(result) == 1 else 0 for result in results]
    lane = group * (width // BLOCK)
    rows, count = picked[0][0].shape[0], len(picked[0])
    columns = width + BLOCK
    if rows % 16:
        blocks = []
        for block, (pieces, begin) in enumerate(zip(picked, begins)):
            held = jnp.zeros((count * rows, columns), jnp.bfloat16)
            for index, piece in enumerate(pieces):
                part = piece[:, begin : begin + width]
                at = picked[-1][index].shape[1] - BLOCK + block * scales + lane
                scale = picked[-1][index][:, at : at + width // BLOCK]
                part = jnp.concatenate([part, jnp.pad(scale, ((0, 0), (0, BLOCK - width // BLOCK)))], axis=1)
                row = rank_of(lax.axis_index("tensor") ^ index, count) * rows
                held = lax.dynamic_update_slice_in_dim(held, part, row, 0)
            blocks.append(held)
        stacked = jnp.stack(blocks)
        return jnp.concatenate([stacked[block_of(other, place, places, len(blocks))] for place in range(places)])
    operands = [piece for pieces in picked for piece in pieces]
    return pl.pallas_call(
        functools.partial(choose_body, len(picked), count, width, begins, other, places, scales, lane),
        out_shape=jax.ShapeDtypeStruct((places * count * rows, columns), jnp.bfloat16),
        in_specs=[VMEM] * len(operands),
        out_specs=VMEM,
        compiler_params=PARAMS,
        cost_estimate=SMALL,
    )(*operands)


def place_body(mine, half, width, count, held, *refs):
    refs = refs[held:]
    scaled = len(refs) > count + 2
    codes_ref, sems = refs[-3 if scaled else -2], refs[-1]
    sub = lax.axis_index("sub")
    side = sub if mine else 1 - sub

    def copies(core):
        return [
            pltpu.make_async_copy(
                refs[group].at[:, :width], codes_ref.at[:, pl.ds(core * half + group * width, width)], sems.at[group]
            )
            for group in range(count)
        ]

    def put(core):
        for copy in copies(core):
            copy.start()
        if scaled:
            order = refs[count : 2 * count] + refs[:count] if core else refs[: 2 * count]
            scales = [ref[:, width : width + width // BLOCK].astype(jnp.float32) for ref in order]
            refs[-2][...] = jnp.concatenate(scales, axis=1).T.astype(jnp.bfloat16)
        for copy in copies(core):
            copy.wait()

    for core in range(2):
        pl.when(side == core)(functools.partial(put, core))


def put_codes(arrays, width, half, mine, codes=None, mine_too=()):
    rows = arrays[0].shape[0]
    operands = list(arrays) + list(mine_too)
    out_shape = [jax.ShapeDtypeStruct((rows, 2 * half), jnp.bfloat16)]
    out_specs = [HBM]
    if mine_too:
        out_shape.append(jax.ShapeDtypeStruct((2 * half // BLOCK, rows), jnp.bfloat16))
        out_specs.append(VMEM)
    held = [] if codes is None else [codes]
    return pl.pallas_call(
        functools.partial(place_body, mine, half, width, len(arrays), len(held)),
        out_shape=out_shape,
        in_specs=[HBM] * len(held) + [VMEM] * len(operands),
        out_specs=out_specs,
        input_output_aliases={0: 0} if held else {},
        scratch_shapes=[pltpu.SemaphoreType.DMA((len(arrays),))],
        compiler_params=PARAMS,
        cost_estimate=SMALL,
    )(*held, *operands)


def cut(depth):
    if depth % UNIT or depth < 8 * UNIT:
        return [depth]
    units = depth // UNIT
    sizes = [max(1, units * share // 13) for share in SHARES]
    return [size * UNIT for size in sizes + [units - sum(sizes)]]


def shards(hidden, down_weight, sign_bits):
    tensor_count = lax.axis_size("tensor")
    seq_count = lax.axis_size("seq")
    sub_count = lax.axis_size("sub")
    depth = hidden.shape[1]
    half = down_weight.shape[1] // sub_count
    per_sub = seq_count // sub_count
    levels = tensor_count.bit_length() - 1
    wide, wide_chunk, wide_merged = (min(size, half // GROUPS) for size in (256, 512, 1024))
    flips = (2 * sign_bits - 1).astype(jnp.float32)[None, :]
    rotation = jnp.asarray(hadamard(BLOCK))

    def swap(values):
        return lax.ppermute(values, "sub", [(0, 1), (1, 0)])

    def exchange(values, level):
        return lax.ppermute(values, "tensor", [(t, t ^ 1 << level) for t in range(tensor_count)])

    def reduce(halves, begin, block, base, last):
        tokens = (yield None) or []
        kept, came = halves[1::2], [swap(sent) for sent in halves[::2]]
        for level in range(levels):
            sent, held = halve(kept, came, level, tokens)
            tokens = (yield sent) or []
            kept, came = [held], [exchange(sent, level)]
        packed, *base[:] = encode(
            kept[0], came[0], begin, base[0], (block * half + begin) // BLOCK, last, flips, rotation, tokens
        )
        yield packed

    def spread(packed):
        pieces = {0: packed}
        for level in reversed(range(levels)):
            for index in list(pieces):
                pieces[index ^ 1 << level] = exchange(pieces[index], level)
        return [pieces[index] for index in range(tensor_count)]

    zeros = jnp.zeros((hidden.shape[0] // tensor_count, BLOCK), jnp.float32)
    sizes = cut(depth)
    places = [sum(sizes[:index]) for index in range(len(sizes))]
    parts = slices_of(hidden, list(zip(places, sizes)))
    arrivals = []
    for shift in range(1, seq_count):
        pairs = [(s, (s + shift) % seq_count) for s in range(seq_count)]
        arrivals.append([lax.ppermute(part, "seq", pairs) for part in parts])

    if len(sizes) == 1:
        outs = multiply([[parts[0]], [arrivals[0][0]]], down_weight, 0, [None, None], [True, True], wide_chunk)
        base = [zeros]
        reduced = [list(reduce(outs[:2], 0, 0, base, False))[-1], list(reduce(outs[2:], 0, 1, base, seq_count == 2))[-1]]
        for block, arrived in enumerate(arrivals[1:], 2):
            outs = multiply([[arrived[0]]], down_weight, 0, [None], [True], wide_chunk)
            reduced.append(list(reduce(outs, 0, block, base, block == seq_count - 1))[-1])
        results = [[spread(packed)] for packed in reduced]
    else:
        (own,) = multiply([parts[1:]], down_weight, sizes[0], [None], [False], wide, tokens=parts[:1])
        *halves, total = multiply(
            [[parts[0]], [arrivals[0][0]]], down_weight, 0, [own, None], [True, False], wide_merged, groups=GROUPS
        )
        own_base = [zeros]
        own_steps = reduce(halves, 0, 0, own_base, False)
        next(own_steps)
        tokens = [own_steps.send([arrivals[0][1]])]
        results = []
        for shift, arrived in enumerate(arrivals):
            if shift:
                (total,) = multiply([[arrived[0]]], down_weight, 0, [None], [False], wide_chunk)
            for index in range(1, len(sizes) - 1):
                (total,) = multiply(
                    [[arrived[index]]], down_weight, places[index], [total], [False], wide_chunk, tokens=tokens
                )
                if not results:
                    step = own_steps.send([total])
                    tokens = [step]
                    if own_base[0] is not zeros:
                        results.append([spread(step)])
            if not results:
                results.append([spread(list(own_steps)[-1])])
            if shift == 0:
                bases = [list(own_base) for _ in range(GROUPS)]
            remote, all_steps = [], []
            for group in range(GROUPS):
                sent, kept = multiply(
                    [[arrived[-1]]], down_weight, places[-1], [total], [True], wide_chunk,
                    groups=GROUPS, only=group, tokens=tokens,
                )
                tokens = [sent]
                if group == GROUPS - 1 and shift == 0 and levels > 1:
                    sent = gate(sent, [results[0][0][1], results[0][0][1 << levels - 1]])
                all_steps.append(reduce([sent, kept], group * half // GROUPS, shift + 1, bases[group], shift == seq_count - 2))
                next(all_steps[-1])
            last = []
            for level in range(levels + 1):
                for group, steps in enumerate(all_steps):
                    wait = list(last) if group == 0 else []
                    if group == GROUPS - 1 and level == levels and shift == 0:
                        wait += results[0][0][1:]
                    step = steps.send(wait)
                    if level == levels:
                        remote.append(spread(step))
                last = [step]
            results.append(remote)
            tokens = []

    groups = max(len(result) for result in results)
    width = half // groups

    def chosen(other):
        return [choose(results, group, width, other, per_sub, half // BLOCK) for group in range(groups)]

    came = [swap(values) for values in chosen(True)]
    mine = chosen(False)
    (codes,) = put_codes(mine, width, half, True)
    codes, flat = put_codes(came, width, half, False, codes, mine)
    return codes, flat.T


def solution(mesh):
    return jax.shard_map(
        shards,
        mesh=mesh,
        in_specs=(P(("groups", "seq"), ("tensor", "sub")), P(("tensor", "sub"), "seq"), P("seq")),
        out_specs=(P(("groups", "sub"), "seq"), P(("groups", "sub"), "seq")),
        check_vma=False,
    )
```

```python
import functools
import math

import jax
import jax.numpy as jnp
import numpy as np
from jax import lax
from jax.experimental import pallas as pl
from jax.experimental.pallas import tpu as pltpu
from jax.sharding import PartitionSpec as P

BLOCK = 128
UNIT = 256
GROUPS = 2
VMEM_LIMIT = 6 * 2**20
SHARES = (8, 7, 6)
epsilon = 1e-06

SMALL = pl.CostEstimate(flops=1, bytes_accessed=1, transcendentals=0)
PARAMS = pltpu.CompilerParams(vmem_limit_bytes=VMEM_LIMIT)
VMEM = pl.BlockSpec(memory_space=pltpu.VMEM)
ANY = pl.BlockSpec(memory_space=pl.ANY)
HBM = pl.BlockSpec(memory_space=pltpu.HBM)


def hadamard(order):
    indices = np.arange(order)
    parity = np.zeros((order, order), np.int64)
    for position in range(order.bit_length() - 1):
        parity = parity + (indices[:, None] >> position & 1) * (indices[None, :] >> position & 1)
    return ((1 - 2 * (parity % 2)) / math.sqrt(order)).astype(np.float32)


def slice_body(places, in_ref, *refs):
    out_refs, arrived = refs[:-1], refs[-1]
    copies = [
        pltpu.make_async_copy(in_ref.at[:, at : at + size], out_ref, arrived.at[index])
        for index, ((at, size), out_ref) in enumerate(zip(places, out_refs))
    ]
    for copy in copies:
        copy.start()
    for copy in copies:
        copy.wait()


def slices_of(values, places):
    return pl.pallas_call(
        functools.partial(slice_body, places),
        out_shape=[jax.ShapeDtypeStruct((values.shape[0], size), values.dtype) for _, size in places],
        in_specs=[HBM],
        out_specs=[VMEM] * len(places),
        scratch_shapes=[pltpu.SemaphoreType.DMA((len(places),))],
        compiler_params=PARAMS,
        cost_estimate=SMALL,
    )(values)


def multiply_body(spans, has_totals, splits, row, groups, only, *refs):
    lefts = [refs[begin:end] for begin, end in spans]
    refs = refs[spans[-1][1] :]
    w_ref, refs = refs[0], refs[1:]
    total_refs, refs = list(refs[: sum(has_totals)]), refs[sum(has_totals) :]
    buffer, arrived = refs[-2:]
    outs_of_split = 2 if only is not None else 2 * groups
    out_count = sum(outs_of_split if split else 1 for split in splits)
    out_refs = refs[-2 - out_count : -2]
    steps, depth, wide = buffer.shape
    rows = lefts[0][0].shape[0]
    in_half = w_ref.shape[1] // wide // 2
    first = in_half // groups
    here = lax.axis_index("sub")

    def column(n):
        if not any(splits):
            return n
        group, place = n // (2 * first), n % (2 * first)
        group = group if only is None else only
        side, place = (here, place - first) if place >= first else (1 - here, place)
        return side * in_half + group * first + place

    def at(block):
        return pl.ds(pl.multiple_of(block * wide, wide), wide)

    def copy(n):
        return pltpu.make_async_copy(w_ref.at[pl.ds(row, depth), at(column(n))], buffer.at[n], arrived.at[n])

    def step(n):
        copy(n).wait()
        product, begin = None, 0
        for index in range(len(lefts[0])):
            parts = [left[index][...] for left in lefts]
            left = parts[0] if len(parts) == 1 else jnp.concatenate(parts, axis=0)
            end = begin + left.shape[1]
            part = jnp.dot(left, buffer[n, begin:end], preferred_element_type=jnp.float32)
            product = part if product is None else product + part
            begin = end
        totals, outs = list(total_refs), list(out_refs)
        for index in range(len(lefts)):
            value = product[index * rows : (index + 1) * rows]
            if has_totals[index]:
                value = value + totals.pop(0)[:, at(column(n))]
            if splits[index]:
                group, place = n // (2 * first), n % (2 * first)
                out_ref = outs[2 * group + place // first]
                begin = place % first * wide
                out_ref[:, begin : begin + wide] = value.astype(out_ref.dtype)
                outs = outs[outs_of_split:]
            else:
                outs.pop(0)[:, at(column(n))] = value

    for n in range(steps):
        copy(n).start()
    if any(splits):
        for n in range(steps):
            step(n)
    else:
        pl.loop(0, steps)(step)


def multiply(lefts, weight, row, totals, splits, wide, groups=1, only=None, tokens=()):
    rows = lefts[0][0].shape[0]
    depth = sum(part.shape[1] for part in lefts[0])
    columns = weight.shape[1]
    steps = columns // wide // (1 if only is None else groups)
    spans = [(index * len(left), (index + 1) * len(left)) for index, left in enumerate(lefts)]
    held = [total for total in totals if total is not None]
    out_shape = []
    for split in splits:
        if split:
            out_shape += [
                jax.ShapeDtypeStruct((rows, columns // 2 // groups), jnp.bfloat16),
                jax.ShapeDtypeStruct((rows, columns // 2 // groups), jnp.float32),
            ] * (groups if only is None else 1)
        else:
            out_shape.append(jax.ShapeDtypeStruct((rows, columns), jnp.float32))
    body = functools.partial(
        multiply_body, spans, [total is not None for total in totals], splits, row, groups, only
    )
    return pl.pallas_call(
        body,
        out_shape=out_shape,
        in_specs=[VMEM] * spans[-1][1] + [HBM] + [VMEM] * len(held) + [ANY] * len(tokens),
        out_specs=[VMEM] * len(out_shape),
        scratch_shapes=[
            pltpu.VMEM((steps, depth, wide), weight.dtype),
            pltpu.SemaphoreType.DMA((steps,)),
        ],
        compiler_params=pltpu.CompilerParams(
            vmem_limit_bytes=2 * steps * depth * wide + VMEM_LIMIT
        ),
        cost_estimate=SMALL,
    )(*[part for left in lefts for part in left], weight, *held, *tokens)


def gate(values, tokens):
    return pl.pallas_call(
        lambda *refs: None,
        out_shape=jax.ShapeDtypeStruct(values.shape, values.dtype),
        in_specs=[ANY] * (1 + len(tokens)),
        out_specs=ANY,
        input_output_aliases={0: 0},
        compiler_params=PARAMS,
        cost_estimate=SMALL,
    )(values, *tokens)


def halve_body(level, count, *refs):
    kept_refs, came_refs, (sent_out, kept_out) = refs[:count], refs[count : 2 * count], refs[-2:]
    half, columns = sent_out.shape
    width = columns // count

    def put(bit):
        mine, other = slice(bit * half, (bit + 1) * half), slice((1 - bit) * half, (2 - bit) * half)
        for index, (kept_ref, came_ref) in enumerate(zip(kept_refs, came_refs)):
            at = slice(index * width, (index + 1) * width)
            kept_out[:, at] = kept_ref[mine] + came_ref[mine].astype(jnp.float32)
            sent_out[:, at] = (kept_ref[other] + came_ref[other].astype(jnp.float32)).astype(jnp.bfloat16)

    for bit in range(2):
        pl.when(lax.axis_index("tensor") >> level & 1 == bit)(functools.partial(put, bit))


def halve(kept, came, level, tokens=()):
    rows, columns = kept[0].shape
    half, columns = rows // 2, columns * len(kept)
    if half % 16:
        total = jnp.concatenate(kept, axis=1) + jnp.concatenate(came, axis=1).astype(jnp.float32)
        bit = lax.axis_index("tensor") >> level & 1
        sent = lax.dynamic_slice_in_dim(total, (1 - bit) * half, half, 0).astype(jnp.bfloat16)
        return sent, lax.dynamic_slice_in_dim(total, bit * half, half, 0)
    return pl.pallas_call(
        functools.partial(halve_body, level, len(kept)),
        out_shape=[
            jax.ShapeDtypeStruct((half, columns), jnp.bfloat16),
            jax.ShapeDtypeStruct((half, columns), jnp.float32),
        ],
        in_specs=[VMEM] * (2 * len(kept)) + [ANY] * len(tokens),
        out_specs=[VMEM, VMEM],
        compiler_params=PARAMS,
        cost_estimate=SMALL,
    )(*kept, *came, *tokens)


def encode_body(begin, lane, last, kept_ref, came_ref, scales_ref, flips_ref, rotation_ref, *refs):
    out_ref = refs[-1 if last else -2]
    rows, columns = kept_ref.shape
    half = flips_ref.shape[1] // 2
    blocks = columns // BLOCK
    lanes = lax.broadcasted_iota(jnp.int32, (rows, BLOCK), 1)
    scales = scales_ref[...]
    totals = []
    for block in range(blocks):
        at = slice(block * BLOCK, (block + 1) * BLOCK)
        place = lax.axis_index("sub") * half + begin + block * BLOCK
        flips = flips_ref[:, pl.ds(pl.multiple_of(place, BLOCK), BLOCK)]
        totals.append((kept_ref[:, at] + came_ref[:, at].astype(jnp.float32)) * flips)
    rotated = jnp.dot(
        jnp.concatenate(totals, axis=0),
        rotation_ref[...],
        precision=lax.Precision.HIGHEST,
        preferred_element_type=jnp.float32,
    )
    largest = jnp.max(jnp.abs(rotated), axis=1, keepdims=True)
    scale = (largest + epsilon).astype(jnp.bfloat16).astype(jnp.float32)
    codes = rotated / scale
    for block in range(blocks):
        part = slice(block * rows, (block + 1) * rows)
        out_ref[:, block * BLOCK : (block + 1) * BLOCK] = codes[part].astype(jnp.bfloat16)
        scales = jnp.where(lanes == lane + block, scale[part], scales)
    if last:
        out_ref[:, columns:] = scales.astype(jnp.bfloat16)
    else:
        refs[-1][...] = scales


def encode(kept, came, begin, scales, lane, last, flips, rotation, tokens=()):
    rows, columns = kept.shape
    out_shape = [jax.ShapeDtypeStruct((rows, columns + (BLOCK if last else 0)), jnp.bfloat16)]
    if not last:
        out_shape.append(jax.ShapeDtypeStruct((rows, BLOCK), jnp.float32))
    return pl.pallas_call(
        functools.partial(encode_body, begin, lane, last),
        out_shape=out_shape,
        in_specs=[VMEM] * 5 + [ANY] * len(tokens),
        out_specs=[VMEM] * len(out_shape),
        compiler_params=PARAMS,
        cost_estimate=SMALL,
    )(kept, came, scales, flips, rotation, *tokens)


def rank_of(index, count):
    levels = count.bit_length() - 1
    return sum((index >> level & 1) << (levels - 1 - level) for level in range(levels))


def block_of(other, place, places, blocks):
    sub = lax.axis_index("sub")
    sub = 1 - sub if other else sub
    return lax.rem(lax.axis_index("seq") - (sub * places + place) + blocks, blocks)


def choose_body(blocks, count, width, begins, other, places, scales, lane, *refs):
    out_ref = refs[-1]
    rows = refs[0].shape[0]

    def put(block, place):
        for piece in range(count):
            row = (place * count + rank_of(lax.axis_index("tensor") ^ piece, count)) * rows
            here = pl.ds(pl.multiple_of(row, rows), rows)
            begin = begins[block]
            out_ref[here, :width] = refs[block * count + piece][:, begin : begin + width]
            ref = refs[(blocks - 1) * count + piece]
            at = ref.shape[1] - BLOCK + block * scales + lane
            out_ref[here, width : width + width // BLOCK] = ref[:, at : at + width // BLOCK]

    for place in range(places):
        for block in range(blocks):
            pl.when(block_of(other, place, places, blocks) == block)(functools.partial(put, block, place))


def choose(results, group, width, other, places, scales):
    picked = [result[0] if len(result) == 1 else result[group] for result in results]
    begins = [group * width if len(result) == 1 else 0 for result in results]
    lane = group * (width // BLOCK)
    rows, count = picked[0][0].shape[0], len(picked[0])
    columns = width + BLOCK
    if rows % 16:
        blocks = []
        for block, (pieces, begin) in enumerate(zip(picked, begins)):
            held = jnp.zeros((count * rows, columns), jnp.bfloat16)
            for index, piece in enumerate(pieces):
                part = piece[:, begin : begin + width]
                at = picked[-1][index].shape[1] - BLOCK + block * scales + lane
                scale = picked[-1][index][:, at : at + width // BLOCK]
                part = jnp.concatenate([part, jnp.pad(scale, ((0, 0), (0, BLOCK - width // BLOCK)))], axis=1)
                row = rank_of(lax.axis_index("tensor") ^ index, count) * rows
                held = lax.dynamic_update_slice_in_dim(held, part, row, 0)
            blocks.append(held)
        stacked = jnp.stack(blocks)
        return jnp.concatenate([stacked[block_of(other, place, places, len(blocks))] for place in range(places)])
    operands = [piece for pieces in picked for piece in pieces]
    return pl.pallas_call(
        functools.partial(choose_body, len(picked), count, width, begins, other, places, scales, lane),
        out_shape=jax.ShapeDtypeStruct((places * count * rows, columns), jnp.bfloat16),
        in_specs=[VMEM] * len(operands),
        out_specs=VMEM,
        compiler_params=PARAMS,
        cost_estimate=SMALL,
    )(*operands)


def place_body(mine, half, width, count, held, *refs):
    refs = refs[held:]
    scaled = len(refs) > count + 2
    codes_ref, sems = refs[2 * count if scaled else count], refs[-1]
    sub = lax.axis_index("sub")
    side = sub if mine else 1 - sub

    def put(core):
        copies = [
            pltpu.make_async_copy(
                refs[group].at[:, :width], codes_ref.at[:, pl.ds(core * half + group * width, width)], sems.at[group]
            )
            for group in range(count)
        ]
        for copy in copies:
            copy.start()
        if scaled:
            out_ref, flat = refs[2 * count + 1 : 2 * count + 3]
            order = refs[count : 2 * count] + refs[:count] if core else refs[: 2 * count]
            scales = [ref[:, width : width + width // BLOCK].astype(jnp.float32) for ref in order]
            flat[...] = jnp.concatenate(scales, axis=1).T.astype(jnp.bfloat16)
            copies.append(pltpu.make_async_copy(flat, out_ref, sems.at[count]))
            copies[-1].start()
        for copy in copies:
            copy.wait()

    for core in range(2):
        pl.when(side == core)(functools.partial(put, core))


def put_codes(arrays, width, half, mine, codes=None, mine_too=()):
    rows = arrays[0].shape[0]
    operands = list(arrays) + list(mine_too)
    out_shape = [jax.ShapeDtypeStruct((rows, 2 * half), jnp.bfloat16)]
    scratch = [pltpu.SemaphoreType.DMA((len(arrays) + 1,))]
    if mine_too:
        out_shape.append(jax.ShapeDtypeStruct((2 * half // BLOCK, rows), jnp.bfloat16))
        scratch.insert(0, pltpu.VMEM((2 * half // BLOCK, rows), jnp.bfloat16))
    held = [] if codes is None else [codes]
    return pl.pallas_call(
        functools.partial(place_body, mine, half, width, len(arrays), len(held)),
        out_shape=out_shape,
        in_specs=[HBM] * len(held) + [VMEM] * len(operands),
        out_specs=[HBM] * len(out_shape),
        input_output_aliases={0: 0} if held else {},
        scratch_shapes=scratch,
        compiler_params=PARAMS,
        cost_estimate=SMALL,
    )(*held, *operands)


def cut(depth):
    if depth % UNIT or depth < 16 * UNIT:
        return [depth]
    units = depth // UNIT
    sizes = [max(1, units * share // 26) for share in SHARES]
    return [size * UNIT for size in sizes + [units - sum(sizes)]]


def shards(hidden, down_weight, sign_bits):
    tensor_count = lax.axis_size("tensor")
    seq_count = lax.axis_size("seq")
    sub_count = lax.axis_size("sub")
    depth = hidden.shape[1]
    half = down_weight.shape[1] // sub_count
    per_sub = seq_count // sub_count
    levels = tensor_count.bit_length() - 1
    wide, wide_chunk, wide_merged = (min(size, half // GROUPS) for size in (256, 512, 1024))
    flips = (2 * sign_bits - 1).astype(jnp.float32)[None, :]
    rotation = jnp.asarray(hadamard(BLOCK))

    def swap(values):
        return lax.ppermute(values, "sub", [(0, 1), (1, 0)])

    def exchange(values, level):
        return lax.ppermute(values, "tensor", [(t, t ^ 1 << level) for t in range(tensor_count)])

    def reduce(halves, begin, block, base, last):
        tokens = (yield None) or []
        kept, came = halves[1::2], [swap(sent) for sent in halves[::2]]
        for level in range(levels):
            sent, held = halve(kept, came, level, tokens)
            tokens = (yield sent) or []
            kept, came = [held], [exchange(sent, level)]
        packed, *base[:] = encode(
            kept[0], came[0], begin, base[0], (block * half + begin) // BLOCK, last, flips, rotation, tokens
        )
        yield packed

    def spread(packed):
        pieces = {0: packed}
        for level in reversed(range(levels)):
            for index in list(pieces):
                pieces[index ^ 1 << level] = exchange(pieces[index], level)
        return [pieces[index] for index in range(tensor_count)]

    zeros = jnp.zeros((hidden.shape[0] // tensor_count, BLOCK), jnp.float32)
    sizes = cut(depth)
    places = [sum(sizes[:index]) for index in range(len(sizes))]
    parts = slices_of(hidden, list(zip(places, sizes)))
    arrivals = []
    for shift in range(1, seq_count):
        pairs = [(s, (s + shift) % seq_count) for s in range(seq_count)]
        arrivals.append([lax.ppermute(part, "seq", pairs) for part in parts])

    if len(sizes) == 1:
        outs = multiply([[parts[0]], [arrivals[0][0]]], down_weight, 0, [None, None], [True, True], wide_chunk)
        base = [zeros]
        reduced = [list(reduce(outs[:2], 0, 0, base, False))[-1], list(reduce(outs[2:], 0, 1, base, seq_count == 2))[-1]]
        for block, arrived in enumerate(arrivals[1:], 2):
            outs = multiply([[arrived[0]]], down_weight, 0, [None], [True], wide_chunk)
            reduced.append(list(reduce(outs, 0, block, base, block == seq_count - 1))[-1])
        results = [[spread(packed)] for packed in reduced]
    else:
        (own,) = multiply([parts[1:]], down_weight, sizes[0], [None], [False], wide, tokens=parts[:1])
        *halves, total = multiply(
            [[parts[0]], [arrivals[0][0]]], down_weight, 0, [own, None], [True, False], wide_merged, groups=GROUPS
        )
        own_base = [zeros]
        own_steps = reduce(halves, 0, 0, own_base, False)
        next(own_steps)
        tokens = [own_steps.send([arrivals[0][1]])]
        results = []
        for shift, arrived in enumerate(arrivals):
            if shift:
                (total,) = multiply([[arrived[0]]], down_weight, 0, [None], [False], wide_chunk)
            for index in range(1, len(sizes) - 1):
                (total,) = multiply(
                    [[arrived[index]]], down_weight, places[index], [total], [False], wide_chunk, tokens=tokens
                )
                if not results:
                    step = own_steps.send([total])
                    tokens = [step]
                    if own_base[0] is not zeros:
                        results.append([spread(step)])
            if not results:
                results.append([spread(list(own_steps)[-1])])
            if shift == 0:
                bases = [list(own_base) for _ in range(GROUPS)]
            remote, all_steps = [], []
            for group in range(GROUPS):
                sent, kept = multiply(
                    [[arrived[-1]]], down_weight, places[-1], [total], [True], wide_chunk,
                    groups=GROUPS, only=group, tokens=tokens,
                )
                tokens = [sent]
                if group == GROUPS - 1 and shift == 0 and levels > 1:
                    sent = gate(sent, [results[0][0][1], results[0][0][1 << levels - 1]])
                all_steps.append(reduce([sent, kept], group * half // GROUPS, shift + 1, bases[group], shift == seq_count - 2))
                next(all_steps[-1])
            last = []
            for level in range(levels + 1):
                for group, steps in enumerate(all_steps):
                    wait = list(last) if group == 0 else []
                    if group == GROUPS - 1 and level == levels and shift == 0:
                        wait += results[0][0][1:]
                    step = steps.send(wait)
                    if level == levels:
                        remote.append(spread(step))
                last = [step]
            results.append(remote)
            tokens = []

    groups = max(len(result) for result in results)
    width = half // groups

    def chosen(other):
        return [choose(results, group, width, other, per_sub, half // BLOCK) for group in range(groups)]

    came = [swap(values) for values in chosen(True)]
    mine = chosen(False)
    (codes,) = put_codes(mine, width, half, True)
    codes, flat = put_codes(came, width, half, False, codes, mine)
    return codes, flat.T


def solution(mesh):
    return jax.shard_map(
        shards,
        mesh=mesh,
        in_specs=(P(("groups", "seq"), ("tensor", "sub")), P(("tensor", "sub"), "seq"), P("seq")),
        out_specs=(P(("groups", "sub"), "seq"), P(("groups", "sub"), "seq")),
        check_vma=False,
    )
```

```python
import functools
import math

import jax
import jax.numpy as jnp
import numpy as np
from jax import lax
from jax.experimental import pallas as pl
from jax.experimental.pallas import tpu as pltpu
from jax.sharding import PartitionSpec as P

BLOCK = 128
UNIT = 256
GROUPS = 2
VMEM_LIMIT = 6 * 2**20
SHARES = (8, 7, 6)
epsilon = 1e-06

SMALL = pl.CostEstimate(flops=1, bytes_accessed=1, transcendentals=0)
PARAMS = pltpu.CompilerParams(vmem_limit_bytes=VMEM_LIMIT)
VMEM = pl.BlockSpec(memory_space=pltpu.VMEM)
ANY = pl.BlockSpec(memory_space=pl.ANY)
HBM = pl.BlockSpec(memory_space=pltpu.HBM)


def hadamard(order):
    indices = np.arange(order)
    parity = np.zeros((order, order), np.int64)
    for position in range(order.bit_length() - 1):
        parity = parity + (indices[:, None] >> position & 1) * (indices[None, :] >> position & 1)
    return ((1 - 2 * (parity % 2)) / math.sqrt(order)).astype(np.float32)


def slice_body(places, in_ref, *refs):
    out_refs, arrived = refs[:-1], refs[-1]
    copies = [
        pltpu.make_async_copy(in_ref.at[:, at : at + size], out_ref, arrived.at[index])
        for index, ((at, size), out_ref) in enumerate(zip(places, out_refs))
    ]
    for copy in copies:
        copy.start()
    for copy in copies:
        copy.wait()


def slices_of(values, places):
    return pl.pallas_call(
        functools.partial(slice_body, places),
        out_shape=[jax.ShapeDtypeStruct((values.shape[0], size), values.dtype) for _, size in places],
        in_specs=[HBM],
        out_specs=[VMEM] * len(places),
        scratch_shapes=[pltpu.SemaphoreType.DMA((len(places),))],
        compiler_params=PARAMS,
        cost_estimate=SMALL,
    )(values)


def multiply_body(spans, has_totals, splits, row, groups, only, *refs):
    lefts = [refs[begin:end] for begin, end in spans]
    refs = refs[spans[-1][1] :]
    w_ref, refs = refs[0], refs[1:]
    total_refs, refs = list(refs[: sum(has_totals)]), refs[sum(has_totals) :]
    buffer, arrived = refs[-2:]
    outs_of_split = 2 if only is not None else 2 * groups
    out_count = sum(outs_of_split if split else 1 for split in splits)
    out_refs = refs[-2 - out_count : -2]
    steps, depth, wide = buffer.shape
    rows = lefts[0][0].shape[0]
    in_half = w_ref.shape[1] // wide // 2
    first = in_half // groups
    here = lax.axis_index("sub")

    def column(n):
        if not any(splits):
            return n
        group, place = n // (2 * first), n % (2 * first)
        group = group if only is None else only
        side, place = (here, place - first) if place >= first else (1 - here, place)
        return side * in_half + group * first + place

    def at(block):
        return pl.ds(pl.multiple_of(block * wide, wide), wide)

    def copy(n):
        return pltpu.make_async_copy(w_ref.at[pl.ds(row, depth), at(column(n))], buffer.at[n], arrived.at[n])

    def step(n):
        copy(n).wait()
        product, begin = None, 0
        for index in range(len(lefts[0])):
            parts = [left[index][...] for left in lefts]
            left = parts[0] if len(parts) == 1 else jnp.concatenate(parts, axis=0)
            end = begin + left.shape[1]
            part = jnp.dot(left, buffer[n, begin:end], preferred_element_type=jnp.float32)
            product = part if product is None else product + part
            begin = end
        totals, outs = list(total_refs), list(out_refs)
        for index in range(len(lefts)):
            value = product[index * rows : (index + 1) * rows]
            if has_totals[index]:
                value = value + totals.pop(0)[:, at(column(n))]
            if splits[index]:
                group, place = n // (2 * first), n % (2 * first)
                out_ref = outs[2 * group + place // first]
                begin = place % first * wide
                out_ref[:, begin : begin + wide] = value.astype(out_ref.dtype)
                outs = outs[outs_of_split:]
            else:
                outs.pop(0)[:, at(column(n))] = value

    for n in range(steps):
        copy(n).start()
    if any(splits):
        for n in range(steps):
            step(n)
    else:
        pl.loop(0, steps)(step)


def multiply(lefts, weight, row, totals, splits, wide, groups=1, only=None, tokens=()):
    rows = lefts[0][0].shape[0]
    depth = sum(part.shape[1] for part in lefts[0])
    columns = weight.shape[1]
    steps = columns // wide // (1 if only is None else groups)
    spans = [(index * len(left), (index + 1) * len(left)) for index, left in enumerate(lefts)]
    held = [total for total in totals if total is not None]
    out_shape = []
    for split in splits:
        if split:
            out_shape += [
                jax.ShapeDtypeStruct((rows, columns // 2 // groups), jnp.bfloat16),
                jax.ShapeDtypeStruct((rows, columns // 2 // groups), jnp.float32),
            ] * (groups if only is None else 1)
        else:
            out_shape.append(jax.ShapeDtypeStruct((rows, columns), jnp.float32))
    body = functools.partial(
        multiply_body, spans, [total is not None for total in totals], splits, row, groups, only
    )
    return pl.pallas_call(
        body,
        out_shape=out_shape,
        in_specs=[VMEM] * spans[-1][1] + [HBM] + [VMEM] * len(held) + [ANY] * len(tokens),
        out_specs=[VMEM] * len(out_shape),
        scratch_shapes=[
            pltpu.VMEM((steps, depth, wide), weight.dtype),
            pltpu.SemaphoreType.DMA((steps,)),
        ],
        compiler_params=pltpu.CompilerParams(
            vmem_limit_bytes=2 * steps * depth * wide + VMEM_LIMIT
        ),
        cost_estimate=SMALL,
    )(*[part for left in lefts for part in left], weight, *held, *tokens)


def gate(values, tokens):
    return pl.pallas_call(
        lambda *refs: None,
        out_shape=jax.ShapeDtypeStruct(values.shape, values.dtype),
        in_specs=[ANY] * (1 + len(tokens)),
        out_specs=ANY,
        input_output_aliases={0: 0},
        compiler_params=PARAMS,
        cost_estimate=SMALL,
    )(values, *tokens)


def join_body(first_ref, second_ref, out_ref):
    rows = first_ref.shape[0]
    out_ref[:rows] = first_ref[...]
    out_ref[rows:] = second_ref[...]


def join(first, second):
    return pl.pallas_call(
        join_body,
        out_shape=jax.ShapeDtypeStruct((2 * first.shape[0], first.shape[1]), first.dtype),
        in_specs=[VMEM, VMEM],
        out_specs=VMEM,
        compiler_params=PARAMS,
        cost_estimate=SMALL,
    )(first, second)


def halve_body(level, count, *refs):
    kept_refs, came_refs, (sent_out, kept_out) = refs[:count], refs[count : 2 * count], refs[-2:]
    half, columns = sent_out.shape
    width = columns // count

    def put(bit):
        mine, other = slice(bit * half, (bit + 1) * half), slice((1 - bit) * half, (2 - bit) * half)
        for index, (kept_ref, came_ref) in enumerate(zip(kept_refs, came_refs)):
            at = slice(index * width, (index + 1) * width)
            kept_out[:, at] = kept_ref[mine] + came_ref[mine].astype(jnp.float32)
            sent_out[:, at] = (kept_ref[other] + came_ref[other].astype(jnp.float32)).astype(jnp.bfloat16)

    for bit in range(2):
        pl.when(lax.axis_index("tensor") >> level & 1 == bit)(functools.partial(put, bit))


def halve(kept, came, level, tokens=()):
    rows, columns = kept[0].shape
    half, columns = rows // 2, columns * len(kept)
    if half % 16:
        total = jnp.concatenate(kept, axis=1) + jnp.concatenate(came, axis=1).astype(jnp.float32)
        bit = lax.axis_index("tensor") >> level & 1
        sent = lax.dynamic_slice_in_dim(total, (1 - bit) * half, half, 0).astype(jnp.bfloat16)
        return sent, lax.dynamic_slice_in_dim(total, bit * half, half, 0)
    return pl.pallas_call(
        functools.partial(halve_body, level, len(kept)),
        out_shape=[
            jax.ShapeDtypeStruct((half, columns), jnp.bfloat16),
            jax.ShapeDtypeStruct((half, columns), jnp.float32),
        ],
        in_specs=[VMEM] * (2 * len(kept)) + [ANY] * len(tokens),
        out_specs=[VMEM, VMEM],
        compiler_params=PARAMS,
        cost_estimate=SMALL,
    )(*kept, *came, *tokens)


def encode_body(begin, lane, last, kept_ref, came_ref, scales_ref, flips_ref, rotation_ref, *refs):
    out_ref = refs[-1 if last else -2]
    rows, columns = kept_ref.shape
    half = flips_ref.shape[1] // 2
    blocks = columns // BLOCK
    lanes = lax.broadcasted_iota(jnp.int32, (rows, BLOCK), 1)
    scales = scales_ref[...]
    totals = []
    for block in range(blocks):
        at = slice(block * BLOCK, (block + 1) * BLOCK)
        place = lax.axis_index("sub") * half + begin + block * BLOCK
        flips = flips_ref[:, pl.ds(pl.multiple_of(place, BLOCK), BLOCK)]
        totals.append((kept_ref[:, at] + came_ref[:, at].astype(jnp.float32)) * flips)
    rotated = jnp.dot(
        jnp.concatenate(totals, axis=0),
        rotation_ref[...],
        precision=lax.Precision.HIGHEST,
        preferred_element_type=jnp.float32,
    )
    largest = jnp.max(jnp.abs(rotated), axis=1, keepdims=True)
    scale = (largest + epsilon).astype(jnp.bfloat16).astype(jnp.float32)
    codes = rotated / scale
    for block in range(blocks):
        part = slice(block * rows, (block + 1) * rows)
        out_ref[:, block * BLOCK : (block + 1) * BLOCK] = codes[part].astype(jnp.bfloat16)
        scales = jnp.where(lanes == lane + block, scale[part], scales)
    if last:
        out_ref[:, columns:] = scales.astype(jnp.bfloat16)
    else:
        refs[-1][...] = scales


def encode(kept, came, begin, scales, lane, last, flips, rotation, tokens=()):
    rows, columns = kept.shape
    out_shape = [jax.ShapeDtypeStruct((rows, columns + (BLOCK if last else 0)), jnp.bfloat16)]
    if not last:
        out_shape.append(jax.ShapeDtypeStruct((rows, BLOCK), jnp.float32))
    return pl.pallas_call(
        functools.partial(encode_body, begin, lane, last),
        out_shape=out_shape,
        in_specs=[VMEM] * 5 + [ANY] * len(tokens),
        out_specs=[VMEM] * len(out_shape),
        compiler_params=PARAMS,
        cost_estimate=SMALL,
    )(kept, came, scales, flips, rotation, *tokens)


def rank_of(index, count):
    levels = count.bit_length() - 1
    return sum((index >> level & 1) << (levels - 1 - level) for level in range(levels))


def block_of(other, place, places, blocks):
    sub = lax.axis_index("sub")
    sub = 1 - sub if other else sub
    return lax.rem(lax.axis_index("seq") - (sub * places + place) + blocks, blocks)


def choose_body(blocks, count, rows, tops, width, begins, other, places, scales, lane, *refs):
    out_ref = refs[-1]

    def put(block, place):
        for piece in range(count):
            row = (place * count + rank_of(lax.axis_index("tensor") ^ piece, count)) * rows
            here = pl.ds(pl.multiple_of(row, rows), rows)
            begin = begins[block]
            ref, top = refs[block * count + piece], tops[block * count + piece]
            out_ref[here, :width] = ref[top : top + rows, begin : begin + width]
            ref, top = refs[(blocks - 1) * count + piece], tops[(blocks - 1) * count + piece]
            at = ref.shape[1] - BLOCK + block * scales + lane
            out_ref[here, width : width + width // BLOCK] = ref[top : top + rows, at : at + width // BLOCK]

    for place in range(places):
        for block in range(blocks):
            pl.when(block_of(other, place, places, blocks) == block)(functools.partial(put, block, place))


def choose(results, group, width, other, places, scales):
    picked = [result[0] if len(result) == 1 else result[group] for result in results]
    begins = [group * width if len(result) == 1 else 0 for result in results]
    lane = group * (width // BLOCK)
    count = len(picked[0])
    picked = [[piece if isinstance(piece, tuple) else (piece, 0) for piece in pieces] for pieces in picked]
    rows = picked[0][0][0].shape[0]
    columns = width + BLOCK
    if rows % 16:
        blocks = []
        for block, (pieces, begin) in enumerate(zip(picked, begins)):
            held = jnp.zeros((count * rows, columns), jnp.bfloat16)
            for index, (piece, top) in enumerate(pieces):
                part = piece[top : top + rows, begin : begin + width]
                scaled, top = picked[-1][index]
                at = scaled.shape[1] - BLOCK + block * scales + lane
                scale = scaled[top : top + rows, at : at + width // BLOCK]
                part = jnp.concatenate([part, jnp.pad(scale, ((0, 0), (0, BLOCK - width // BLOCK)))], axis=1)
                row = rank_of(lax.axis_index("tensor") ^ index, count) * rows
                held = lax.dynamic_update_slice_in_dim(held, part, row, 0)
            blocks.append(held)
        stacked = jnp.stack(blocks)
        return jnp.concatenate([stacked[block_of(other, place, places, len(blocks))] for place in range(places)])
    operands = [piece for pieces in picked for piece, _ in pieces]
    tops = [top for pieces in picked for _, top in pieces]
    return pl.pallas_call(
        functools.partial(choose_body, len(picked), count, rows, tops, width, begins, other, places, scales, lane),
        out_shape=jax.ShapeDtypeStruct((places * count * rows, columns), jnp.bfloat16),
        in_specs=[VMEM] * len(operands),
        out_specs=VMEM,
        compiler_params=PARAMS,
        cost_estimate=SMALL,
    )(*operands)


def place_body(mine, half, width, count, held, *refs):
    refs = refs[held:]
    scaled = len(refs) > count + 2
    codes_ref, sems = refs[2 * count if scaled else count], refs[-1]
    sub = lax.axis_index("sub")
    side = sub if mine else 1 - sub

    def put(core):
        copies = [
            pltpu.make_async_copy(
                refs[group].at[:, :width], codes_ref.at[:, pl.ds(core * half + group * width, width)], sems.at[group]
            )
            for group in range(count)
        ]
        for copy in copies:
            copy.start()
        if scaled:
            out_ref, flat = refs[2 * count + 1 : 2 * count + 3]
            order = refs[count : 2 * count] + refs[:count] if core else refs[: 2 * count]
            scales = [ref[:, width : width + width // BLOCK].astype(jnp.float32) for ref in order]
            flat[...] = jnp.concatenate(scales, axis=1).T.astype(jnp.bfloat16)
            copies.append(pltpu.make_async_copy(flat, out_ref, sems.at[count]))
            copies[-1].start()
        for copy in copies:
            copy.wait()

    for core in range(2):
        pl.when(side == core)(functools.partial(put, core))


def put_codes(arrays, width, half, mine, codes=None, mine_too=()):
    rows = arrays[0].shape[0]
    operands = list(arrays) + list(mine_too)
    out_shape = [jax.ShapeDtypeStruct((rows, 2 * half), jnp.bfloat16)]
    scratch = [pltpu.SemaphoreType.DMA((len(arrays) + 1,))]
    if mine_too:
        out_shape.append(jax.ShapeDtypeStruct((2 * half // BLOCK, rows), jnp.bfloat16))
        scratch.insert(0, pltpu.VMEM((2 * half // BLOCK, rows), jnp.bfloat16))
    held = [] if codes is None else [codes]
    return pl.pallas_call(
        functools.partial(place_body, mine, half, width, len(arrays), len(held)),
        out_shape=out_shape,
        in_specs=[HBM] * len(held) + [VMEM] * len(operands),
        out_specs=[HBM] * len(out_shape),
        input_output_aliases={0: 0} if held else {},
        scratch_shapes=scratch,
        compiler_params=PARAMS,
        cost_estimate=SMALL,
    )(*held, *operands)


def cut(depth):
    if depth % UNIT or depth < 16 * UNIT:
        return [depth]
    units = depth // UNIT
    sizes = [max(1, units * share // 26) for share in SHARES]
    return [size * UNIT for size in sizes + [units - sum(sizes)]]


def shards(hidden, down_weight, sign_bits):
    tensor_count = lax.axis_size("tensor")
    seq_count = lax.axis_size("seq")
    sub_count = lax.axis_size("sub")
    depth = hidden.shape[1]
    half = down_weight.shape[1] // sub_count
    per_sub = seq_count // sub_count
    levels = tensor_count.bit_length() - 1
    wide, wide_chunk, wide_merged = (min(size, half // GROUPS) for size in (256, 512, 1024))
    flips = (2 * sign_bits - 1).astype(jnp.float32)[None, :]
    rotation = jnp.asarray(hadamard(BLOCK))

    def swap(values):
        return lax.ppermute(values, "sub", [(0, 1), (1, 0)])

    def exchange(values, level):
        return lax.ppermute(values, "tensor", [(t, t ^ 1 << level) for t in range(tensor_count)])

    def reduce(halves, begin, block, base, last):
        tokens = (yield None) or []
        kept, came = halves[1::2], [swap(sent) for sent in halves[::2]]
        for level in range(levels):
            sent, held = halve(kept, came, level, tokens)
            tokens = (yield sent) or []
            kept, came = [held], [exchange(sent, level)]
        packed, *base[:] = encode(
            kept[0], came[0], begin, base[0], (block * half + begin) // BLOCK, last, flips, rotation, tokens
        )
        yield packed

    def spread(packed):
        pieces = {0: packed}
        for level in reversed(range(levels)):
            for index in list(pieces):
                pieces[index ^ 1 << level] = exchange(pieces[index], level)
        return [pieces[index] for index in range(tensor_count)]

    zeros = jnp.zeros((hidden.shape[0] // tensor_count, BLOCK), jnp.float32)
    def spread_joined(packed):
        rows, here = packed.shape[0], packed
        pieces = {0: (packed, 0)}
        for level in reversed(range(levels)):
            came = exchange(here, level)
            order = list(pieces)
            for place, index in enumerate(order):
                pieces[index ^ 1 << level] = (came, place * rows)
            if level:
                here = join(here, came)
        return [pieces[index] for index in range(tensor_count)]

    sizes = cut(depth)
    places = [sum(sizes[:index]) for index in range(len(sizes))]
    parts = slices_of(hidden, list(zip(places, sizes)))

    def from_seq(part, shift):
        return lax.ppermute(part, "seq", [(s, (s + shift) % seq_count) for s in range(seq_count)])

    early = max(1, len(sizes) - 1)
    arrivals = [[from_seq(part, shift) for part in parts[:early]] for shift in range(1, seq_count)]

    if len(sizes) == 1:
        outs = multiply([[parts[0]], [arrivals[0][0]]], down_weight, 0, [None, None], [True, True], wide_chunk)
        base = [zeros]
        reduced = [list(reduce(outs[:2], 0, 0, base, False))[-1], list(reduce(outs[2:], 0, 1, base, seq_count == 2))[-1]]
        for block, arrived in enumerate(arrivals[1:], 2):
            outs = multiply([[arrived[0]]], down_weight, 0, [None], [True], wide_chunk)
            reduced.append(list(reduce(outs, 0, block, base, block == seq_count - 1))[-1])
        results = [[spread(packed)] for packed in reduced]
    else:
        (own,) = multiply([parts[1:]], down_weight, sizes[0], [None], [False], wide, tokens=parts[:1])
        *halves, total = multiply(
            [[parts[0]], [arrivals[0][0]]], down_weight, 0, [own, None], [True, False], wide_merged, groups=GROUPS
        )
        own_base = [zeros]
        own_steps = reduce(halves, 0, 0, own_base, False)
        next(own_steps)
        tokens = [own_steps.send([arrivals[0][1]])]
        results = []
        for shift, arrived in enumerate(arrivals):
            if shift:
                (total,) = multiply([[arrived[0]]], down_weight, 0, [None], [False], wide_chunk)
            for index in range(1, len(sizes) - 1):
                (total,) = multiply(
                    [[arrived[index]]], down_weight, places[index], [total], [False], wide_chunk, tokens=tokens
                )
                if index == 1 and shift == 0:
                    late = gate(parts[-1], [total])
                if not results:
                    step = own_steps.send([total])
                    tokens = [step]
                    if own_base[0] is not zeros:
                        results.append([spread(step)])
            if not results:
                results.append([spread(list(own_steps)[-1])])
            if shift == 0:
                bases = [list(own_base) for _ in range(GROUPS)]
            outs = multiply(
                [[from_seq(late, shift + 1)]], down_weight, places[-1], [total], [True], wide_chunk,
                groups=GROUPS, tokens=tokens,
            )
            remote, all_steps = [], []
            for group in range(GROUPS):
                sent, kept = outs[2 * group : 2 * group + 2]
                if group == GROUPS - 1 and shift == 0 and levels > 1:
                    sent = gate(sent, [results[0][0][1], results[0][0][1 << levels - 1]])
                all_steps.append(reduce([sent, kept], group * half // GROUPS, shift + 1, bases[group], shift == seq_count - 2))
                next(all_steps[-1])
            last = []
            for level in range(levels + 1):
                for group, steps in enumerate(all_steps):
                    wait = list(last) if group == 0 else []
                    if group == GROUPS - 1 and level == levels and shift == 0:
                        wait += results[0][0][1:]
                    step = steps.send(wait)
                    if level == levels:
                        remote.append(spread_joined(step))
                last = [step]
            results.append(remote)
            tokens = []

    groups = max(len(result) for result in results)
    width = half // groups

    def chosen(other):
        return [choose(results, group, width, other, per_sub, half // BLOCK) for group in range(groups)]

    came = [swap(values) for values in chosen(True)]
    mine = chosen(False)
    (codes,) = put_codes(mine, width, half, True)
    codes, flat = put_codes(came, width, half, False, codes, mine)
    return codes, flat.T


def solution(mesh):
    return jax.shard_map(
        shards,
        mesh=mesh,
        in_specs=(P(("groups", "seq"), ("tensor", "sub")), P(("tensor", "sub"), "seq"), P("seq")),
        out_specs=(P(("groups", "sub"), "seq"), P(("groups", "sub"), "seq")),
        check_vma=False,
    )
```

```python
import functools
import math

import jax
import jax.numpy as jnp
import numpy as np
from jax import lax
from jax.experimental import pallas as pl
from jax.experimental.pallas import tpu as pltpu
from jax.sharding import PartitionSpec as P

BLOCK = 128
UNIT = 256
GROUPS = 2
VMEM_LIMIT = 6 * 2**20
SHARES = (8, 7, 6)
epsilon = 1e-06

SMALL = pl.CostEstimate(flops=1, bytes_accessed=1, transcendentals=0)
PARAMS = pltpu.CompilerParams(vmem_limit_bytes=VMEM_LIMIT)
VMEM = pl.BlockSpec(memory_space=pltpu.VMEM)
ANY = pl.BlockSpec(memory_space=pl.ANY)
HBM = pl.BlockSpec(memory_space=pltpu.HBM)


def hadamard(order):
    indices = np.arange(order)
    parity = np.zeros((order, order), np.int64)
    for position in range(order.bit_length() - 1):
        parity = parity + (indices[:, None] >> position & 1) * (indices[None, :] >> position & 1)
    return ((1 - 2 * (parity % 2)) / math.sqrt(order)).astype(np.float32)


def slice_body(places, in_ref, *refs):
    out_refs, arrived = refs[:-1], refs[-1]
    copies = [
        pltpu.make_async_copy(in_ref.at[:, at : at + size], out_ref, arrived.at[index])
        for index, ((at, size), out_ref) in enumerate(zip(places, out_refs))
    ]
    for copy in copies:
        copy.start()
    for copy in copies:
        copy.wait()


def slices_of(values, places):
    return pl.pallas_call(
        functools.partial(slice_body, places),
        out_shape=[jax.ShapeDtypeStruct((values.shape[0], size), values.dtype) for _, size in places],
        in_specs=[HBM],
        out_specs=[VMEM] * len(places),
        scratch_shapes=[pltpu.SemaphoreType.DMA((len(places),))],
        compiler_params=PARAMS,
        cost_estimate=SMALL,
    )(values)


def multiply_body(spans, has_totals, splits, row, groups, only, *refs):
    lefts = [refs[begin:end] for begin, end in spans]
    refs = refs[spans[-1][1] :]
    w_ref, refs = refs[0], refs[1:]
    total_refs, refs = list(refs[: sum(has_totals)]), refs[sum(has_totals) :]
    buffer, arrived = refs[-2:]
    outs_of_split = 2 if only is not None else 2 * groups
    out_count = sum(outs_of_split if split else 1 for split in splits)
    out_refs = refs[-2 - out_count : -2]
    steps, depth, wide = buffer.shape
    rows = lefts[0][0].shape[0]
    in_half = w_ref.shape[1] // wide // 2
    first = in_half // groups
    ahead = min(steps, max(2, steps // 2))
    here = lax.axis_index("sub")

    def column(n):
        if not any(splits):
            return n
        group, place = n // (2 * first), n % (2 * first)
        group = group if only is None else only
        side, place = (here, place - first) if place >= first else (1 - here, place)
        return side * in_half + group * first + place

    def at(block):
        return pl.ds(pl.multiple_of(block * wide, wide), wide)

    def copy(n):
        return pltpu.make_async_copy(w_ref.at[pl.ds(row, depth), at(column(n))], buffer.at[n], arrived.at[n])

    def step(n):
        copy(n).wait()
        if any(splits):
            if n + ahead < steps:
                copy(n + ahead).start()
        else:
            pl.when(n + ahead < steps)(lambda: copy(n + ahead).start())
        product, begin = None, 0
        for index in range(len(lefts[0])):
            parts = [left[index][...] for left in lefts]
            left = parts[0] if len(parts) == 1 else jnp.concatenate(parts, axis=0)
            end = begin + left.shape[1]
            part = jnp.dot(left, buffer[n, begin:end], preferred_element_type=jnp.float32)
            product = part if product is None else product + part
            begin = end
        totals, outs = list(total_refs), list(out_refs)
        for index in range(len(lefts)):
            value = product[index * rows : (index + 1) * rows]
            if has_totals[index]:
                value = value + totals.pop(0)[:, at(column(n))]
            if splits[index]:
                group, place = n // (2 * first), n % (2 * first)
                out_ref = outs[2 * group + place // first]
                begin = place % first * wide
                out_ref[:, begin : begin + wide] = value.astype(out_ref.dtype)
                outs = outs[outs_of_split:]
            else:
                outs.pop(0)[:, at(column(n))] = value

    for n in range(ahead):
        copy(n).start()
    if any(splits):
        for n in range(steps):
            step(n)
    else:
        pl.loop(0, steps)(step)


def multiply(lefts, weight, row, totals, splits, wide, groups=1, only=None, tokens=()):
    rows = lefts[0][0].shape[0]
    depth = sum(part.shape[1] for part in lefts[0])
    columns = weight.shape[1]
    steps = columns // wide // (1 if only is None else groups)
    spans = [(index * len(left), (index + 1) * len(left)) for index, left in enumerate(lefts)]
    held = [total for total in totals if total is not None]
    out_shape = []
    for split in splits:
        if split:
            out_shape += [
                jax.ShapeDtypeStruct((rows, columns // 2 // groups), jnp.bfloat16),
                jax.ShapeDtypeStruct((rows, columns // 2 // groups), jnp.float32),
            ] * (groups if only is None else 1)
        else:
            out_shape.append(jax.ShapeDtypeStruct((rows, columns), jnp.float32))
    body = functools.partial(
        multiply_body, spans, [total is not None for total in totals], splits, row, groups, only
    )
    return pl.pallas_call(
        body,
        out_shape=out_shape,
        in_specs=[VMEM] * spans[-1][1] + [HBM] + [VMEM] * len(held) + [ANY] * len(tokens),
        out_specs=[VMEM] * len(out_shape),
        scratch_shapes=[
            pltpu.VMEM((steps, depth, wide), weight.dtype),
            pltpu.SemaphoreType.DMA((steps,)),
        ],
        compiler_params=pltpu.CompilerParams(
            vmem_limit_bytes=2 * steps * depth * wide + VMEM_LIMIT
        ),
        cost_estimate=SMALL,
    )(*[part for left in lefts for part in left], weight, *held, *tokens)


def gate(values, tokens):
    return pl.pallas_call(
        lambda *refs: None,
        out_shape=jax.ShapeDtypeStruct(values.shape, values.dtype),
        in_specs=[ANY] * (1 + len(tokens)),
        out_specs=ANY,
        input_output_aliases={0: 0},
        compiler_params=PARAMS,
        cost_estimate=SMALL,
    )(values, *tokens)


def halve_body(level, count, *refs):
    kept_refs, came_refs, (sent_out, kept_out) = refs[:count], refs[count : 2 * count], refs[-2:]
    half, columns = sent_out.shape
    width = columns // count

    def put(bit):
        mine, other = slice(bit * half, (bit + 1) * half), slice((1 - bit) * half, (2 - bit) * half)
        for index, (kept_ref, came_ref) in enumerate(zip(kept_refs, came_refs)):
            at = slice(index * width, (index + 1) * width)
            kept_out[:, at] = kept_ref[mine] + came_ref[mine].astype(jnp.float32)
            sent_out[:, at] = (kept_ref[other] + came_ref[other].astype(jnp.float32)).astype(jnp.bfloat16)

    for bit in range(2):
        pl.when(lax.axis_index("tensor") >> level & 1 == bit)(functools.partial(put, bit))


def halve(kept, came, level, tokens=()):
    rows, columns = kept[0].shape
    half, columns = rows // 2, columns * len(kept)
    if half % 16:
        total = jnp.concatenate(kept, axis=1) + jnp.concatenate(came, axis=1).astype(jnp.float32)
        bit = lax.axis_index("tensor") >> level & 1
        sent = lax.dynamic_slice_in_dim(total, (1 - bit) * half, half, 0).astype(jnp.bfloat16)
        return sent, lax.dynamic_slice_in_dim(total, bit * half, half, 0)
    return pl.pallas_call(
        functools.partial(halve_body, level, len(kept)),
        out_shape=[
            jax.ShapeDtypeStruct((half, columns), jnp.bfloat16),
            jax.ShapeDtypeStruct((half, columns), jnp.float32),
        ],
        in_specs=[VMEM] * (2 * len(kept)) + [ANY] * len(tokens),
        out_specs=[VMEM, VMEM],
        compiler_params=PARAMS,
        cost_estimate=SMALL,
    )(*kept, *came, *tokens)


def encode_body(begin, lane, last, kept_ref, came_ref, scales_ref, flips_ref, rotation_ref, *refs):
    out_ref = refs[-1 if last else -2]
    rows, columns = kept_ref.shape
    half = flips_ref.shape[1] // 2
    blocks = columns // BLOCK
    lanes = lax.broadcasted_iota(jnp.int32, (rows, BLOCK), 1)
    scales = scales_ref[...]
    totals = []
    for block in range(blocks):
        at = slice(block * BLOCK, (block + 1) * BLOCK)
        place = lax.axis_index("sub") * half + begin + block * BLOCK
        flips = flips_ref[:, pl.ds(pl.multiple_of(place, BLOCK), BLOCK)]
        totals.append((kept_ref[:, at] + came_ref[:, at].astype(jnp.float32)) * flips)
    rotated = jnp.dot(
        jnp.concatenate(totals, axis=0),
        rotation_ref[...],
        precision=lax.Precision.HIGHEST,
        preferred_element_type=jnp.float32,
    )
    largest = jnp.max(jnp.abs(rotated), axis=1, keepdims=True)
    scale = (largest + epsilon).astype(jnp.bfloat16).astype(jnp.float32)
    codes = rotated / scale
    for block in range(blocks):
        part = slice(block * rows, (block + 1) * rows)
        out_ref[:, block * BLOCK : (block + 1) * BLOCK] = codes[part].astype(jnp.bfloat16)
        scales = jnp.where(lanes == lane + block, scale[part], scales)
    if last:
        out_ref[:, columns:] = scales.astype(jnp.bfloat16)
    else:
        refs[-1][...] = scales


def encode(kept, came, begin, scales, lane, last, flips, rotation, tokens=()):
    rows, columns = kept.shape
    out_shape = [jax.ShapeDtypeStruct((rows, columns + (BLOCK if last else 0)), jnp.bfloat16)]
    if not last:
        out_shape.append(jax.ShapeDtypeStruct((rows, BLOCK), jnp.float32))
    return pl.pallas_call(
        functools.partial(encode_body, begin, lane, last),
        out_shape=out_shape,
        in_specs=[VMEM] * 5 + [ANY] * len(tokens),
        out_specs=[VMEM] * len(out_shape),
        compiler_params=PARAMS,
        cost_estimate=SMALL,
    )(kept, came, scales, flips, rotation, *tokens)


def rank_of(index, count):
    levels = count.bit_length() - 1
    return sum((index >> level & 1) << (levels - 1 - level) for level in range(levels))


def block_of(other, place, places, blocks):
    sub = lax.axis_index("sub")
    sub = 1 - sub if other else sub
    return lax.rem(lax.axis_index("seq") - (sub * places + place) + blocks, blocks)


def choose_body(blocks, count, rows, tops, width, begins, other, places, scales, lane, *refs):
    out_ref = refs[-1]

    def put(block, place):
        for piece in range(count):
            row = (place * count + rank_of(lax.axis_index("tensor") ^ piece, count)) * rows
            here = pl.ds(pl.multiple_of(row, rows), rows)
            begin = begins[block]
            ref, top = refs[block * count + piece], tops[block * count + piece]
            out_ref[here, :width] = ref[top : top + rows, begin : begin + width]
            ref, top = refs[(blocks - 1) * count + piece], tops[(blocks - 1) * count + piece]
            at = ref.shape[1] - BLOCK + block * scales + lane
            out_ref[here, width : width + width // BLOCK] = ref[top : top + rows, at : at + width // BLOCK]

    for place in range(places):
        for block in range(blocks):
            pl.when(block_of(other, place, places, blocks) == block)(functools.partial(put, block, place))


def choose(results, group, width, other, places, scales):
    picked = [result[0] if len(result) == 1 else result[group] for result in results]
    begins = [group * width if len(result) == 1 else 0 for result in results]
    lane = group * (width // BLOCK)
    count = len(picked[0])
    picked = [[piece if isinstance(piece, tuple) else (piece, 0) for piece in pieces] for pieces in picked]
    rows = picked[0][0][0].shape[0]
    columns = width + BLOCK
    if rows % 16:
        blocks = []
        for block, (pieces, begin) in enumerate(zip(picked, begins)):
            held = jnp.zeros((count * rows, columns), jnp.bfloat16)
            for index, (piece, top) in enumerate(pieces):
                part = piece[top : top + rows, begin : begin + width]
                scaled, top = picked[-1][index]
                at = scaled.shape[1] - BLOCK + block * scales + lane
                scale = scaled[top : top + rows, at : at + width // BLOCK]
                part = jnp.concatenate([part, jnp.pad(scale, ((0, 0), (0, BLOCK - width // BLOCK)))], axis=1)
                row = rank_of(lax.axis_index("tensor") ^ index, count) * rows
                held = lax.dynamic_update_slice_in_dim(held, part, row, 0)
            blocks.append(held)
        stacked = jnp.stack(blocks)
        return jnp.concatenate([stacked[block_of(other, place, places, len(blocks))] for place in range(places)])
    operands = [piece for pieces in picked for piece, _ in pieces]
    tops = [top for pieces in picked for _, top in pieces]
    return pl.pallas_call(
        functools.partial(choose_body, len(picked), count, rows, tops, width, begins, other, places, scales, lane),
        out_shape=jax.ShapeDtypeStruct((places * count * rows, columns), jnp.bfloat16),
        in_specs=[VMEM] * len(operands),
        out_specs=VMEM,
        compiler_params=PARAMS,
        cost_estimate=SMALL,
    )(*operands)


def place_body(mine, half, width, count, held, *refs):
    refs = refs[held:]
    scaled = len(refs) > count + 2
    codes_ref, sems = refs[2 * count if scaled else count], refs[-1]
    sub = lax.axis_index("sub")
    side = sub if mine else 1 - sub

    def put(core):
        copies = [
            pltpu.make_async_copy(
                refs[group].at[:, :width], codes_ref.at[:, pl.ds(core * half + group * width, width)], sems.at[group]
            )
            for group in range(count)
        ]
        for copy in copies:
            copy.start()
        if scaled:
            out_ref, flat = refs[2 * count + 1 : 2 * count + 3]
            order = refs[count : 2 * count] + refs[:count] if core else refs[: 2 * count]
            scales = [ref[:, width : width + width // BLOCK].astype(jnp.float32) for ref in order]
            flat[...] = jnp.concatenate(scales, axis=1).T.astype(jnp.bfloat16)
            copies.append(pltpu.make_async_copy(flat, out_ref, sems.at[count]))
            copies[-1].start()
        for copy in copies:
            copy.wait()

    for core in range(2):
        pl.when(side == core)(functools.partial(put, core))


def put_codes(arrays, width, half, mine, codes=None, mine_too=()):
    rows = arrays[0].shape[0]
    operands = list(arrays) + list(mine_too)
    out_shape = [jax.ShapeDtypeStruct((rows, 2 * half), jnp.bfloat16)]
    scratch = [pltpu.SemaphoreType.DMA((len(arrays) + 1,))]
    if mine_too:
        out_shape.append(jax.ShapeDtypeStruct((2 * half // BLOCK, rows), jnp.bfloat16))
        scratch.insert(0, pltpu.VMEM((2 * half // BLOCK, rows), jnp.bfloat16))
    held = [] if codes is None else [codes]
    return pl.pallas_call(
        functools.partial(place_body, mine, half, width, len(arrays), len(held)),
        out_shape=out_shape,
        in_specs=[HBM] * len(held) + [VMEM] * len(operands),
        out_specs=[HBM] * len(out_shape),
        input_output_aliases={0: 0} if held else {},
        scratch_shapes=scratch,
        compiler_params=PARAMS,
        cost_estimate=SMALL,
    )(*held, *operands)


def cut(depth):
    if depth % UNIT or depth < 16 * UNIT:
        return [depth]
    units = depth // UNIT
    sizes = [max(1, units * share // 26) for share in SHARES]
    return [size * UNIT for size in sizes + [units - sum(sizes)]]


def shards(hidden, down_weight, sign_bits):
    tensor_count = lax.axis_size("tensor")
    seq_count = lax.axis_size("seq")
    sub_count = lax.axis_size("sub")
    depth = hidden.shape[1]
    half = down_weight.shape[1] // sub_count
    per_sub = seq_count // sub_count
    levels = tensor_count.bit_length() - 1
    wide, wide_chunk, wide_merged = (min(size, half // GROUPS) for size in (256, 512, 1024))
    flips = (2 * sign_bits - 1).astype(jnp.float32)[None, :]
    rotation = jnp.asarray(hadamard(BLOCK))

    def swap(values):
        return lax.ppermute(values, "sub", [(0, 1), (1, 0)])

    def exchange(values, level):
        return lax.ppermute(values, "tensor", [(t, t ^ 1 << level) for t in range(tensor_count)])

    def reduce(halves, begin, block, base, last):
        tokens = (yield None) or []
        kept, came = halves[1::2], [swap(sent) for sent in halves[::2]]
        for level in range(levels):
            sent, held = halve(kept, came, level, tokens)
            tokens = (yield sent) or []
            kept, came = [held], [exchange(sent, level)]
        packed, *base[:] = encode(
            kept[0], came[0], begin, base[0], (block * half + begin) // BLOCK, last, flips, rotation, tokens
        )
        yield packed

    def spread(packed):
        pieces = {0: packed}
        for level in reversed(range(levels)):
            for index in list(pieces):
                pieces[index ^ 1 << level] = exchange(pieces[index], level)
        return [pieces[index] for index in range(tensor_count)]

    zeros = jnp.zeros((hidden.shape[0] // tensor_count, BLOCK), jnp.float32)
    sizes = cut(depth)
    places = [sum(sizes[:index]) for index in range(len(sizes))]
    parts = slices_of(hidden, list(zip(places, sizes)))

    def from_seq(part, shift):
        return lax.ppermute(part, "seq", [(s, (s + shift) % seq_count) for s in range(seq_count)])

    arrivals = [[from_seq(part, shift) for part in parts] for shift in range(1, seq_count)]

    if len(sizes) == 1:
        outs = multiply([[parts[0]], [arrivals[0][0]]], down_weight, 0, [None, None], [True, True], wide_chunk)
        base = [zeros]
        reduced = [list(reduce(outs[:2], 0, 0, base, False))[-1], list(reduce(outs[2:], 0, 1, base, seq_count == 2))[-1]]
        for block, arrived in enumerate(arrivals[1:], 2):
            outs = multiply([[arrived[0]]], down_weight, 0, [None], [True], wide_chunk)
            reduced.append(list(reduce(outs, 0, block, base, block == seq_count - 1))[-1])
        results = [[spread(packed)] for packed in reduced]
    else:
        (own,) = multiply([parts[1:]], down_weight, sizes[0], [None], [False], wide, tokens=parts[:1])
        *halves, total = multiply(
            [[parts[0]], [arrivals[0][0]]], down_weight, 0, [own, None], [True, False], wide_merged, groups=GROUPS
        )
        own_base = [zeros]
        own_steps = reduce(halves, 0, 0, own_base, False)
        next(own_steps)
        tokens = [own_steps.send([arrivals[0][1]])]
        results = []
        for shift, arrived in enumerate(arrivals):
            if shift:
                (total,) = multiply([[arrived[0]]], down_weight, 0, [None], [False], wide_chunk)
            for index in range(1, len(sizes) - 1):
                (total,) = multiply(
                    [[arrived[index]]], down_weight, places[index], [total], [False], wide_chunk, tokens=tokens
                )
                if not results:
                    step = own_steps.send([total])
                    tokens = [step]
                    if own_base[0] is not zeros:
                        results.append([spread(step)])
            if not results:
                results.append([spread(list(own_steps)[-1])])
            if shift == 0:
                bases = [list(own_base) for _ in range(GROUPS)]
            outs = multiply(
                [[arrived[-1]]], down_weight, places[-1], [total], [True], wide_chunk,
                groups=GROUPS, tokens=tokens,
            )
            remote, all_steps = [], []
            for group in range(GROUPS):
                sent, kept = outs[2 * group : 2 * group + 2]
                if group == GROUPS - 1 and shift == 0 and levels > 1:
                    sent = gate(sent, [results[0][0][1], results[0][0][1 << levels - 1]])
                all_steps.append(reduce([sent, kept], group * half // GROUPS, shift + 1, bases[group], shift == seq_count - 2))
                next(all_steps[-1])
            last = []
            for level in range(levels + 1):
                for group, steps in enumerate(all_steps):
                    wait = list(last) if group == 0 else []
                    if group == GROUPS - 1 and level == levels and shift == 0:
                        wait += results[0][0][1:]
                    step = steps.send(wait)
                    if level == levels:
                        remote.append(spread(step))
                last = [step]
            results.append(remote)
            tokens = []

    groups = max(len(result) for result in results)
    width = half // groups

    def chosen(other):
        return [choose(results, group, width, other, per_sub, half // BLOCK) for group in range(groups)]

    came = [swap(values) for values in chosen(True)]
    mine = chosen(False)
    (codes,) = put_codes(mine, width, half, True)
    codes, flat = put_codes(came, width, half, False, codes, mine)
    return codes, flat.T


def solution(mesh):
    return jax.shard_map(
        shards,
        mesh=mesh,
        in_specs=(P(("groups", "seq"), ("tensor", "sub")), P(("tensor", "sub"), "seq"), P("seq")),
        out_specs=(P(("groups", "sub"), "seq"), P(("groups", "sub"), "seq")),
        check_vma=False,
    )
```

```python
import functools
import math

import jax
import jax.numpy as jnp
import numpy as np
from jax import lax
from jax.experimental import pallas as pl
from jax.experimental.pallas import tpu as pltpu
from jax.sharding import PartitionSpec as P

BLOCK = 128
UNIT = 256
GROUPS = 2
VMEM_LIMIT = 6 * 2**20
SHARES = (8, 7, 6)
epsilon = 1e-06

SMALL = pl.CostEstimate(flops=1, bytes_accessed=1, transcendentals=0)
PARAMS = pltpu.CompilerParams(vmem_limit_bytes=VMEM_LIMIT)
VMEM = pl.BlockSpec(memory_space=pltpu.VMEM)
ANY = pl.BlockSpec(memory_space=pl.ANY)
HBM = pl.BlockSpec(memory_space=pltpu.HBM)


def hadamard(order):
    indices = np.arange(order)
    parity = np.zeros((order, order), np.int64)
    for position in range(order.bit_length() - 1):
        parity = parity + (indices[:, None] >> position & 1) * (indices[None, :] >> position & 1)
    return ((1 - 2 * (parity % 2)) / math.sqrt(order)).astype(np.float32)


def slice_body(places, in_ref, *refs):
    out_refs, arrived = refs[:-1], refs[-1]
    copies = [
        pltpu.make_async_copy(in_ref.at[:, at : at + size], out_ref, arrived.at[index])
        for index, ((at, size), out_ref) in enumerate(zip(places, out_refs))
    ]
    for copy in copies:
        copy.start()
    for copy in copies:
        copy.wait()


def slices_of(values, places):
    return pl.pallas_call(
        functools.partial(slice_body, places),
        out_shape=[jax.ShapeDtypeStruct((values.shape[0], size), values.dtype) for _, size in places],
        in_specs=[HBM],
        out_specs=[VMEM] * len(places),
        scratch_shapes=[pltpu.SemaphoreType.DMA((len(places),))],
        compiler_params=PARAMS,
        cost_estimate=SMALL,
    )(values)


def multiply_body(spans, has_totals, splits, row, groups, only, *refs):
    lefts = [refs[begin:end] for begin, end in spans]
    refs = refs[spans[-1][1] :]
    w_ref, refs = refs[0], refs[1:]
    total_refs, refs = list(refs[: sum(has_totals)]), refs[sum(has_totals) :]
    buffer, arrived = refs[-2:]
    outs_of_split = 2 if only is not None else 2 * groups
    out_count = sum(outs_of_split if split else 1 for split in splits)
    out_refs = refs[-2 - out_count : -2]
    steps, depth, wide = buffer.shape
    rows = lefts[0][0].shape[0]
    in_half = w_ref.shape[1] // wide // 2
    first = in_half // groups
    here = lax.axis_index("sub")

    def column(n):
        if not any(splits):
            return n
        group, place = n // (2 * first), n % (2 * first)
        group = group if only is None else only
        side, place = (here, place - first) if place >= first else (1 - here, place)
        return side * in_half + group * first + place

    def at(block):
        return pl.ds(pl.multiple_of(block * wide, wide), wide)

    def copy(n):
        return pltpu.make_async_copy(w_ref.at[pl.ds(row, depth), at(column(n))], buffer.at[n], arrived.at[n])

    def step(n):
        copy(n).wait()
        product, begin = None, 0
        for index in range(len(lefts[0])):
            parts = [left[index][...] for left in lefts]
            left = parts[0] if len(parts) == 1 else jnp.concatenate(parts, axis=0)
            end = begin + left.shape[1]
            part = jnp.dot(left, buffer[n, begin:end], preferred_element_type=jnp.float32)
            product = part if product is None else product + part
            begin = end
        totals, outs = list(total_refs), list(out_refs)
        for index in range(len(lefts)):
            value = product[index * rows : (index + 1) * rows]
            if has_totals[index]:
                value = value + totals.pop(0)[:, at(column(n))]
            if splits[index]:
                group, place = n // (2 * first), n % (2 * first)
                out_ref = outs[2 * group + place // first]
                begin = place % first * wide
                out_ref[:, begin : begin + wide] = value.astype(out_ref.dtype)
                outs = outs[outs_of_split:]
            else:
                outs.pop(0)[:, at(column(n))] = value

    for n in range(steps):
        copy(n).start()
    if any(splits):
        for n in range(steps):
            step(n)
    else:
        pl.loop(0, steps)(step)


def multiply(lefts, weight, row, totals, splits, wide, groups=1, only=None, tokens=()):
    rows = lefts[0][0].shape[0]
    depth = sum(part.shape[1] for part in lefts[0])
    columns = weight.shape[1]
    steps = columns // wide // (1 if only is None else groups)
    spans = [(index * len(left), (index + 1) * len(left)) for index, left in enumerate(lefts)]
    held = [total for total in totals if total is not None]
    out_shape = []
    for split in splits:
        if split:
            out_shape += [
                jax.ShapeDtypeStruct((rows, columns // 2 // groups), jnp.bfloat16),
                jax.ShapeDtypeStruct((rows, columns // 2 // groups), jnp.float32),
            ] * (groups if only is None else 1)
        else:
            out_shape.append(jax.ShapeDtypeStruct((rows, columns), jnp.float32))
    body = functools.partial(
        multiply_body, spans, [total is not None for total in totals], splits, row, groups, only
    )
    return pl.pallas_call(
        body,
        out_shape=out_shape,
        in_specs=[VMEM] * spans[-1][1] + [HBM] + [VMEM] * len(held) + [ANY] * len(tokens),
        out_specs=[VMEM] * len(out_shape),
        scratch_shapes=[
            pltpu.VMEM((steps, depth, wide), weight.dtype),
            pltpu.SemaphoreType.DMA((steps,)),
        ],
        compiler_params=pltpu.CompilerParams(
            vmem_limit_bytes=2 * steps * depth * wide + VMEM_LIMIT
        ),
        cost_estimate=SMALL,
    )(*[part for left in lefts for part in left], weight, *held, *tokens)


def gate(values, tokens):
    return pl.pallas_call(
        lambda *refs: None,
        out_shape=jax.ShapeDtypeStruct(values.shape, values.dtype),
        in_specs=[ANY] * (1 + len(tokens)),
        out_specs=ANY,
        input_output_aliases={0: 0},
        compiler_params=PARAMS,
        cost_estimate=SMALL,
    )(values, *tokens)


def halve_body(level, count, *refs):
    kept_refs, came_refs, (sent_out, kept_out) = refs[:count], refs[count : 2 * count], refs[-2:]
    half, columns = sent_out.shape
    width = columns // count

    def put(bit):
        mine, other = slice(bit * half, (bit + 1) * half), slice((1 - bit) * half, (2 - bit) * half)
        for index, (kept_ref, came_ref) in enumerate(zip(kept_refs, came_refs)):
            at = slice(index * width, (index + 1) * width)
            kept_out[:, at] = kept_ref[mine] + came_ref[mine].astype(jnp.float32)
            sent_out[:, at] = (kept_ref[other] + came_ref[other].astype(jnp.float32)).astype(jnp.bfloat16)

    for bit in range(2):
        pl.when(lax.axis_index("tensor") >> level & 1 == bit)(functools.partial(put, bit))


def halve(kept, came, level, tokens=()):
    rows, columns = kept[0].shape
    half, columns = rows // 2, columns * len(kept)
    if half % 16:
        total = jnp.concatenate(kept, axis=1) + jnp.concatenate(came, axis=1).astype(jnp.float32)
        bit = lax.axis_index("tensor") >> level & 1
        sent = lax.dynamic_slice_in_dim(total, (1 - bit) * half, half, 0).astype(jnp.bfloat16)
        return sent, lax.dynamic_slice_in_dim(total, bit * half, half, 0)
    return pl.pallas_call(
        functools.partial(halve_body, level, len(kept)),
        out_shape=[
            jax.ShapeDtypeStruct((half, columns), jnp.bfloat16),
            jax.ShapeDtypeStruct((half, columns), jnp.float32),
        ],
        in_specs=[VMEM] * (2 * len(kept)) + [ANY] * len(tokens),
        out_specs=[VMEM, VMEM],
        compiler_params=PARAMS,
        cost_estimate=SMALL,
    )(*kept, *came, *tokens)


def encode_body(begin, lane, last, kept_ref, came_ref, scales_ref, flips_ref, rotation_ref, *refs):
    out_ref = refs[-1 if last else -2]
    rows, columns = kept_ref.shape
    half = flips_ref.shape[1] // 2
    blocks = columns // BLOCK
    lanes = lax.broadcasted_iota(jnp.int32, (rows, BLOCK), 1)
    scales = scales_ref[...]
    totals = []
    for block in range(blocks):
        at = slice(block * BLOCK, (block + 1) * BLOCK)
        place = lax.axis_index("sub") * half + begin + block * BLOCK
        flips = flips_ref[:, pl.ds(pl.multiple_of(place, BLOCK), BLOCK)]
        totals.append((kept_ref[:, at] + came_ref[:, at].astype(jnp.float32)) * flips)
    rotated = jnp.dot(
        jnp.concatenate(totals, axis=0),
        rotation_ref[...],
        precision=lax.Precision.HIGHEST,
        preferred_element_type=jnp.float32,
    )
    largest = jnp.max(jnp.abs(rotated), axis=1, keepdims=True)
    scale = (largest + epsilon).astype(jnp.bfloat16).astype(jnp.float32)
    codes = rotated / scale
    for block in range(blocks):
        part = slice(block * rows, (block + 1) * rows)
        out_ref[:, block * BLOCK : (block + 1) * BLOCK] = codes[part].astype(jnp.bfloat16)
        scales = jnp.where(lanes == lane + block, scale[part], scales)
    if last:
        out_ref[:, columns:] = scales.astype(jnp.bfloat16)
    else:
        refs[-1][...] = scales


def encode(kept, came, begin, scales, lane, last, flips, rotation, tokens=()):
    rows, columns = kept.shape
    out_shape = [jax.ShapeDtypeStruct((rows, columns + (BLOCK if last else 0)), jnp.bfloat16)]
    if not last:
        out_shape.append(jax.ShapeDtypeStruct((rows, BLOCK), jnp.float32))
    return pl.pallas_call(
        functools.partial(encode_body, begin, lane, last),
        out_shape=out_shape,
        in_specs=[VMEM] * 5 + [ANY] * len(tokens),
        out_specs=[VMEM] * len(out_shape),
        compiler_params=PARAMS,
        cost_estimate=SMALL,
    )(kept, came, scales, flips, rotation, *tokens)


def rank_of(index, count):
    levels = count.bit_length() - 1
    return sum((index >> level & 1) << (levels - 1 - level) for level in range(levels))


def block_of(other, place, places, blocks):
    sub = lax.axis_index("sub")
    sub = 1 - sub if other else sub
    return lax.rem(lax.axis_index("seq") - (sub * places + place) + blocks, blocks)


def choose_body(blocks, count, rows, tops, width, begins, other, places, scales, lane, *refs):
    out_ref = refs[-1]

    def put(block, place):
        for piece in range(count):
            row = (place * count + rank_of(lax.axis_index("tensor") ^ piece, count)) * rows
            here = pl.ds(pl.multiple_of(row, rows), rows)
            begin = begins[block]
            ref, top = refs[block * count + piece], tops[block * count + piece]
            out_ref[here, :width] = ref[top : top + rows, begin : begin + width]
            ref, top = refs[(blocks - 1) * count + piece], tops[(blocks - 1) * count + piece]
            at = ref.shape[1] - BLOCK + block * scales + lane
            out_ref[here, width : width + width // BLOCK] = ref[top : top + rows, at : at + width // BLOCK]

    for place in range(places):
        for block in range(blocks):
            pl.when(block_of(other, place, places, blocks) == block)(functools.partial(put, block, place))


def choose(results, group, width, other, places, scales):
    picked = [result[0] if len(result) == 1 else result[group] for result in results]
    begins = [group * width if len(result) == 1 else 0 for result in results]
    lane = group * (width // BLOCK)
    count = len(picked[0])
    picked = [[piece if isinstance(piece, tuple) else (piece, 0) for piece in pieces] for pieces in picked]
    rows = picked[0][0][0].shape[0]
    columns = width + BLOCK
    if rows % 16:
        blocks = []
        for block, (pieces, begin) in enumerate(zip(picked, begins)):
            held = jnp.zeros((count * rows, columns), jnp.bfloat16)
            for index, (piece, top) in enumerate(pieces):
                part = piece[top : top + rows, begin : begin + width]
                scaled, top = picked[-1][index]
                at = scaled.shape[1] - BLOCK + block * scales + lane
                scale = scaled[top : top + rows, at : at + width // BLOCK]
                part = jnp.concatenate([part, jnp.pad(scale, ((0, 0), (0, BLOCK - width // BLOCK)))], axis=1)
                row = rank_of(lax.axis_index("tensor") ^ index, count) * rows
                held = lax.dynamic_update_slice_in_dim(held, part, row, 0)
            blocks.append(held)
        stacked = jnp.stack(blocks)
        return jnp.concatenate([stacked[block_of(other, place, places, len(blocks))] for place in range(places)])
    operands = [piece for pieces in picked for piece, _ in pieces]
    tops = [top for pieces in picked for _, top in pieces]
    return pl.pallas_call(
        functools.partial(choose_body, len(picked), count, rows, tops, width, begins, other, places, scales, lane),
        out_shape=jax.ShapeDtypeStruct((places * count * rows, columns), jnp.bfloat16),
        in_specs=[VMEM] * len(operands),
        out_specs=VMEM,
        compiler_params=PARAMS,
        cost_estimate=SMALL,
    )(*operands)


def place_body(mine, half, width, count, held, *refs):
    refs = refs[held:]
    scaled = len(refs) > count + 2
    codes_ref, sems = refs[2 * count if scaled else count], refs[-1]
    sub = lax.axis_index("sub")
    side = sub if mine else 1 - sub

    def put(core):
        copies = [
            pltpu.make_async_copy(
                refs[group].at[:, :width], codes_ref.at[:, pl.ds(core * half + group * width, width)], sems.at[group]
            )
            for group in range(count)
        ]
        for copy in copies:
            copy.start()
        if scaled:
            out_ref, flat = refs[2 * count + 1 : 2 * count + 3]
            order = refs[count : 2 * count] + refs[:count] if core else refs[: 2 * count]
            scales = [ref[:, width : width + width // BLOCK].astype(jnp.float32) for ref in order]
            flat[...] = jnp.concatenate(scales, axis=1).T.astype(jnp.bfloat16)
            copies.append(pltpu.make_async_copy(flat, out_ref, sems.at[count]))
            copies[-1].start()
        for copy in copies:
            copy.wait()

    for core in range(2):
        pl.when(side == core)(functools.partial(put, core))


def put_codes(arrays, width, half, mine, codes=None, mine_too=()):
    rows = arrays[0].shape[0]
    operands = list(arrays) + list(mine_too)
    out_shape = [jax.ShapeDtypeStruct((rows, 2 * half), jnp.bfloat16)]
    scratch = [pltpu.SemaphoreType.DMA((len(arrays) + 1,))]
    if mine_too:
        out_shape.append(jax.ShapeDtypeStruct((2 * half // BLOCK, rows), jnp.bfloat16))
        scratch.insert(0, pltpu.VMEM((2 * half // BLOCK, rows), jnp.bfloat16))
    held = [] if codes is None else [codes]
    return pl.pallas_call(
        functools.partial(place_body, mine, half, width, len(arrays), len(held)),
        out_shape=out_shape,
        in_specs=[HBM] * len(held) + [VMEM] * len(operands),
        out_specs=[HBM] * len(out_shape),
        input_output_aliases={0: 0} if held else {},
        scratch_shapes=scratch,
        compiler_params=PARAMS,
        cost_estimate=SMALL,
    )(*held, *operands)


def cut(depth):
    if depth % UNIT or depth < 16 * UNIT:
        return [depth]
    units = depth // UNIT
    sizes = [max(1, units * share // 26) for share in SHARES]
    return [size * UNIT for size in sizes + [units - sum(sizes)]]


def shards(hidden, down_weight, sign_bits):
    tensor_count = lax.axis_size("tensor")
    seq_count = lax.axis_size("seq")
    sub_count = lax.axis_size("sub")
    depth = hidden.shape[1]
    half = down_weight.shape[1] // sub_count
    per_sub = seq_count // sub_count
    levels = tensor_count.bit_length() - 1
    wide, wide_chunk, wide_merged = (min(size, half // GROUPS) for size in (256, 512, 1024))
    flips = (2 * sign_bits - 1).astype(jnp.float32)[None, :]
    rotation = jnp.asarray(hadamard(BLOCK))

    def swap(values):
        return lax.ppermute(values, "sub", [(0, 1), (1, 0)])

    def exchange(values, level):
        return lax.ppermute(values, "tensor", [(t, t ^ 1 << level) for t in range(tensor_count)])

    def reduce(halves, begin, block, base, last):
        tokens = (yield None) or []
        kept, came = halves[1::2], [swap(sent) for sent in halves[::2]]
        for level in range(levels):
            sent, held = halve(kept, came, level, tokens)
            tokens = (yield sent) or []
            kept, came = [held], [exchange(sent, level)]
        packed, *base[:] = encode(
            kept[0], came[0], begin, base[0], (block * half + begin) // BLOCK, last, flips, rotation, tokens
        )
        yield packed

    def spread(packed):
        pieces = {0: packed}
        for level in reversed(range(levels)):
            for index in list(pieces):
                pieces[index ^ 1 << level] = exchange(pieces[index], level)
        return [pieces[index] for index in range(tensor_count)]

    zeros = jnp.zeros((hidden.shape[0] // tensor_count, BLOCK), jnp.float32)
    sizes = cut(depth)
    places = [sum(sizes[:index]) for index in range(len(sizes))]
    parts = slices_of(hidden, list(zip(places, sizes)))

    def from_seq(part, shift):
        return lax.ppermute(part, "seq", [(s, (s + shift) % seq_count) for s in range(seq_count)])

    arrivals = [[from_seq(part, shift) for part in parts] for shift in range(1, seq_count)]

    if len(sizes) == 1:
        outs = multiply([[parts[0]], [arrivals[0][0]]], down_weight, 0, [None, None], [True, True], wide_chunk)
        base = [zeros]
        reduced = [list(reduce(outs[:2], 0, 0, base, False))[-1], list(reduce(outs[2:], 0, 1, base, seq_count == 2))[-1]]
        for block, arrived in enumerate(arrivals[1:], 2):
            outs = multiply([[arrived[0]]], down_weight, 0, [None], [True], wide_chunk)
            reduced.append(list(reduce(outs, 0, block, base, block == seq_count - 1))[-1])
        results = [[spread(packed)] for packed in reduced]
    else:
        (own,) = multiply([parts[1:]], down_weight, sizes[0], [None], [False], wide, tokens=parts[:1])
        *halves, total = multiply(
            [[parts[0]], [arrivals[0][0]]], down_weight, 0, [own, None], [True, False], wide_merged, groups=GROUPS
        )
        own_base = [zeros]
        own_steps = reduce(halves, 0, 0, own_base, False)
        next(own_steps)
        tokens = [own_steps.send([arrivals[0][1]])]
        results = []
        for shift, arrived in enumerate(arrivals):
            if shift:
                (total,) = multiply([[arrived[0]]], down_weight, 0, [None], [False], wide_chunk)
            for index in range(1, len(sizes) - 1):
                (total,) = multiply(
                    [[arrived[index]]], down_weight, places[index], [total], [False], wide_chunk, tokens=tokens
                )
                if not results:
                    step = own_steps.send([total])
                    tokens = [step]
                    if own_base[0] is not zeros:
                        results.append([spread(step)])
            if not results:
                results.append([spread(list(own_steps)[-1])])
            if shift == 0:
                bases = [list(own_base) for _ in range(GROUPS)]
            outs = multiply(
                [[arrived[-1]]], down_weight, places[-1], [total], [True], wide_chunk,
                groups=GROUPS, tokens=tokens,
            )
            remote, all_steps = [], []
            for group in range(GROUPS):
                sent, kept = outs[2 * group : 2 * group + 2]
                if group == GROUPS - 1 and shift == 0 and levels > 1:
                    sent = gate(sent, [results[0][0][1], results[0][0][1 << levels - 1]])
                all_steps.append(reduce([sent, kept], group * half // GROUPS, shift + 1, bases[group], shift == seq_count - 2))
                next(all_steps[-1])
            last = []
            for level in range(levels + 1):
                for group, steps in enumerate(all_steps):
                    wait = list(last) if group == 0 else []
                    if group == GROUPS - 1 and level == levels and shift == 0:
                        wait += results[0][0][1:]
                    step = steps.send(wait)
                    if level == levels:
                        remote.append(spread(step))
                last = [step]
            results.append(remote)
            tokens = []

    groups = max(len(result) for result in results)
    width = half // groups

    def chosen(other):
        return [choose(results, group, width, other, per_sub, half // BLOCK) for group in range(groups)]

    came = [swap(values) for values in chosen(True)]
    mine = chosen(False)
    (codes,) = put_codes(mine, width, half, True)
    codes, flat = put_codes(came, width, half, False, codes, mine)
    return codes, flat.T


def solution(mesh):
    return jax.shard_map(
        shards,
        mesh=mesh,
        in_specs=(P(("groups", "seq"), ("tensor", "sub")), P(("tensor", "sub"), "seq"), P("seq")),
        out_specs=(P(("groups", "sub"), "seq"), P(("groups", "sub"), "seq")),
        check_vma=False,
    )
```

```python
import functools
import math

import jax
import jax.numpy as jnp
import numpy as np
from jax import lax
from jax.experimental import pallas as pl
from jax.experimental.pallas import tpu as pltpu
from jax.sharding import PartitionSpec as P

BLOCK = 128
UNIT = 256
GROUPS = 2
VMEM_LIMIT = 6 * 2**20
SHARES = (8, 7, 6)
epsilon = 1e-06

SMALL = pl.CostEstimate(flops=1, bytes_accessed=1, transcendentals=0)
PARAMS = pltpu.CompilerParams(vmem_limit_bytes=VMEM_LIMIT)
VMEM = pl.BlockSpec(memory_space=pltpu.VMEM)
ANY = pl.BlockSpec(memory_space=pl.ANY)
HBM = pl.BlockSpec(memory_space=pltpu.HBM)


def hadamard(order):
    indices = np.arange(order)
    parity = np.zeros((order, order), np.int64)
    for position in range(order.bit_length() - 1):
        parity = parity + (indices[:, None] >> position & 1) * (indices[None, :] >> position & 1)
    return ((1 - 2 * (parity % 2)) / math.sqrt(order)).astype(np.float32)


def slice_body(places, in_ref, *refs):
    out_refs, arrived = refs[:-1], refs[-1]
    copies = [
        pltpu.make_async_copy(in_ref.at[:, at : at + size], out_ref, arrived.at[index])
        for index, ((at, size), out_ref) in enumerate(zip(places, out_refs))
    ]
    for copy in copies:
        copy.start()
    for copy in copies:
        copy.wait()


def slices_of(values, places):
    return pl.pallas_call(
        functools.partial(slice_body, places),
        out_shape=[jax.ShapeDtypeStruct((values.shape[0], size), values.dtype) for _, size in places],
        in_specs=[HBM],
        out_specs=[VMEM] * len(places),
        scratch_shapes=[pltpu.SemaphoreType.DMA((len(places),))],
        compiler_params=PARAMS,
        cost_estimate=SMALL,
    )(values)


def multiply_body(spans, has_totals, splits, row, groups, only, *refs):
    lefts = [refs[begin:end] for begin, end in spans]
    refs = refs[spans[-1][1] :]
    w_ref, refs = refs[0], refs[1:]
    total_refs, refs = list(refs[: sum(has_totals)]), refs[sum(has_totals) :]
    buffer, arrived = refs[-2:]
    outs_of_split = 2 if only is not None else 2 * groups
    out_count = sum(outs_of_split if split else 1 for split in splits)
    out_refs = refs[-2 - out_count : -2]
    steps, depth, wide = buffer.shape
    rows = lefts[0][0].shape[0]
    in_half = w_ref.shape[1] // wide // 2
    first = in_half // groups
    here = lax.axis_index("sub")

    def column(n):
        if not any(splits):
            return n
        group, place = n // (2 * first), n % (2 * first)
        group = group if only is None else only
        side, place = (here, place - first) if place >= first else (1 - here, place)
        return side * in_half + group * first + place

    def at(block):
        return pl.ds(pl.multiple_of(block * wide, wide), wide)

    def copy(n):
        return pltpu.make_async_copy(w_ref.at[pl.ds(row, depth), at(column(n))], buffer.at[n], arrived.at[n])

    def step(n):
        copy(n).wait()
        product, begin = None, 0
        for index in range(len(lefts[0])):
            parts = [left[index][...] for left in lefts]
            left = parts[0] if len(parts) == 1 else jnp.concatenate(parts, axis=0)
            end = begin + left.shape[1]
            part = jnp.dot(left, buffer[n, begin:end], preferred_element_type=jnp.float32)
            product = part if product is None else product + part
            begin = end
        totals, outs = list(total_refs), list(out_refs)
        for index in range(len(lefts)):
            value = product[index * rows : (index + 1) * rows]
            if has_totals[index]:
                value = value + totals.pop(0)[:, at(column(n))]
            if splits[index]:
                group, place = n // (2 * first), n % (2 * first)
                out_ref = outs[2 * group + place // first]
                begin = place % first * wide
                out_ref[:, begin : begin + wide] = value.astype(out_ref.dtype)
                outs = outs[outs_of_split:]
            else:
                outs.pop(0)[:, at(column(n))] = value

    for n in range(steps):
        copy(n).start()
    if any(splits):
        for n in range(steps):
            step(n)
    else:
        pl.loop(0, steps)(step)


def multiply(lefts, weight, row, totals, splits, wide, groups=1, only=None, tokens=()):
    rows = lefts[0][0].shape[0]
    depth = sum(part.shape[1] for part in lefts[0])
    columns = weight.shape[1]
    steps = columns // wide // (1 if only is None else groups)
    spans = [(index * len(left), (index + 1) * len(left)) for index, left in enumerate(lefts)]
    held = [total for total in totals if total is not None]
    out_shape = []
    for split in splits:
        if split:
            out_shape += [
                jax.ShapeDtypeStruct((rows, columns // 2 // groups), jnp.bfloat16),
                jax.ShapeDtypeStruct((rows, columns // 2 // groups), jnp.float32),
            ] * (groups if only is None else 1)
        else:
            out_shape.append(jax.ShapeDtypeStruct((rows, columns), jnp.float32))
    body = functools.partial(
        multiply_body, spans, [total is not None for total in totals], splits, row, groups, only
    )
    return pl.pallas_call(
        body,
        out_shape=out_shape,
        in_specs=[VMEM] * spans[-1][1] + [HBM] + [VMEM] * len(held) + [ANY] * len(tokens),
        out_specs=[VMEM] * len(out_shape),
        scratch_shapes=[
            pltpu.VMEM((steps, depth, wide), weight.dtype),
            pltpu.SemaphoreType.DMA((steps,)),
        ],
        compiler_params=pltpu.CompilerParams(
            vmem_limit_bytes=2 * steps * depth * wide + VMEM_LIMIT
        ),
        cost_estimate=SMALL,
    )(*[part for left in lefts for part in left], weight, *held, *tokens)


def gate(values, tokens):
    return pl.pallas_call(
        lambda *refs: None,
        out_shape=jax.ShapeDtypeStruct(values.shape, values.dtype),
        in_specs=[ANY] * (1 + len(tokens)),
        out_specs=ANY,
        input_output_aliases={0: 0},
        compiler_params=PARAMS,
        cost_estimate=SMALL,
    )(values, *tokens)


def halve_body(level, count, *refs):
    kept_refs, came_refs, (sent_out, kept_out) = refs[:count], refs[count : 2 * count], refs[-2:]
    half, columns = sent_out.shape
    width = columns // count

    def put(bit):
        mine, other = slice(bit * half, (bit + 1) * half), slice((1 - bit) * half, (2 - bit) * half)
        for index, (kept_ref, came_ref) in enumerate(zip(kept_refs, came_refs)):
            at = slice(index * width, (index + 1) * width)
            kept_out[:, at] = kept_ref[mine] + came_ref[mine].astype(jnp.float32)
            sent_out[:, at] = (kept_ref[other] + came_ref[other].astype(jnp.float32)).astype(jnp.bfloat16)

    for bit in range(2):
        pl.when(lax.axis_index("tensor") >> level & 1 == bit)(functools.partial(put, bit))


def halve(kept, came, level, tokens=()):
    rows, columns = kept[0].shape
    half, columns = rows // 2, columns * len(kept)
    if half % 16:
        total = jnp.concatenate(kept, axis=1) + jnp.concatenate(came, axis=1).astype(jnp.float32)
        bit = lax.axis_index("tensor") >> level & 1
        sent = lax.dynamic_slice_in_dim(total, (1 - bit) * half, half, 0).astype(jnp.bfloat16)
        return sent, lax.dynamic_slice_in_dim(total, bit * half, half, 0)
    return pl.pallas_call(
        functools.partial(halve_body, level, len(kept)),
        out_shape=[
            jax.ShapeDtypeStruct((half, columns), jnp.bfloat16),
            jax.ShapeDtypeStruct((half, columns), jnp.float32),
        ],
        in_specs=[VMEM] * (2 * len(kept)) + [ANY] * len(tokens),
        out_specs=[VMEM, VMEM],
        compiler_params=PARAMS,
        cost_estimate=SMALL,
    )(*kept, *came, *tokens)


def encode_body(begin, lane, last, kept_ref, came_ref, scales_ref, flips_ref, rotation_ref, *refs):
    out_ref = refs[-1 if last else -2]
    rows, columns = kept_ref.shape
    half = flips_ref.shape[1] // 2
    blocks = columns // BLOCK
    lanes = lax.broadcasted_iota(jnp.int32, (rows, BLOCK), 1)
    scales = scales_ref[...]
    totals = []
    for block in range(blocks):
        at = slice(block * BLOCK, (block + 1) * BLOCK)
        place = lax.axis_index("sub") * half + begin + block * BLOCK
        flips = flips_ref[:, pl.ds(pl.multiple_of(place, BLOCK), BLOCK)]
        totals.append((kept_ref[:, at] + came_ref[:, at].astype(jnp.float32)) * flips)
    rotated = jnp.dot(
        jnp.concatenate(totals, axis=0),
        rotation_ref[...],
        precision=lax.Precision.HIGHEST,
        preferred_element_type=jnp.float32,
    )
    largest = jnp.max(jnp.abs(rotated), axis=1, keepdims=True)
    scale = (largest + epsilon).astype(jnp.bfloat16).astype(jnp.float32)
    codes = rotated / scale
    for block in range(blocks):
        part = slice(block * rows, (block + 1) * rows)
        out_ref[:, block * BLOCK : (block + 1) * BLOCK] = codes[part].astype(jnp.bfloat16)
        scales = jnp.where(lanes == lane + block, scale[part], scales)
    if last:
        out_ref[:, columns:] = scales.astype(jnp.bfloat16)
    else:
        refs[-1][...] = scales


def encode(kept, came, begin, scales, lane, last, flips, rotation, tokens=()):
    rows, columns = kept.shape
    out_shape = [jax.ShapeDtypeStruct((rows, columns + (BLOCK if last else 0)), jnp.bfloat16)]
    if not last:
        out_shape.append(jax.ShapeDtypeStruct((rows, BLOCK), jnp.float32))
    return pl.pallas_call(
        functools.partial(encode_body, begin, lane, last),
        out_shape=out_shape,
        in_specs=[VMEM] * 5 + [ANY] * len(tokens),
        out_specs=[VMEM] * len(out_shape),
        compiler_params=PARAMS,
        cost_estimate=SMALL,
    )(kept, came, scales, flips, rotation, *tokens)


def rank_of(index, count):
    levels = count.bit_length() - 1
    return sum((index >> level & 1) << (levels - 1 - level) for level in range(levels))


def block_of(other, place, places, blocks):
    sub = lax.axis_index("sub")
    sub = 1 - sub if other else sub
    return lax.rem(lax.axis_index("seq") - (sub * places + place) + blocks, blocks)


def choose_body(blocks, count, rows, tops, width, begins, other, places, scales, lane, *refs):
    out_ref = refs[-1]

    def put(block, place):
        for piece in range(count):
            row = (place * count + rank_of(lax.axis_index("tensor") ^ piece, count)) * rows
            here = pl.ds(pl.multiple_of(row, rows), rows)
            begin = begins[block]
            ref, top = refs[block * count + piece], tops[block * count + piece]
            out_ref[here, :width] = ref[top : top + rows, begin : begin + width]
            ref, top = refs[(blocks - 1) * count + piece], tops[(blocks - 1) * count + piece]
            at = ref.shape[1] - BLOCK + block * scales + lane
            out_ref[here, width : width + width // BLOCK] = ref[top : top + rows, at : at + width // BLOCK]

    for place in range(places):
        for block in range(blocks):
            pl.when(block_of(other, place, places, blocks) == block)(functools.partial(put, block, place))


def choose(results, group, width, other, places, scales):
    picked = [result[0] if len(result) == 1 else result[group] for result in results]
    begins = [group * width if len(result) == 1 else 0 for result in results]
    lane = group * (width // BLOCK)
    count = len(picked[0])
    picked = [[piece if isinstance(piece, tuple) else (piece, 0) for piece in pieces] for pieces in picked]
    rows = picked[0][0][0].shape[0]
    columns = width + BLOCK
    if rows % 16:
        blocks = []
        for block, (pieces, begin) in enumerate(zip(picked, begins)):
            held = jnp.zeros((count * rows, columns), jnp.bfloat16)
            for index, (piece, top) in enumerate(pieces):
                part = piece[top : top + rows, begin : begin + width]
                scaled, top = picked[-1][index]
                at = scaled.shape[1] - BLOCK + block * scales + lane
                scale = scaled[top : top + rows, at : at + width // BLOCK]
                part = jnp.concatenate([part, jnp.pad(scale, ((0, 0), (0, BLOCK - width // BLOCK)))], axis=1)
                row = rank_of(lax.axis_index("tensor") ^ index, count) * rows
                held = lax.dynamic_update_slice_in_dim(held, part, row, 0)
            blocks.append(held)
        stacked = jnp.stack(blocks)
        return jnp.concatenate([stacked[block_of(other, place, places, len(blocks))] for place in range(places)])
    operands = [piece for pieces in picked for piece, _ in pieces]
    tops = [top for pieces in picked for _, top in pieces]
    return pl.pallas_call(
        functools.partial(choose_body, len(picked), count, rows, tops, width, begins, other, places, scales, lane),
        out_shape=jax.ShapeDtypeStruct((places * count * rows, columns), jnp.bfloat16),
        in_specs=[VMEM] * len(operands),
        out_specs=VMEM,
        compiler_params=PARAMS,
        cost_estimate=SMALL,
    )(*operands)


def place_body(mine, half, width, count, held, *refs):
    refs = refs[held:]
    scaled = len(refs) > count + 2
    codes_ref, sems = refs[2 * count if scaled else count], refs[-1]
    sub = lax.axis_index("sub")
    side = sub if mine else 1 - sub

    def put(core):
        copies = [
            pltpu.make_async_copy(
                refs[group].at[:, :width], codes_ref.at[:, pl.ds(core * half + group * width, width)], sems.at[group]
            )
            for group in range(count)
        ]
        for copy in copies:
            copy.start()
        if scaled:
            out_ref, flat = refs[2 * count + 1 : 2 * count + 3]
            order = refs[count : 2 * count] + refs[:count] if core else refs[: 2 * count]
            scales = [ref[:, width : width + width // BLOCK].astype(jnp.float32) for ref in order]
            flat[...] = jnp.concatenate(scales, axis=1).T.astype(jnp.bfloat16)
            copies.append(pltpu.make_async_copy(flat, out_ref, sems.at[count]))
            copies[-1].start()
        for copy in copies:
            copy.wait()

    for core in range(2):
        pl.when(side == core)(functools.partial(put, core))


def put_codes(arrays, width, half, mine, codes=None, mine_too=()):
    rows = arrays[0].shape[0]
    operands = list(arrays) + list(mine_too)
    out_shape = [jax.ShapeDtypeStruct((rows, 2 * half), jnp.bfloat16)]
    scratch = [pltpu.SemaphoreType.DMA((len(arrays) + 1,))]
    if mine_too:
        out_shape.append(jax.ShapeDtypeStruct((2 * half // BLOCK, rows), jnp.bfloat16))
        scratch.insert(0, pltpu.VMEM((2 * half // BLOCK, rows), jnp.bfloat16))
    held = [] if codes is None else [codes]
    return pl.pallas_call(
        functools.partial(place_body, mine, half, width, len(arrays), len(held)),
        out_shape=out_shape,
        in_specs=[HBM] * len(held) + [VMEM] * len(operands),
        out_specs=[HBM] * len(out_shape),
        input_output_aliases={0: 0} if held else {},
        scratch_shapes=scratch,
        compiler_params=PARAMS,
        cost_estimate=SMALL,
    )(*held, *operands)


def cut(depth):
    if depth % UNIT or depth < 16 * UNIT:
        return [depth]
    units = depth // UNIT
    sizes = [max(1, units * share // 26) for share in SHARES]
    return [size * UNIT for size in sizes + [units - sum(sizes)]]


def shards(hidden, down_weight, sign_bits):
    tensor_count = lax.axis_size("tensor")
    seq_count = lax.axis_size("seq")
    sub_count = lax.axis_size("sub")
    depth = hidden.shape[1]
    half = down_weight.shape[1] // sub_count
    per_sub = seq_count // sub_count
    levels = tensor_count.bit_length() - 1
    wide, wide_chunk, wide_merged = (min(size, half // GROUPS) for size in (256, 512, 1024))
    flips = (2 * sign_bits - 1).astype(jnp.float32)[None, :]
    rotation = jnp.asarray(hadamard(BLOCK))

    def swap(values):
        return lax.ppermute(values, "sub", [(0, 1), (1, 0)])

    def exchange(values, level):
        return lax.ppermute(values, "tensor", [(t, t ^ 1 << level) for t in range(tensor_count)])

    def reduce(halves, begin, block, base, last):
        tokens = (yield None) or []
        kept, came = halves[1::2], [swap(sent) for sent in halves[::2]]
        for level in range(levels):
            sent, held = halve(kept, came, level, tokens)
            tokens = (yield sent) or []
            kept, came = [held], [exchange(sent, level)]
        packed, *base[:] = encode(
            kept[0], came[0], begin, base[0], (block * half + begin) // BLOCK, last, flips, rotation, tokens
        )
        yield packed

    def spread(packed):
        pieces = {0: packed}
        for level in reversed(range(levels)):
            for index in list(pieces):
                pieces[index ^ 1 << level] = exchange(pieces[index], level)
        return [pieces[index] for index in range(tensor_count)]

    zeros = jnp.zeros((hidden.shape[0] // tensor_count, BLOCK), jnp.float32)
    sizes = cut(depth)
    places = [sum(sizes[:index]) for index in range(len(sizes))]
    parts = slices_of(hidden, list(zip(places, sizes)))

    def from_seq(part, shift):
        return lax.ppermute(part, "seq", [(s, (s + shift) % seq_count) for s in range(seq_count)])

    arrivals = [[from_seq(part, shift) for part in parts] for shift in range(1, seq_count)]

    if len(sizes) == 1:
        outs = multiply([[parts[0]], [arrivals[0][0]]], down_weight, 0, [None, None], [True, True], wide_chunk)
        base = [zeros]
        reduced = [list(reduce(outs[:2], 0, 0, base, False))[-1], list(reduce(outs[2:], 0, 1, base, seq_count == 2))[-1]]
        for block, arrived in enumerate(arrivals[1:], 2):
            outs = multiply([[arrived[0]]], down_weight, 0, [None], [True], wide_chunk)
            reduced.append(list(reduce(outs, 0, block, base, block == seq_count - 1))[-1])
        results = [[spread(packed)] for packed in reduced]
    else:
        (own,) = multiply([parts[1:]], down_weight, sizes[0], [None], [False], wide, tokens=parts[:1])
        *halves, total = multiply(
            [[parts[0]], [arrivals[0][0]]], down_weight, 0, [own, None], [True, False], wide_merged, groups=GROUPS
        )
        own_base = [zeros]
        own_steps = reduce(halves, 0, 0, own_base, False)
        next(own_steps)
        tokens = [own_steps.send([arrivals[0][1]])]
        results = []
        for shift, arrived in enumerate(arrivals):
            if shift:
                (total,) = multiply([[arrived[0]]], down_weight, 0, [None], [False], wide_chunk)
            for index in range(1, len(sizes) - 1):
                (total,) = multiply(
                    [[arrived[index]]], down_weight, places[index], [total], [False], wide_chunk, tokens=tokens
                )
                if not results:
                    step = own_steps.send([total])
                    tokens = [step]
                    if own_base[0] is not zeros:
                        results.append([spread(step)])
            if not results:
                results.append([spread(list(own_steps)[-1])])
            if shift == 0:
                bases = [list(own_base) for _ in range(GROUPS)]
            outs = multiply(
                [[arrived[-1]]], down_weight, places[-1], [total], [True], wide_chunk,
                groups=GROUPS, tokens=tokens,
            )
            remote, all_steps = [], []
            for group in range(GROUPS):
                sent, kept = outs[2 * group : 2 * group + 2]
                all_steps.append(reduce([sent, kept], group * half // GROUPS, shift + 1, bases[group], shift == seq_count - 2))
                next(all_steps[-1])
            last = []
            for level in range(levels + 1):
                for group, steps in enumerate(all_steps):
                    wait = list(last) if group == 0 else []
                    if group == 0 and level == levels and shift == 0:
                        wait += [results[0][0][1 << place] for place in range(levels)]
                    step = steps.send(wait)
                    if level == levels:
                        remote.append(spread(step))
                last = [step]
            results.append(remote)
            tokens = []

    groups = max(len(result) for result in results)
    width = half // groups

    def chosen(other):
        return [choose(results, group, width, other, per_sub, half // BLOCK) for group in range(groups)]

    came = [swap(values) for values in chosen(True)]
    mine = chosen(False)
    (codes,) = put_codes(mine, width, half, True)
    codes, flat = put_codes(came, width, half, False, codes, mine)
    return codes, flat.T


def solution(mesh):
    return jax.shard_map(
        shards,
        mesh=mesh,
        in_specs=(P(("groups", "seq"), ("tensor", "sub")), P(("tensor", "sub"), "seq"), P("seq")),
        out_specs=(P(("groups", "sub"), "seq"), P(("groups", "sub"), "seq")),
        check_vma=False,
    )
```

```python
import functools
import math

import jax
import jax.numpy as jnp
import numpy as np
from jax import lax
from jax.experimental import pallas as pl
from jax.experimental.pallas import tpu as pltpu
from jax.sharding import PartitionSpec as P

BLOCK = 128
UNIT = 256
GROUPS = 2
VMEM_LIMIT = 6 * 2**20
SHARES = (8, 7, 6)
epsilon = 1e-06

SMALL = pl.CostEstimate(flops=1, bytes_accessed=1, transcendentals=0)
PARAMS = pltpu.CompilerParams(vmem_limit_bytes=VMEM_LIMIT)
VMEM = pl.BlockSpec(memory_space=pltpu.VMEM)
ANY = pl.BlockSpec(memory_space=pl.ANY)
HBM = pl.BlockSpec(memory_space=pltpu.HBM)


def hadamard(order):
    indices = np.arange(order)
    parity = np.zeros((order, order), np.int64)
    for position in range(order.bit_length() - 1):
        parity = parity + (indices[:, None] >> position & 1) * (indices[None, :] >> position & 1)
    return ((1 - 2 * (parity % 2)) / math.sqrt(order)).astype(np.float32)


def slice_body(places, in_ref, *refs):
    out_refs, arrived = refs[:-1], refs[-1]
    copies = [
        pltpu.make_async_copy(in_ref.at[:, at : at + size], out_ref, arrived.at[index])
        for index, ((at, size), out_ref) in enumerate(zip(places, out_refs))
    ]
    for copy in copies:
        copy.start()
    for copy in copies:
        copy.wait()


def slices_of(values, places):
    return pl.pallas_call(
        functools.partial(slice_body, places),
        out_shape=[jax.ShapeDtypeStruct((values.shape[0], size), values.dtype) for _, size in places],
        in_specs=[HBM],
        out_specs=[VMEM] * len(places),
        scratch_shapes=[pltpu.SemaphoreType.DMA((len(places),))],
        compiler_params=PARAMS,
        cost_estimate=SMALL,
    )(values)


def multiply_body(spans, has_totals, splits, row, groups, only, *refs):
    lefts = [refs[begin:end] for begin, end in spans]
    refs = refs[spans[-1][1] :]
    w_ref, refs = refs[0], refs[1:]
    total_refs, refs = list(refs[: sum(has_totals)]), refs[sum(has_totals) :]
    buffer, arrived = refs[-2:]
    outs_of_split = 2 if only is not None else 2 * groups
    out_count = sum(outs_of_split if split else 1 for split in splits)
    out_refs = refs[-2 - out_count : -2]
    steps, depth, wide = buffer.shape
    rows = lefts[0][0].shape[0]
    in_half = w_ref.shape[1] // wide // 2
    first = in_half // groups
    here = lax.axis_index("sub")

    def column(n):
        if not any(splits):
            return n
        group, place = n // (2 * first), n % (2 * first)
        group = group if only is None else only
        side, place = (here, place - first) if place >= first else (1 - here, place)
        return side * in_half + group * first + place

    def at(block):
        return pl.ds(pl.multiple_of(block * wide, wide), wide)

    def copy(n):
        return pltpu.make_async_copy(w_ref.at[pl.ds(row, depth), at(column(n))], buffer.at[n], arrived.at[n])

    def step(n):
        copy(n).wait()
        product, begin = None, 0
        for index in range(len(lefts[0])):
            parts = [left[index][...] for left in lefts]
            left = parts[0] if len(parts) == 1 else jnp.concatenate(parts, axis=0)
            end = begin + left.shape[1]
            part = jnp.dot(left, buffer[n, begin:end], preferred_element_type=jnp.float32)
            product = part if product is None else product + part
            begin = end
        totals, outs = list(total_refs), list(out_refs)
        for index in range(len(lefts)):
            value = product[index * rows : (index + 1) * rows]
            if has_totals[index]:
                value = value + totals.pop(0)[:, at(column(n))]
            if splits[index]:
                group, place = n // (2 * first), n % (2 * first)
                out_ref = outs[2 * group + place // first]
                begin = place % first * wide
                out_ref[:, begin : begin + wide] = value.astype(out_ref.dtype)
                outs = outs[outs_of_split:]
            else:
                outs.pop(0)[:, at(column(n))] = value

    for n in range(steps):
        copy(n).start()
    if any(splits):
        for n in range(steps):
            step(n)
    else:
        pl.loop(0, steps)(step)


def multiply(lefts, weight, row, totals, splits, wide, groups=1, only=None, tokens=()):
    rows = lefts[0][0].shape[0]
    depth = sum(part.shape[1] for part in lefts[0])
    columns = weight.shape[1]
    steps = columns // wide // (1 if only is None else groups)
    spans = [(index * len(left), (index + 1) * len(left)) for index, left in enumerate(lefts)]
    held = [total for total in totals if total is not None]
    out_shape = []
    for split in splits:
        if split:
            out_shape += [
                jax.ShapeDtypeStruct((rows, columns // 2 // groups), jnp.bfloat16),
                jax.ShapeDtypeStruct((rows, columns // 2 // groups), jnp.float32),
            ] * (groups if only is None else 1)
        else:
            out_shape.append(jax.ShapeDtypeStruct((rows, columns), jnp.float32))
    body = functools.partial(
        multiply_body, spans, [total is not None for total in totals], splits, row, groups, only
    )
    return pl.pallas_call(
        body,
        out_shape=out_shape,
        in_specs=[VMEM] * spans[-1][1] + [HBM] + [VMEM] * len(held) + [ANY] * len(tokens),
        out_specs=[VMEM] * len(out_shape),
        scratch_shapes=[
            pltpu.VMEM((steps, depth, wide), weight.dtype),
            pltpu.SemaphoreType.DMA((steps,)),
        ],
        compiler_params=pltpu.CompilerParams(
            vmem_limit_bytes=2 * steps * depth * wide + VMEM_LIMIT
        ),
        cost_estimate=SMALL,
    )(*[part for left in lefts for part in left], weight, *held, *tokens)


def gate(values, tokens):
    return pl.pallas_call(
        lambda *refs: None,
        out_shape=jax.ShapeDtypeStruct(values.shape, values.dtype),
        in_specs=[ANY] * (1 + len(tokens)),
        out_specs=ANY,
        input_output_aliases={0: 0},
        compiler_params=PARAMS,
        cost_estimate=SMALL,
    )(values, *tokens)


def halve_body(level, count, *refs):
    kept_refs, came_refs, (sent_out, kept_out) = refs[:count], refs[count : 2 * count], refs[-2:]
    half, columns = sent_out.shape
    width = columns // count

    def put(bit):
        mine, other = slice(bit * half, (bit + 1) * half), slice((1 - bit) * half, (2 - bit) * half)
        for index, (kept_ref, came_ref) in enumerate(zip(kept_refs, came_refs)):
            at = slice(index * width, (index + 1) * width)
            kept_out[:, at] = kept_ref[mine] + came_ref[mine].astype(jnp.float32)
            sent_out[:, at] = (kept_ref[other] + came_ref[other].astype(jnp.float32)).astype(jnp.bfloat16)

    for bit in range(2):
        pl.when(lax.axis_index("tensor") >> level & 1 == bit)(functools.partial(put, bit))


def halve(kept, came, level, tokens=()):
    rows, columns = kept[0].shape
    half, columns = rows // 2, columns * len(kept)
    if half % 16:
        total = jnp.concatenate(kept, axis=1) + jnp.concatenate(came, axis=1).astype(jnp.float32)
        bit = lax.axis_index("tensor") >> level & 1
        sent = lax.dynamic_slice_in_dim(total, (1 - bit) * half, half, 0).astype(jnp.bfloat16)
        return sent, lax.dynamic_slice_in_dim(total, bit * half, half, 0)
    return pl.pallas_call(
        functools.partial(halve_body, level, len(kept)),
        out_shape=[
            jax.ShapeDtypeStruct((half, columns), jnp.bfloat16),
            jax.ShapeDtypeStruct((half, columns), jnp.float32),
        ],
        in_specs=[VMEM] * (2 * len(kept)) + [ANY] * len(tokens),
        out_specs=[VMEM, VMEM],
        compiler_params=PARAMS,
        cost_estimate=SMALL,
    )(*kept, *came, *tokens)


def encode_body(begin, lane, last, kept_ref, came_ref, scales_ref, flips_ref, rotation_ref, *refs):
    out_ref = refs[-1 if last else -2]
    rows, columns = kept_ref.shape
    half = flips_ref.shape[1] // 2
    blocks = columns // BLOCK
    lanes = lax.broadcasted_iota(jnp.int32, (rows, BLOCK), 1)
    scales = scales_ref[...]
    totals = []
    for block in range(blocks):
        at = slice(block * BLOCK, (block + 1) * BLOCK)
        place = lax.axis_index("sub") * half + begin + block * BLOCK
        flips = flips_ref[:, pl.ds(pl.multiple_of(place, BLOCK), BLOCK)]
        totals.append((kept_ref[:, at] + came_ref[:, at].astype(jnp.float32)) * flips)
    rotated = jnp.dot(
        jnp.concatenate(totals, axis=0),
        rotation_ref[...],
        precision=lax.Precision.HIGHEST,
        preferred_element_type=jnp.float32,
    )
    largest = jnp.max(jnp.abs(rotated), axis=1, keepdims=True)
    scale = (largest + epsilon).astype(jnp.bfloat16).astype(jnp.float32)
    codes = rotated / scale
    for block in range(blocks):
        part = slice(block * rows, (block + 1) * rows)
        out_ref[:, block * BLOCK : (block + 1) * BLOCK] = codes[part].astype(jnp.bfloat16)
        scales = jnp.where(lanes == lane + block, scale[part], scales)
    if last:
        out_ref[:, columns:] = scales.astype(jnp.bfloat16)
    else:
        refs[-1][...] = scales


def encode(kept, came, begin, scales, lane, last, flips, rotation, tokens=()):
    rows, columns = kept.shape
    out_shape = [jax.ShapeDtypeStruct((rows, columns + (BLOCK if last else 0)), jnp.bfloat16)]
    if not last:
        out_shape.append(jax.ShapeDtypeStruct((rows, BLOCK), jnp.float32))
    return pl.pallas_call(
        functools.partial(encode_body, begin, lane, last),
        out_shape=out_shape,
        in_specs=[VMEM] * 5 + [ANY] * len(tokens),
        out_specs=[VMEM] * len(out_shape),
        compiler_params=PARAMS,
        cost_estimate=SMALL,
    )(kept, came, scales, flips, rotation, *tokens)


def rank_of(index, count):
    levels = count.bit_length() - 1
    return sum((index >> level & 1) << (levels - 1 - level) for level in range(levels))


def block_of(other, place, places, blocks):
    sub = lax.axis_index("sub")
    sub = 1 - sub if other else sub
    return lax.rem(lax.axis_index("seq") - (sub * places + place) + blocks, blocks)


def choose_body(blocks, count, rows, tops, width, begins, other, places, scales, lane, *refs):
    out_ref = refs[-1]

    def put(block, place):
        for piece in range(count):
            row = (place * count + rank_of(lax.axis_index("tensor") ^ piece, count)) * rows
            here = pl.ds(pl.multiple_of(row, rows), rows)
            begin = begins[block]
            ref, top = refs[block * count + piece], tops[block * count + piece]
            out_ref[here, :width] = ref[top : top + rows, begin : begin + width]
            ref, top = refs[(blocks - 1) * count + piece], tops[(blocks - 1) * count + piece]
            at = ref.shape[1] - BLOCK + block * scales + lane
            out_ref[here, width : width + width // BLOCK] = ref[top : top + rows, at : at + width // BLOCK]

    for place in range(places):
        for block in range(blocks):
            pl.when(block_of(other, place, places, blocks) == block)(functools.partial(put, block, place))


def choose(results, group, width, other, places, scales):
    picked = [result[0] if len(result) == 1 else result[group] for result in results]
    begins = [group * width if len(result) == 1 else 0 for result in results]
    lane = group * (width // BLOCK)
    count = len(picked[0])
    picked = [[piece if isinstance(piece, tuple) else (piece, 0) for piece in pieces] for pieces in picked]
    rows = picked[0][0][0].shape[0]
    columns = width + BLOCK
    if rows % 16:
        blocks = []
        for block, (pieces, begin) in enumerate(zip(picked, begins)):
            held = jnp.zeros((count * rows, columns), jnp.bfloat16)
            for index, (piece, top) in enumerate(pieces):
                part = piece[top : top + rows, begin : begin + width]
                scaled, top = picked[-1][index]
                at = scaled.shape[1] - BLOCK + block * scales + lane
                scale = scaled[top : top + rows, at : at + width // BLOCK]
                part = jnp.concatenate([part, jnp.pad(scale, ((0, 0), (0, BLOCK - width // BLOCK)))], axis=1)
                row = rank_of(lax.axis_index("tensor") ^ index, count) * rows
                held = lax.dynamic_update_slice_in_dim(held, part, row, 0)
            blocks.append(held)
        stacked = jnp.stack(blocks)
        return jnp.concatenate([stacked[block_of(other, place, places, len(blocks))] for place in range(places)])
    operands = [piece for pieces in picked for piece, _ in pieces]
    tops = [top for pieces in picked for _, top in pieces]
    return pl.pallas_call(
        functools.partial(choose_body, len(picked), count, rows, tops, width, begins, other, places, scales, lane),
        out_shape=jax.ShapeDtypeStruct((places * count * rows, columns), jnp.bfloat16),
        in_specs=[VMEM] * len(operands),
        out_specs=VMEM,
        compiler_params=PARAMS,
        cost_estimate=SMALL,
    )(*operands)


def place_body(mine, half, width, count, held, *refs):
    refs = refs[held:]
    scaled = len(refs) > count + 2
    codes_ref, sems = refs[2 * count if scaled else count], refs[-1]
    sub = lax.axis_index("sub")
    side = sub if mine else 1 - sub

    def put(core):
        copies = [
            pltpu.make_async_copy(
                refs[group].at[:, :width], codes_ref.at[:, pl.ds(core * half + group * width, width)], sems.at[group]
            )
            for group in range(count)
        ]
        for copy in copies:
            copy.start()
        if scaled:
            out_ref, flat = refs[2 * count + 1 : 2 * count + 3]
            order = refs[count : 2 * count] + refs[:count] if core else refs[: 2 * count]
            scales = [ref[:, width : width + width // BLOCK].astype(jnp.float32) for ref in order]
            flat[...] = jnp.concatenate(scales, axis=1).T.astype(jnp.bfloat16)
            copies.append(pltpu.make_async_copy(flat, out_ref, sems.at[count]))
            copies[-1].start()
        for copy in copies:
            copy.wait()

    for core in range(2):
        pl.when(side == core)(functools.partial(put, core))


def put_codes(arrays, width, half, mine, codes=None, mine_too=()):
    rows = arrays[0].shape[0]
    operands = list(arrays) + list(mine_too)
    out_shape = [jax.ShapeDtypeStruct((rows, 2 * half), jnp.bfloat16)]
    scratch = [pltpu.SemaphoreType.DMA((len(arrays) + 1,))]
    if mine_too:
        out_shape.append(jax.ShapeDtypeStruct((2 * half // BLOCK, rows), jnp.bfloat16))
        scratch.insert(0, pltpu.VMEM((2 * half // BLOCK, rows), jnp.bfloat16))
    held = [] if codes is None else [codes]
    return pl.pallas_call(
        functools.partial(place_body, mine, half, width, len(arrays), len(held)),
        out_shape=out_shape,
        in_specs=[HBM] * len(held) + [VMEM] * len(operands),
        out_specs=[HBM] * len(out_shape),
        input_output_aliases={0: 0} if held else {},
        scratch_shapes=scratch,
        compiler_params=PARAMS,
        cost_estimate=SMALL,
    )(*held, *operands)


def cut(depth):
    if depth % UNIT or depth < 16 * UNIT:
        return [depth]
    units = depth // UNIT
    sizes = [max(1, units * share // 26) for share in SHARES]
    return [size * UNIT for size in sizes + [units - sum(sizes)]]


def shards(hidden, down_weight, sign_bits):
    tensor_count = lax.axis_size("tensor")
    seq_count = lax.axis_size("seq")
    sub_count = lax.axis_size("sub")
    depth = hidden.shape[1]
    half = down_weight.shape[1] // sub_count
    per_sub = seq_count // sub_count
    levels = tensor_count.bit_length() - 1
    wide, wide_chunk, wide_merged = (min(size, half // GROUPS) for size in (256, 256, 1024))
    flips = (2 * sign_bits - 1).astype(jnp.float32)[None, :]
    rotation = jnp.asarray(hadamard(BLOCK))

    def swap(values):
        return lax.ppermute(values, "sub", [(0, 1), (1, 0)])

    def exchange(values, level):
        return lax.ppermute(values, "tensor", [(t, t ^ 1 << level) for t in range(tensor_count)])

    def reduce(halves, begin, block, base, last):
        tokens = (yield None) or []
        kept, came = halves[1::2], [swap(sent) for sent in halves[::2]]
        for level in range(levels):
            sent, held = halve(kept, came, level, tokens)
            tokens = (yield sent) or []
            kept, came = [held], [exchange(sent, level)]
        packed, *base[:] = encode(
            kept[0], came[0], begin, base[0], (block * half + begin) // BLOCK, last, flips, rotation, tokens
        )
        yield packed

    def spread(packed):
        pieces = {0: packed}
        for level in reversed(range(levels)):
            for index in list(pieces):
                pieces[index ^ 1 << level] = exchange(pieces[index], level)
        return [pieces[index] for index in range(tensor_count)]

    zeros = jnp.zeros((hidden.shape[0] // tensor_count, BLOCK), jnp.float32)
    sizes = cut(depth)
    places = [sum(sizes[:index]) for index in range(len(sizes))]
    parts = slices_of(hidden, list(zip(places, sizes)))

    def from_seq(part, shift):
        return lax.ppermute(part, "seq", [(s, (s + shift) % seq_count) for s in range(seq_count)])

    arrivals = [[from_seq(part, shift) for part in parts] for shift in range(1, seq_count)]

    if len(sizes) == 1:
        outs = multiply([[parts[0]], [arrivals[0][0]]], down_weight, 0, [None, None], [True, True], wide_chunk)
        base = [zeros]
        reduced = [list(reduce(outs[:2], 0, 0, base, False))[-1], list(reduce(outs[2:], 0, 1, base, seq_count == 2))[-1]]
        for block, arrived in enumerate(arrivals[1:], 2):
            outs = multiply([[arrived[0]]], down_weight, 0, [None], [True], wide_chunk)
            reduced.append(list(reduce(outs, 0, block, base, block == seq_count - 1))[-1])
        results = [[spread(packed)] for packed in reduced]
    else:
        (own,) = multiply([parts[1:]], down_weight, sizes[0], [None], [False], wide, tokens=parts[:1])
        *halves, total = multiply(
            [[parts[0]], [arrivals[0][0]]], down_weight, 0, [own, None], [True, False], wide_merged, groups=GROUPS
        )
        own_base = [zeros]
        own_steps = reduce(halves, 0, 0, own_base, False)
        next(own_steps)
        tokens = [own_steps.send([arrivals[0][1]])]
        results = []
        for shift, arrived in enumerate(arrivals):
            if shift:
                (total,) = multiply([[arrived[0]]], down_weight, 0, [None], [False], wide_chunk)
            for index in range(1, len(sizes) - 1):
                (total,) = multiply(
                    [[arrived[index]]], down_weight, places[index], [total], [False], wide_chunk, tokens=tokens
                )
                if not results:
                    step = own_steps.send([total])
                    tokens = [step]
                    if own_base[0] is not zeros:
                        results.append([spread(step)])
            if not results:
                results.append([spread(list(own_steps)[-1])])
            if shift == 0:
                bases = [list(own_base) for _ in range(GROUPS)]
            outs = multiply(
                [[arrived[-1]]], down_weight, places[-1], [total], [True], wide_chunk,
                groups=GROUPS, tokens=tokens,
            )
            remote, all_steps = [], []
            for group in range(GROUPS):
                sent, kept = outs[2 * group : 2 * group + 2]
                if group == GROUPS - 1 and shift == 0 and levels > 1:
                    sent = gate(sent, [results[0][0][1], results[0][0][1 << levels - 1]])
                all_steps.append(reduce([sent, kept], group * half // GROUPS, shift + 1, bases[group], shift == seq_count - 2))
                next(all_steps[-1])
            last = []
            for level in range(levels + 1):
                for group, steps in enumerate(all_steps):
                    wait = list(last) if group == 0 else []
                    if group == GROUPS - 1 and level == levels and shift == 0:
                        wait += results[0][0][1:]
                    step = steps.send(wait)
                    if level == levels:
                        remote.append(spread(step))
                last = [step]
            results.append(remote)
            tokens = []

    groups = max(len(result) for result in results)
    width = half // groups

    def chosen(other):
        return [choose(results, group, width, other, per_sub, half // BLOCK) for group in range(groups)]

    came = [swap(values) for values in chosen(True)]
    mine = chosen(False)
    (codes,) = put_codes(mine, width, half, True)
    codes, flat = put_codes(came, width, half, False, codes, mine)
    return codes, flat.T


def solution(mesh):
    return jax.shard_map(
        shards,
        mesh=mesh,
        in_specs=(P(("groups", "seq"), ("tensor", "sub")), P(("tensor", "sub"), "seq"), P("seq")),
        out_specs=(P(("groups", "sub"), "seq"), P(("groups", "sub"), "seq")),
        check_vma=False,
    )
```
